512 devices in a mesh: group: 32 (over z, core), tensor: 16 (over y, x).
Axes of the slice: x: 4, y: 4, z: 16, core: 2. Of those that a mesh axis runs over, the one named last changes fastest.
Arguments:
- queries: bfloat16 [384, 4, 8192], P('group', None, 'tensor'), may hold values from -603 to 603
- new_entries: bfloat16 [384, 4, 2048], P('group'), may hold values from -6 to 6
- resident_cache: bfloat16 [128, 512, 2048], P('group', 'tensor'), may hold values from -6 to 6
- prefill_cache: bfloat16 [256, 512, 2048], P('group', 'tensor'), may hold values from -6 to 6
- resident_kept: int32 [128], replicated, may hold values from 256 to 512, as said below
- kept_tokens: int32 [256], replicated, may hold values from 1 to 512, as said below
- prefill_slot: int32 [256], replicated, may hold values from 0 to 255, as said below
- decode_slot: int32 [256], replicated, may hold values from 4 to 383, as said below
Outputs:
- attended: bfloat16 [384, 4, 8192], P('group', None, 'tensor')
The draws below stay inside these ranges and needn't reach their ends.
Inputs may be any that keep to these rules, and one draw needn't show every extreme that they name: `kept_tokens`: some request keeps exactly 512 positions. `prefill_slot`: A permutation of the 256 prefill slots; slot s lies in prefill group s // 8. `decode_slot`: every slot g * 12 + l with l >= 4 is named by exactly one request; from one prefill group to one decode group go at most 1 request, and exactly 1 for some pairs. `resident_kept`: some resident request keeps exactly 512 positions.
All inputs are finite; a program needn't handle non-finite values.
Results may differ from the reference program's by a relative error of at most 0.0044.
Values may be sent and summed in bfloat16 or wider, within the bound.
No kernel may reach another device: no remote copies, remote signals or barrier semaphores. Data moves between devices by JAX's collectives and lax.ppermute only.
A program may use at most 128 MiB of HBM per device.

```python
import math
import jax
import jax.numpy as jnp
from jax import lax

H = 64
KVH = 8
HD = 128
STEPS = 4
CAP = 512
MIG_DEV = 8
RES_DEV = 4
DSLOTS = 384
REQS = 256
PAIR_MOST = 1
N_GROUP = 32


def migration_plan(key):
    base = jax.random.fold_in(key, 7)
    subkeys = jax.random.split(base, 5)
    slot_count = MIG_DEV * N_GROUP
    rotation = jax.random.randint(subkeys[0], (), 0, 4)
    every_slot = jnp.arange(slot_count, dtype=jnp.int32)
    home_group = every_slot // MIG_DEV
    home_local = every_slot % MIG_DEV
    load_level = 1 + (home_group + rotation) % 4
    jitter = jax.random.randint(subkeys[1], (slot_count,), 0, CAP // 8)
    jitter = jnp.where((load_level == 4) & (home_local == 0), 0, jitter)
    kept_by_slot = load_level * (CAP // 4) - jitter
    group_order = jax.random.permutation(subkeys[2], N_GROUP).astype(jnp.int32)
    local_order = jax.random.permutation(subkeys[3], MIG_DEV).astype(jnp.int32)
    lane_index = home_local // PAIR_MOST
    target_group = group_order[(home_group + lane_index) % N_GROUP]
    target_local = RES_DEV + local_order[lane_index * PAIR_MOST + home_local % PAIR_MOST]
    target_slot = target_group * (RES_DEV + MIG_DEV) + target_local
    request_slot = jax.random.permutation(subkeys[4], slot_count).astype(jnp.int32)
    return (kept_by_slot[request_slot], request_slot, target_slot[request_slot])


def draw_kept_tokens(key, part):
    return migration_plan(key)[0].astype(jnp.int32)


def draw_prefill_slot(key, part):
    return migration_plan(key)[1].astype(jnp.int32)


def draw_decode_slot(key, part):
    return migration_plan(key)[2].astype(jnp.int32)


def draw_resident_kept(key, part):
    sub_key = jax.random.fold_in(key, 11)
    picked = jax.random.randint(sub_key, (N_GROUP * RES_DEV,), CAP // 2, CAP + 1)
    return jnp.where(jnp.arange(N_GROUP * RES_DEV) == 0, CAP, picked).astype(jnp.int32)


def token_draws(key):
    base = jax.random.fold_in(key, 23)
    subkeys = jax.random.split(base, 2)
    row_total = DSLOTS
    new_part = jnp.clip(jax.random.normal(subkeys[0], (row_total, STEPS, 2, KVH, HD), jnp.float32), -6.0, 6.0)
    spread_part = jnp.clip(jax.random.normal(subkeys[1], (row_total, STEPS, KVH, H // KVH, HD), jnp.float32), -6.0, 6.0)
    asking = spread_part + 0.5 * new_part[:, :, 0, :, None, :]
    return (asking.reshape(row_total, STEPS, H * HD), new_part.reshape(row_total, STEPS, 2 * KVH * HD))


def draw_queries(key, part):
    return token_draws(key)[0].astype(jnp.bfloat16)


def draw_new_entries(key, part):
    return token_draws(key)[1].astype(jnp.bfloat16)


def level_of(own_key, dims, cuts, smallest, largest):
    level = 1.0
    for position, parts in cuts:
        heights = jax.random.uniform(jax.random.fold_in(jax.random.fold_in(own_key, 6), position), (parts,), jnp.float32, smallest / len(cuts), largest / len(cuts))
        level = level * jnp.repeat(jnp.exp(heights), dims[position] // parts).reshape((-1,) + (1,) * (len(dims) - 1 - position))
    return level


def centred(own_key, shape, spread, reach, shards=(), kind=jnp.bfloat16):
    factor_of = level_of(own_key, shape, shards, -0.22, 0.18) if shards else 1.0
    result = jax.random.normal(own_key, shape, jnp.float32) * spread * factor_of
    return jnp.minimum(jnp.maximum(result, -reach), reach).astype(kind)


def setup_inputs(seed: int = 0) -> dict:
    splits = jax.random.split(jax.random.key(seed), 9)
    return {
        "queries": draw_queries(jax.random.fold_in(splits[8], 71), 0),
        "new_entries": draw_new_entries(jax.random.fold_in(splits[8], 71), 0),
        "resident_cache": centred(splits[2], (N_GROUP * RES_DEV, CAP, 2 * KVH * HD), 1.0, 6.0, ((0, 32), (1, 16))),
        "prefill_cache": centred(splits[3], (REQS, CAP, 2 * KVH * HD), 1.0, 6.0, ((0, 32), (1, 16))),
        "resident_kept": draw_resident_kept(jax.random.fold_in(splits[8], 71), 0),
        "kept_tokens": draw_kept_tokens(jax.random.fold_in(splits[8], 71), 0),
        "prefill_slot": draw_prefill_slot(jax.random.fold_in(splits[8], 71), 0),
        "decode_slot": draw_decode_slot(jax.random.fold_in(splits[8], 71), 0),
    }


def attend_one(asking, newest_in, stored, length):
    sharing = H // KVH
    temper = 1.0 / math.sqrt(HD)
    asked_rows = asking.astype(jnp.float32).reshape(STEPS, KVH, sharing, HD)
    entries = stored.astype(jnp.float32).reshape(CAP, 2, KVH, HD)
    newest = newest_in.astype(jnp.float32).reshape(STEPS, 2, KVH, HD)
    old_scores = jnp.einsum('tkgd,pkd->tkgp', asked_rows, entries[:, 0]) * temper
    new_scores = jnp.einsum('tkgd,ukd->tkgu', asked_rows, newest[:, 0]) * temper
    old_usable = (jnp.arange(CAP) < length)[None, None, None, :]
    new_usable = (jnp.arange(STEPS)[None, :] <= jnp.arange(STEPS)[:, None])[:, None, None, :]
    highest = jnp.maximum(lax.optimization_barrier(jnp.max(jnp.where(old_usable, old_scores, -1e+30), axis=3)), lax.optimization_barrier(jnp.max(jnp.where(new_usable, new_scores, -1e+30), axis=3)))
    old_weights = jnp.where(old_usable, jnp.exp(old_scores - highest[..., None]), 0.0)
    new_weights = jnp.where(new_usable, jnp.exp(new_scores - highest[..., None]), 0.0)
    totals = lax.optimization_barrier(jnp.sum(old_weights, axis=3)) + lax.optimization_barrier(jnp.sum(new_weights, axis=3))
    old_rounded = lax.optimization_barrier(old_weights.astype(jnp.bfloat16)).astype(jnp.float32)
    new_rounded = lax.optimization_barrier(new_weights.astype(jnp.bfloat16)).astype(jnp.float32)
    blended = jnp.einsum('tkgp,pkd->tkgd', old_rounded, entries[:, 1]) + jnp.einsum('tkgu,ukd->tkgd', new_rounded, newest[:, 1])
    return (blended / totals[..., None]).reshape(STEPS, H * HD).astype(jnp.bfloat16)

def reference(queries, new_entries, resident_cache, prefill_cache, resident_kept, kept_tokens, prefill_slot, decode_slot):
    per_group = RES_DEV + MIG_DEV
    total_slots = N_GROUP * per_group
    source = jnp.zeros((total_slots,), jnp.int32).at[decode_slot].set(prefill_slot.astype(jnp.int32))
    moved_len = jnp.zeros((total_slots,), jnp.int32).at[decode_slot].set(kept_tokens.astype(jnp.int32))
    everyone = jnp.arange(total_slots, dtype=jnp.int32)
    owner_group = everyone // per_group
    within = everyone % per_group
    is_resident = within < RES_DEV
    resident_row = (owner_group * RES_DEV + jnp.minimum(within, RES_DEV - 1)).astype(jnp.int32)
    lengths = jnp.where(is_resident, resident_kept[resident_row], moved_len)

    def handle(record):
        slot_id, resident_id, source_id, is_local, length = record
        stored = jnp.where(is_local, resident_cache[resident_id], prefill_cache[source_id])
        return attend_one(queries[slot_id], new_entries[slot_id], stored, length)
    return lax.map(handle, (everyone, resident_row, source, is_resident, lengths))
```

```python
import math

import jax
import jax.numpy as jnp
from jax import lax
from jax.experimental import pallas as pl
from jax.experimental.pallas import tpu as pltpu
from jax.sharding import PartitionSpec as P

H = 64
KVH = 8
HD = 128
STEPS = 4
MIG = 8
RES = 4
SLOTS = MIG + RES
GROUPS = 32
SHARDS = 16
STRIDE = 32
HEADS = H // SHARDS
QROWS = HEADS * STEPS
ROWS = SLOTS * QROWS
FEATURES = KVH * HD
CHUNK = QROWS + 2 * STEPS
PAYLOAD = ROWS + 16
FLOOR = -1e30
SCALE = 1.0 / math.sqrt(HD)
LIMIT = 48 * 1024 * 1024
BF = jnp.bfloat16
F32 = jnp.float32

VM = pl.BlockSpec(memory_space=pltpu.VMEM)
SM = pl.BlockSpec(memory_space=pltpu.SMEM)


def call(kernel, outs, specs, flops=0, moved=0, scratch=()):
    return pl.pallas_call(
        kernel,
        out_shape=outs,
        in_specs=specs,
        out_specs=jax.tree.map(lambda _: VM, outs),
        scratch_shapes=scratch,
        compiler_params=pltpu.CompilerParams(vmem_limit_bytes=LIMIT),
        cost_estimate=pl.CostEstimate(flops=flops, bytes_accessed=moved, transcendentals=0),
    )


def pack_kernel(target, where, asked, fresh, sent, kept):
    sent[...] = jnp.zeros_like(sent)
    pair = pl.multiple_of(where[0] // 2 * HD, HD)

    def chunk(slot):
        keys = fresh[slot, :, pl.ds(pair, HD)].astype(F32)
        values = fresh[slot, :, pl.ds(pair + FEATURES, HD)].astype(F32)
        entries = jnp.concatenate([keys, values], 0)
        return jnp.concatenate([asked[slot].astype(F32), entries], 0).astype(BF)

    for slot in range(RES):
        kept[slot] = chunk(slot)
    for slot in range(MIG):
        sent[target[slot]] = chunk(RES + slot)


def spread_kernel(origin, arrived, kept, asking, recent):
    recent[...] = jnp.zeros_like(recent)
    for row in range(SLOTS):
        chunk = arrived[origin[row]] if row < MIG else kept[row - MIG]
        for peer in range(SHARDS):
            asking[peer, row * QROWS : (row + 1) * QROWS, :] = chunk[:QROWS]
        recent[row * 8 : (row + 1) * 8, :] = chunk[QROWS:].astype(F32)


def scores_of(left, right):
    return lax.dot_general(left, right, (((1,), (1,)), ((), ())), preferred_element_type=F32) * SCALE


def partial_kernel(lengths, where, asking, moved, resident, payload, stats):
    stats[...] = jnp.zeros_like(stats)
    lane = lax.broadcasted_iota(jnp.int32, (QROWS, HD), 1)
    column = lax.broadcasted_iota(jnp.int32, (2 * QROWS, STRIDE), 1) + where[0] * STRIDE
    for row in range(SLOTS):
        cache = moved.at[row] if row < MIG else resident.at[row - MIG]
        usable = column < lengths[row]
        span = slice(row * QROWS, (row + 1) * QROWS)
        table = jnp.zeros((QROWS, HD), F32)
        for pair in range(KVH):
            keys = cache[:, pair * HD : (pair + 1) * HD]
            values = cache[:, FEATURES + pair * HD : FEATURES + (pair + 1) * HD]
            asked = jnp.concatenate([asking[2 * pair, span, :], asking[2 * pair + 1, span, :]], 0)
            scores = jnp.where(usable, scores_of(asked, keys), FLOOR)
            top = jnp.max(scores, axis=1, keepdims=True)
            first = top.astype(BF).astype(F32)
            second = (top - first).astype(BF).astype(F32)
            weights = jnp.where(usable, jnp.exp(scores - (first + second)), 0.0)
            total = jnp.sum(weights, axis=1, keepdims=True)
            blended = jnp.dot(weights.astype(BF), values, preferred_element_type=F32).astype(BF)
            total_first = total.astype(BF).astype(F32)
            columns = (first, total_first, second, total - total_first)
            for half in range(2):
                peer = 2 * pair + half
                rows = slice(half * QROWS, (half + 1) * QROWS)
                payload[peer, span, :] = blended[rows]
                for place, value in enumerate(columns):
                    table = jnp.where(lane == peer * 8 + place, value[rows], table)
        stats[span, :] = table
    low = stats[:HD, :].T.reshape(SHARDS, 8, HD)
    high = stats[HD:, :].T.reshape(SHARDS, 8, HD)
    payload[:, ROWS:, :] = jnp.concatenate([low, high], 1).astype(BF)


def merge_kernel(origin, gathered, asked, recent, sent, kept):
    entries = recent[...].astype(BF)
    row = lax.broadcasted_iota(jnp.int32, (ROWS, HD), 0)
    lane = lax.broadcasted_iota(jnp.int32, (ROWS, HD), 1)
    causal = (lane // 8 == row // QROWS) & (lane % 8 <= row % STEPS)
    fresh = jnp.where(causal, scores_of(asked[...], entries), FLOOR)
    fresh_top = jnp.max(fresh, axis=1, keepdims=True)

    tops = gathered[:, ROWS:, :].astype(F32)
    low = tops[:, :8, :].reshape(HD, HD).T
    high = tops[:, 8:, :].reshape(HD, HD).T[: ROWS - HD]
    pairs = jnp.concatenate([low, high], 0)
    both = pairs + pltpu.roll(pairs, HD - 2, 1)
    is_top = lane % 8 == 0
    tops = jnp.where(is_top, both, FLOOR)
    sums = pltpu.roll(both, HD - 1, 1)
    highest = jnp.maximum(jnp.max(tops, axis=1, keepdims=True), fresh_top)
    factors = jnp.where(is_top, jnp.exp(tops - highest), 0.0)
    fresh_weights = jnp.where(causal, jnp.exp(fresh - highest), 0.0)
    totals = jnp.sum(jnp.where(is_top, factors * sums, 0.0) + fresh_weights, axis=1, keepdims=True)
    blended = jnp.dot(
        pltpu.roll(fresh_weights, STEPS, 1).astype(BF), entries, preferred_element_type=F32
    )
    for peer in range(SHARDS):
        blended += factors[:, peer * 8 : peer * 8 + 1] * gathered[peer, :ROWS, :].astype(F32)
    result = (blended / totals).astype(BF)

    sent[...] = jnp.zeros_like(sent)
    for slot in range(MIG):
        sent[origin[slot]] = result[slot * QROWS : (slot + 1) * QROWS]
    for slot in range(RES):
        kept[slot] = result[(MIG + slot) * QROWS : (MIG + slot + 1) * QROWS]


def select_kernel(target, returned, kept, out):
    for slot in range(RES):
        out[slot] = kept[slot]
    for slot in range(MIG):
        out[RES + slot] = returned[target[slot]]


def body(
    queries,
    new_entries,
    resident_cache,
    prefill_cache,
    resident_kept,
    kept_tokens,
    prefill_slot,
    decode_slot,
):
    group = lax.axis_index("group")
    shard = lax.axis_index("tensor")

    def looked_up(names, first, values):
        wanted = first + jnp.arange(MIG, dtype=jnp.int32)
        return jnp.sum(jnp.where(names[None, :] == wanted[:, None], values[None, :], 0), axis=1)

    target = looked_up(decode_slot, group * SLOTS + RES, prefill_slot) // MIG
    origin = looked_up(prefill_slot, group * MIG, decode_slot) // SLOTS
    moved_len = looked_up(prefill_slot, group * MIG, kept_tokens)
    resident_len = lax.dynamic_slice_in_dim(resident_kept, group * RES, RES)
    lengths = jnp.concatenate([moved_len, resident_len])
    where = shard.reshape(1)

    asked = queries.reshape(SLOTS, STEPS, HEADS, HD).transpose(0, 2, 1, 3)
    asked = asked.reshape(SLOTS, QROWS, HD)
    shape = jax.ShapeDtypeStruct

    sent, kept = call(
        pack_kernel,
        (shape((GROUPS, CHUNK, HD), BF), shape((RES, CHUNK, HD), BF)),
        [SM, SM, VM, VM],
    )(target, where, asked, new_entries)
    arrived = lax.all_to_all(sent, "group", 0, 0, tiled=True)

    asking, recent = call(
        spread_kernel,
        (shape((SHARDS, ROWS, HD), BF), shape((HD, HD), F32)),
        [SM, VM, VM],
    )(origin, arrived, kept)
    everyone = lax.all_to_all(asking, "tensor", 0, 0, tiled=True)

    payload = call(
        partial_kernel,
        shape((SHARDS, PAYLOAD, HD), BF),
        [SM, SM, VM, VM, VM],
        flops=10**8,
        moved=3 * 2**20,
        scratch=[pltpu.VMEM((2 * HD, HD), F32)],
    )(lengths, where, everyone, prefill_cache, resident_cache)
    gathered = lax.all_to_all(payload, "tensor", 0, 0, tiled=True)

    finished, here = call(
        merge_kernel,
        (shape((GROUPS, QROWS, HD), BF), shape((RES, QROWS, HD), BF)),
        [SM, VM, VM, VM],
    )(origin, gathered, asking[0], recent)
    returned = lax.all_to_all(finished, "group", 0, 0, tiled=True)

    result = call(select_kernel, shape((SLOTS, QROWS, HD), BF), [SM, VM, VM])(target, returned, here)
    result = result.reshape(SLOTS, HEADS, STEPS, HD).transpose(0, 2, 1, 3)
    return result.reshape(SLOTS, STEPS, HEADS * HD)


def solution(mesh):
    in_specs = (
        P("group", None, "tensor"),
        P("group", None, None),
        P("group", "tensor", None),
        P("group", "tensor", None),
        P(),
        P(),
        P(),
        P(),
    )
    out_specs = P("group", None, "tensor")
    return jax.shard_map(body, mesh=mesh, in_specs=in_specs, out_specs=out_specs, check_vma=False)
```

```python
import math

import jax
import jax.numpy as jnp
from jax import lax
from jax.experimental import pallas as pl
from jax.experimental.pallas import tpu as pltpu
from jax.sharding import PartitionSpec as P

H = 64
KVH = 8
HD = 128
STEPS = 4
MIG = 8
RES = 4
SLOTS = MIG + RES
GROUPS = 32
SHARDS = 16
SIDE = 4
STRIDE = 32
HEADS = H // SHARDS
PAIRS = KVH // SIDE
QROWS = HEADS * STEPS
ROWS = SLOTS * QROWS
FEATURES = KVH * HD
WIDTH = PAIRS * HD
CHUNK = QROWS + 2 * STEPS
PAYLOAD = ROWS + 16
FLOOR = -(2.0**100)
SCALE = 1.0 / math.sqrt(HD)
LIMIT = 48 * 1024 * 1024
BF = jnp.bfloat16
F32 = jnp.float32

VM = pl.BlockSpec(memory_space=pltpu.VMEM)
SM = pl.BlockSpec(memory_space=pltpu.SMEM)


def call(kernel, outs, specs, flops=0, moved=0, scratch=()):
    return pl.pallas_call(
        kernel,
        out_shape=outs,
        in_specs=specs,
        out_specs=jax.tree.map(lambda _: VM, outs),
        scratch_shapes=scratch,
        compiler_params=pltpu.CompilerParams(vmem_limit_bytes=LIMIT),
        cost_estimate=pl.CostEstimate(flops=flops, bytes_accessed=moved, transcendentals=0),
    )


def pack_kernel(target, where, asked, fresh, sent, kept):
    sent[...] = jnp.zeros_like(sent)
    pair = pl.multiple_of(where[0] // 2 * HD, HD)

    def chunk(slot):
        keys = fresh[slot, :, pl.ds(pair, HD)].astype(F32)
        values = fresh[slot, :, pl.ds(pair + FEATURES, HD)].astype(F32)
        entries = jnp.concatenate([keys, values], 0)
        return jnp.concatenate([asked[slot].astype(F32), entries], 0).astype(BF)

    for slot in range(RES):
        kept[slot] = chunk(slot)
    for slot in range(MIG):
        sent[target[slot]] = chunk(RES + slot)


def split_kernel(where, moved, resident, *outs):
    along = where[0] // SIDE
    for step, out in enumerate(outs):
        first = pl.multiple_of((along + step) % SIDE * WIDTH, WIDTH)
        for part in range(2):
            lanes = pl.ds(first + part * FEATURES, WIDTH)
            columns = slice(part * WIDTH, (part + 1) * WIDTH)
            out[:MIG, :, columns] = moved[:, :, lanes]
            out[MIG:, :, columns] = resident[:, :, lanes]


def spread_kernel(origin, arrived, kept, asking, own, recent):
    recent[...] = jnp.zeros_like(recent)
    for row in range(SLOTS):
        chunk = arrived[origin[row]] if row < MIG else kept[row - MIG]
        span = slice(row * QROWS, (row + 1) * QROWS)
        for peer in range(SIDE):
            asking[peer, span, :] = chunk[:QROWS]
        own[span, :] = chunk[:QROWS]
        recent[row * 8 : (row + 1) * 8, :] = chunk[QROWS:].astype(F32)


def scores_of(left, right):
    return lax.dot_general(left, right, (((1,), (1,)), ((), ())), preferred_element_type=F32) * SCALE


def partial_kernel(lengths, where, asking, *rest):
    *blocks, payload, scores, weights, stats = rest
    along, across = where[0] // SIDE, where[0] % SIDE
    column = lax.broadcasted_iota(jnp.int32, (1, HD), 1)
    source = ((along - column // STRIDE) & (SIDE - 1)) * SIDE + across
    position = source * STRIDE + column % STRIDE

    def stored(row, place):
        lanes = slice(place * HD, (place + 1) * HD)
        return jnp.concatenate([block[row, :, lanes] for block in blocks], 0)

    for row in range(SLOTS):
        usable = position < lengths[row]
        span = slice(row * QROWS, (row + 1) * QROWS)
        for pair in range(PAIRS):
            asked = jnp.concatenate([asking[2 * pair, span, :], asking[2 * pair + 1, span, :]], 0)
            found = jnp.where(usable, scores_of(asked, stored(row, pair)), FLOOR)
            scores[2 * pair, span, :] = found[:QROWS]
            scores[2 * pair + 1, span, :] = found[QROWS:]
    lane = lax.broadcasted_iota(jnp.int32, (ROWS, HD), 1)
    table = jnp.zeros((ROWS, HD), F32)
    for peer in range(SIDE):
        found = scores[peer]
        top = jnp.max(found, axis=1, keepdims=True)
        first = top.astype(BF).astype(F32)
        second = (top - first).astype(BF).astype(F32)
        weight = jnp.exp(found - (first + second))
        total = jnp.sum(weight, axis=1, keepdims=True)
        weights[peer] = weight.astype(BF)
        total_first = total.astype(BF).astype(F32)
        for place, value in enumerate((first, total_first, second, total - total_first)):
            table = jnp.where(lane == peer * 8 + place, value, table)
    stats[:ROWS, :] = table
    stats[ROWS:, :] = jnp.zeros((2 * HD - ROWS, HD), F32)
    low = stats[:HD, :].T
    high = stats[HD:, :].T
    for peer in range(SIDE):
        rows = slice(peer * 8, (peer + 1) * 8)
        payload[peer, ROWS:, :] = jnp.concatenate([low[rows], high[rows]], 0).astype(BF)
    for row in range(SLOTS):
        span = slice(row * QROWS, (row + 1) * QROWS)
        for pair in range(PAIRS):
            weight = jnp.concatenate([weights[2 * pair, span, :], weights[2 * pair + 1, span, :]], 0)
            blended = jnp.dot(weight, stored(row, PAIRS + pair), preferred_element_type=F32).astype(BF)
            payload[2 * pair, span, :] = blended[:QROWS]
            payload[2 * pair + 1, span, :] = blended[QROWS:]


def merge_kernel(origin, gathered, asked, recent, sent, kept):
    entries = recent[...].astype(BF)
    row = lax.broadcasted_iota(jnp.int32, (ROWS, HD), 0)
    lane = lax.broadcasted_iota(jnp.int32, (ROWS, HD), 1)
    causal = (lane // 8 == row // QROWS) & (lane % 8 <= row % STEPS)
    fresh = jnp.where(causal, scores_of(asked[...], entries), FLOOR)
    fresh_top = jnp.max(fresh, axis=1, keepdims=True)

    tops = gathered[:, ROWS:, :].astype(F32)
    blank = jnp.zeros((HD - SIDE * 8, HD), F32)
    low = jnp.concatenate([tops[:, :8, :].reshape(SIDE * 8, HD), blank], 0).T
    high = jnp.concatenate([tops[:, 8:, :].reshape(SIDE * 8, HD), blank], 0).T[: ROWS - HD]
    pairs = jnp.concatenate([low, high], 0)
    both = pairs + pltpu.roll(pairs, HD - 2, 1)
    is_top = (lane % 8 == 0) & (lane < SIDE * 8)
    tops = jnp.where(is_top, both, FLOOR)
    sums = pltpu.roll(both, HD - 1, 1)
    highest = jnp.maximum(jnp.max(tops, axis=1, keepdims=True), fresh_top)
    factors = jnp.where(is_top, jnp.exp(tops - highest), 0.0)
    fresh_weights = jnp.where(causal, jnp.exp(fresh - highest), 0.0)
    totals = jnp.sum(jnp.where(is_top, factors * sums, 0.0) + fresh_weights, axis=1, keepdims=True)
    blended = jnp.dot(
        pltpu.roll(fresh_weights, STEPS, 1).astype(BF), entries, preferred_element_type=F32
    )
    for peer in range(SIDE):
        blended += factors[:, peer * 8 : peer * 8 + 1] * gathered[peer, :ROWS, :].astype(F32)
    result = (blended / totals).astype(BF)

    sent[...] = jnp.zeros_like(sent)
    for slot in range(MIG):
        sent[origin[slot]] = result[slot * QROWS : (slot + 1) * QROWS]
    for slot in range(RES):
        kept[slot] = result[(MIG + slot) * QROWS : (MIG + slot + 1) * QROWS]


def select_kernel(target, returned, kept, out):
    for slot in range(RES):
        out[slot] = kept[slot]
    for slot in range(MIG):
        out[RES + slot] = returned[target[slot]]


def body(
    queries,
    new_entries,
    resident_cache,
    prefill_cache,
    resident_kept,
    kept_tokens,
    prefill_slot,
    decode_slot,
):
    group = lax.axis_index("group")
    shard = lax.axis_index("tensor")

    def looked_up(names, first, values):
        wanted = first + jnp.arange(MIG, dtype=jnp.int32)
        return jnp.sum(jnp.where(names[None, :] == wanted[:, None], values[None, :], 0), axis=1)

    target = looked_up(decode_slot, group * SLOTS + RES, prefill_slot) // MIG
    origin = looked_up(prefill_slot, group * MIG, decode_slot) // SLOTS
    moved_len = looked_up(prefill_slot, group * MIG, kept_tokens)
    resident_len = lax.dynamic_slice_in_dim(resident_kept, group * RES, RES)
    lengths = jnp.concatenate([moved_len, resident_len])
    where = shard.reshape(1)
    rings = [[SIDE * y + x for x in range(SIDE)] for y in range(SIDE)]

    def across(array):
        return lax.all_to_all(array, "tensor", 0, 0, axis_index_groups=rings, tiled=True)


    asked = queries.reshape(SLOTS, STEPS, HEADS, HD).transpose(0, 2, 1, 3)
    asked = asked.reshape(SLOTS, QROWS, HD)
    shape = jax.ShapeDtypeStruct

    sent, kept = call(
        pack_kernel,
        (shape((GROUPS, CHUNK, HD), BF), shape((RES, CHUNK, HD), BF)),
        [SM, SM, VM, VM],
    )(target, where, asked, new_entries)
    arrived = lax.all_to_all(sent, "group", 0, 0, tiled=True)

    split = call(
        split_kernel,
        (shape((SLOTS, STRIDE, 2 * WIDTH), BF),) * SIDE,
        [SM, VM, VM],
        moved=3 * 2**20,
    )(where, prefill_cache, resident_cache)
    blocks = [split[0]]
    for step in range(1, SIDE):
        steps = [(t, (t + step * SIDE) % SHARDS) for t in range(SHARDS)]
        blocks.append(lax.ppermute(split[step], "tensor", steps))

    asking, own, recent = call(
        spread_kernel,
        (shape((SIDE, ROWS, HD), BF), shape((ROWS, HD), BF), shape((HD, HD), F32)),
        [SM, VM, VM],
    )(origin, arrived, kept)
    everyone = across(asking)

    payload = call(
        partial_kernel,
        shape((SIDE, PAYLOAD, HD), BF),
        [SM, SM] + [VM] * (1 + SIDE),
        flops=10**8,
        moved=3 * 2**20,
        scratch=[
            pltpu.VMEM((SIDE, ROWS, HD), F32),
            pltpu.VMEM((SIDE, ROWS, HD), BF),
            pltpu.VMEM((2 * HD, HD), F32),
        ],
    )(lengths, where, everyone, *blocks)
    gathered = across(payload)

    finished, here = call(
        merge_kernel,
        (shape((GROUPS, QROWS, HD), BF), shape((RES, QROWS, HD), BF)),
        [SM, VM, VM, VM],
    )(origin, gathered, own, recent)
    returned = lax.all_to_all(finished, "group", 0, 0, tiled=True)

    result = call(select_kernel, shape((SLOTS, QROWS, HD), BF), [SM, VM, VM])(target, returned, here)
    result = result.reshape(SLOTS, HEADS, STEPS, HD).transpose(0, 2, 1, 3)
    return result.reshape(SLOTS, STEPS, HEADS * HD)


def solution(mesh):
    in_specs = (
        P("group", None, "tensor"),
        P("group", None, None),
        P("group", "tensor", None),
        P("group", "tensor", None),
        P(),
        P(),
        P(),
        P(),
    )
    out_specs = P("group", None, "tensor")
    return jax.shard_map(body, mesh=mesh, in_specs=in_specs, out_specs=out_specs, check_vma=False)
```

```python
import math

import jax
import jax.numpy as jnp
from jax import lax
from jax.experimental import pallas as pl
from jax.experimental.pallas import tpu as pltpu
from jax.sharding import PartitionSpec as P

H = 64
KVH = 8
HD = 128
STEPS = 4
MIG = 8
RES = 4
SLOTS = MIG + RES
GROUPS = 32
SHARDS = 16
SIDE = 4
STRIDE = 32
HEADS = H // SHARDS
PAIRS = KVH // SIDE
QROWS = HEADS * STEPS
ROWS = SLOTS * QROWS
FEATURES = KVH * HD
TILES = HEADS + 1
ENTRIES = SLOTS * STEPS
PAYLOAD = ROWS + 16
FLOOR = -(2.0**100)
SCALE = 1.0 / math.sqrt(HD)
LIMIT = 48 * 1024 * 1024
FULL = 63 * 1024 * 1024
BF = jnp.bfloat16
F32 = jnp.float32

VM = pl.BlockSpec(memory_space=pltpu.VMEM)
SM = pl.BlockSpec(memory_space=pltpu.SMEM)
HB = pl.BlockSpec(memory_space=pltpu.HBM)


def call(kernel, outs, specs, flops=0, moved=0, scratch=(), limit=LIMIT, place=VM):
    return pl.pallas_call(
        kernel,
        out_shape=outs,
        in_specs=specs,
        out_specs=jax.tree.map(lambda _: place, outs),
        scratch_shapes=scratch,
        compiler_params=pltpu.CompilerParams(vmem_limit_bytes=limit),
        cost_estimate=pl.CostEstimate(flops=flops, bytes_accessed=moved, transcendentals=0),
    )


def swapped(step, y, x):
    return y ^ (step % 2), x ^ (step // 2 * 3)


def class_of(y, x):
    return jnp.minimum(y, 3 - y), x // 2


def place_of():
    shard = lax.axis_index("tensor")
    return shard // SIDE, shard % SIDE


def pack_kernel(named, holders, asked, fresh, sent, kept, asked_here, fresh_here, named_here, holders_here, sems):
    shard = lax.axis_index("tensor")
    first = pl.multiple_of(shard % 2 * FEATURES + shard // 2 * HD, HD)
    copies = [
        pltpu.make_async_copy(source, target, sems.at[n])
        for n, (source, target) in enumerate(
            (
                (named, named_here),
                (holders, holders_here),
                (asked, asked_here),
                (fresh.at[:, :, pl.ds(first, HD)], fresh_here),
            )
        )
    ]
    for copy in copies:
        copy.start()
    sent[...] = jnp.zeros_like(sent)
    for copy in copies:
        copy.wait()
    names = named_here[...]
    slots = holders_here[...].astype(F32)
    for slot in range(RES):
        kept[slot, :HEADS] = asked_here[slot]
        kept[slot, HEADS] = fresh_here[slot]
    groups = []
    for slot in range(RES, SLOTS):
        mine = names == lax.axis_index("group") * SLOTS + slot
        groups.append(jnp.sum(jnp.where(mine, slots, 0.0)).astype(jnp.int32) // MIG)
    for slot, group in zip(range(RES, SLOTS), groups):
        sent[group, :HEADS] = asked_here[slot]
        sent[group, HEADS] = fresh_here[slot]


def split_kernel(moved, resident, *rest):
    *outs, sems = rest
    here = place_of()
    copies = []
    for step in (*range(1, SIDE), 0):
        low, half = class_of(*swapped(step, *here))
        for place, pair in enumerate((2 * low + half, 6 - 2 * low + half)):
            for part in range(2):
                lanes = pl.ds(pl.multiple_of(pair * HD + part * FEATURES, HD), HD)
                columns = pl.ds((part * PAIRS + place) * HD, HD)
                for source, rows in ((moved, pl.ds(0, MIG)), (resident, pl.ds(MIG, RES))):
                    target = outs[step].at[rows, :, columns]
                    sem = sems.at[len(copies)]
                    copies.append(pltpu.make_async_copy(source.at[:, :, lanes], target, sem))
    for copy in copies:
        copy.start()
    for copy in copies:
        copy.wait()


def spread_kernel(origin, arrived, kept, asking):
    for row in range(SLOTS):
        chunk = arrived.at[origin[row]] if row < MIG else kept.at[row - MIG]
        for peer in range(SIDE):
            asking[peer, row * HEADS : (row + 1) * HEADS] = chunk[:HEADS]
            asking[peer, SLOTS * HEADS + row] = chunk[HEADS]


def scores_of(left, right):
    return lax.dot_general(left, right, (((1,), (1,)), ((), ())), preferred_element_type=F32) * SCALE


def partial_kernel(lengths, asking, *rest):
    *blocks, payload, scores, weights, stats = rest
    column = lax.broadcasted_iota(jnp.int32, (1, HD), 1)
    y, x = swapped(column // STRIDE, *place_of())
    position = (y * SIDE + x) * STRIDE + column % STRIDE

    def stored(row, place):
        lanes = slice(place * HD, (place + 1) * HD)
        return jnp.concatenate([block[row, :, lanes] for block in blocks], 0)

    for row in range(SLOTS):
        usable = position < lengths[row]
        span = slice(row * QROWS, (row + 1) * QROWS)
        for pair in range(PAIRS):
            asked = jnp.concatenate([asking[2 * pair, span, :], asking[2 * pair + 1, span, :]], 0)
            found = jnp.where(usable, scores_of(asked, stored(row, pair)), FLOOR)
            scores[2 * pair, span, :] = found[:QROWS]
            scores[2 * pair + 1, span, :] = found[QROWS:]
    lane = lax.broadcasted_iota(jnp.int32, (ROWS, HD), 1)
    table = jnp.zeros((ROWS, HD), F32)
    for peer in range(SIDE):
        found = scores[peer]
        top = jnp.max(found, axis=1, keepdims=True)
        first = top.astype(BF).astype(F32)
        second = (top - first).astype(BF).astype(F32)
        weight = jnp.exp(found - (first + second))
        total = jnp.sum(weight, axis=1, keepdims=True)
        weights[peer] = weight.astype(BF)
        total_first = total.astype(BF).astype(F32)
        for place, value in enumerate((first, total_first, second, total - total_first)):
            table = jnp.where(lane == peer * 8 + place, value, table)
    stats[:ROWS, :] = table
    stats[ROWS:, :] = jnp.zeros((2 * HD - ROWS, HD), F32)
    low = stats[:HD, :].T
    high = stats[HD:, :].T
    for peer in range(SIDE):
        rows = slice(peer * 8, (peer + 1) * 8)
        payload[peer, ROWS:, :] = jnp.concatenate([low[rows], high[rows]], 0).astype(BF)
    for row in range(SLOTS):
        span = slice(row * QROWS, (row + 1) * QROWS)
        for pair in range(PAIRS):
            weight = jnp.concatenate([weights[2 * pair, span, :], weights[2 * pair + 1, span, :]], 0)
            blended = jnp.dot(weight, stored(row, PAIRS + pair), preferred_element_type=F32).astype(BF)
            payload[2 * pair, span, :] = blended[:QROWS]
            payload[2 * pair + 1, span, :] = blended[QROWS:]


def merge_kernel(origin, gathered, everyone, sent, kept):
    y, x = place_of()
    first = jnp.where(y > 1, 2, 0)
    asked = everyone[first + x % 2, :ROWS, :]
    keys = everyone[first, ROWS:, :]
    values = everyone[first + 1, ROWS:, :]
    row = lax.broadcasted_iota(jnp.int32, (ROWS, ENTRIES), 0)
    lane = lax.broadcasted_iota(jnp.int32, (ROWS, ENTRIES), 1)
    causal = (lane // STEPS == row // QROWS) & (lane % STEPS <= row % STEPS)
    fresh = jnp.where(causal, scores_of(asked, keys), FLOOR)
    fresh_top = jnp.max(fresh, axis=1, keepdims=True)

    tops = gathered[:, ROWS:, :].astype(F32)
    blank = jnp.zeros((HD - SIDE * 8, HD), F32)
    low = jnp.concatenate([tops[:, :8, :].reshape(SIDE * 8, HD), blank], 0).T
    high = jnp.concatenate([tops[:, 8:, :].reshape(SIDE * 8, HD), blank], 0).T[: ROWS - HD]
    pairs = jnp.concatenate([low, high], 0)
    both = pairs + pltpu.roll(pairs, HD - 2, 1)
    lane = lax.broadcasted_iota(jnp.int32, (ROWS, HD), 1)
    is_top = (lane % 8 == 0) & (lane < SIDE * 8)
    tops = jnp.where(is_top, both, FLOOR)
    sums = pltpu.roll(both, HD - 1, 1)
    highest = jnp.maximum(jnp.max(tops, axis=1, keepdims=True), fresh_top)
    factors = jnp.where(is_top, jnp.exp(tops - highest), 0.0)
    fresh_weights = jnp.where(causal, jnp.exp(fresh - highest), 0.0)
    totals = jnp.sum(jnp.where(is_top, factors * sums, 0.0), axis=1, keepdims=True)
    totals += jnp.sum(fresh_weights, axis=1, keepdims=True)
    blended = jnp.dot(fresh_weights.astype(BF), values, preferred_element_type=F32)
    for peer in range(SIDE):
        blended += factors[:, peer * 8 : peer * 8 + 1] * gathered[peer, :ROWS, :].astype(F32)
    result = (blended / totals).astype(BF)

    sent[...] = jnp.zeros_like(sent)
    for slot in range(MIG):
        sent[origin[slot]] = result[slot * QROWS : (slot + 1) * QROWS]
    for slot in range(RES):
        kept[slot] = result[(MIG + slot) * QROWS : (MIG + slot + 1) * QROWS]


def select_kernel(target, returned, kept, out):
    for slot in range(RES):
        out[slot] = kept[slot]
    for slot in range(MIG):
        out[RES + slot] = returned[target[slot]]


def body(
    queries,
    new_entries,
    resident_cache,
    prefill_cache,
    resident_kept,
    kept_tokens,
    prefill_slot,
    decode_slot,
):
    shape = jax.ShapeDtypeStruct
    whole = [(y, x) for y in range(SIDE) for x in range(SIDE)]
    peers = [[y * SIDE + x for y in (low, 3 - low) for x in (2 * half, 2 * half + 1)] for low in range(2) for half in range(2)]

    def across(array):
        return lax.all_to_all(array, "tensor", 0, 0, axis_index_groups=peers, tiled=True)

    asked = queries.reshape(SLOTS, STEPS, HEADS, HD).transpose(0, 2, 1, 3)
    sent, kept = call(
        pack_kernel,
        (shape((GROUPS, TILES, STEPS, HD), BF), shape((RES, TILES, STEPS, HD), BF)),
        [HB] * 4,
        scratch=[
            pltpu.VMEM((SLOTS, HEADS, STEPS, HD), BF),
            pltpu.VMEM((SLOTS, STEPS, HD), BF),
            pltpu.VMEM((2, HD), jnp.int32),
            pltpu.VMEM((2, HD), jnp.int32),
            pltpu.SemaphoreType.DMA((4,)),
        ],
        limit=FULL,
    )(decode_slot.reshape(2, HD), prefill_slot.reshape(2, HD), asked, new_entries)
    arrived = lax.all_to_all(sent, "group", 0, 0, tiled=True)

    (resident_kept, kept_tokens, prefill_slot, decode_slot), kept = lax.optimization_barrier(
        ((resident_kept, kept_tokens, prefill_slot, decode_slot), kept)
    )
    group = lax.axis_index("group")

    def looked_up(names, first, values):
        wanted = first + jnp.arange(MIG, dtype=jnp.int32)
        return jnp.sum(jnp.where(names[None, :] == wanted[:, None], values[None, :], 0), axis=1)

    target = looked_up(decode_slot, group * SLOTS + RES, prefill_slot) // MIG
    origin = looked_up(prefill_slot, group * MIG, decode_slot) // SLOTS
    moved_len = looked_up(prefill_slot, group * MIG, kept_tokens)
    resident_len = lax.dynamic_slice_in_dim(resident_kept, group * RES, RES)
    lengths = jnp.concatenate([moved_len, resident_len])

    split = call(
        split_kernel,
        (shape((SLOTS, STRIDE, 2 * PAIRS * HD), BF),) * SIDE,
        [HB, HB],
        moved=3 * 2**20,
        scratch=[pltpu.SemaphoreType.DMA((8 * SIDE,))],
        limit=FULL,
        place=HB,
    )(prefill_cache, resident_cache)
    blocks = [split[0]]
    for step in range(1, SIDE):
        steps = []
        for y, x in whole:
            other, side = swapped(step, y, x)
            steps.append((y * SIDE + x, other * SIDE + side))
        blocks.append(lax.ppermute(split[step], "tensor", steps))

    asking = call(
        spread_kernel, shape((SIDE, SLOTS * TILES, STEPS, HD), BF), [SM, VM, VM]
    )(origin, arrived, kept)
    everyone = across(asking).reshape(SIDE, ROWS + ENTRIES, HD)

    payload = call(
        partial_kernel,
        shape((SIDE, PAYLOAD, HD), BF),
        [SM] + [VM] * (1 + SIDE),
        flops=10**8,
        moved=3 * 2**20,
        scratch=[
            pltpu.VMEM((SIDE, ROWS, HD), F32),
            pltpu.VMEM((SIDE, ROWS, HD), BF),
            pltpu.VMEM((2 * HD, HD), F32),
        ],
    )(lengths, everyone, *blocks)
    gathered = across(payload)

    finished, here = call(
        merge_kernel,
        (shape((GROUPS, QROWS, HD), BF), shape((RES, QROWS, HD), BF)),
        [SM, VM, VM],
    )(origin, gathered, everyone)
    returned = lax.all_to_all(finished, "group", 0, 0, tiled=True)

    result = call(select_kernel, shape((SLOTS, QROWS, HD), BF), [SM, VM, VM])(target, returned, here)
    result = result.reshape(SLOTS, HEADS, STEPS, HD).transpose(0, 2, 1, 3)
    return result.reshape(SLOTS, STEPS, HEADS * HD)


def solution(mesh):
    in_specs = (
        P("group", None, "tensor"),
        P("group", None, None),
        P("group", "tensor", None),
        P("group", "tensor", None),
        P(),
        P(),
        P(),
        P(),
    )
    out_specs = P("group", None, "tensor")
    return jax.shard_map(body, mesh=mesh, in_specs=in_specs, out_specs=out_specs, check_vma=False)
```

```python
import math

import jax
import jax.numpy as jnp
from jax import lax
from jax.experimental import pallas as pl
from jax.experimental.pallas import tpu as pltpu
from jax.sharding import PartitionSpec as P

H = 64
KVH = 8
HD = 128
STEPS = 4
MIG = 8
RES = 4
SLOTS = MIG + RES
GROUPS = 32
SHARDS = 16
SIDE = 4
STRIDE = 32
HEADS = H // SHARDS
PAIRS = KVH // SIDE
QROWS = HEADS * STEPS
ROWS = SLOTS * QROWS
FEATURES = KVH * HD
TILES = HEADS + 1
ENTRIES = SLOTS * STEPS
PAYLOAD = ROWS + 16
FLOOR = -(2.0**100)
SCALE = 1.0 / math.sqrt(HD)
LIMIT = 48 * 1024 * 1024
FULL = 63 * 1024 * 1024
BF = jnp.bfloat16
F32 = jnp.float32

VM = pl.BlockSpec(memory_space=pltpu.VMEM)
SM = pl.BlockSpec(memory_space=pltpu.SMEM)
HB = pl.BlockSpec(memory_space=pltpu.HBM)


def call(kernel, outs, specs, flops=0, moved=0, scratch=(), limit=LIMIT):
    return pl.pallas_call(
        kernel,
        out_shape=outs,
        in_specs=specs,
        out_specs=jax.tree.map(lambda _: VM, outs),
        scratch_shapes=scratch,
        compiler_params=pltpu.CompilerParams(vmem_limit_bytes=limit),
        cost_estimate=pl.CostEstimate(flops=flops, bytes_accessed=moved, transcendentals=0),
    )


def swapped(step, y, x):
    return y ^ (step % 2), x ^ (step // 2 * 3)


def class_of(y, x):
    return jnp.minimum(y, 3 - y), x // 2


def place_of():
    shard = lax.axis_index("tensor")
    return shard // SIDE, shard % SIDE


def pack_kernel(named, holders, asked, fresh, sent, kept, asked_here, fresh_here, named_here, holders_here, sems):
    shard = lax.axis_index("tensor")
    first = pl.multiple_of(shard % 2 * FEATURES + shard // 2 * HD, HD)
    copies = [
        pltpu.make_async_copy(source, target, sems.at[n])
        for n, (source, target) in enumerate(
            (
                (named, named_here),
                (holders, holders_here),
                (asked, asked_here),
                (fresh.at[:, :, pl.ds(first, HD)], fresh_here),
            )
        )
    ]
    for copy in copies:
        copy.start()
    sent[...] = jnp.zeros_like(sent)
    for copy in copies:
        copy.wait()
    names = named_here[...]
    slots = holders_here[...].astype(F32)
    for slot in range(RES):
        kept[slot, :HEADS] = asked_here[slot]
        kept[slot, HEADS] = fresh_here[slot]
    groups = []
    for slot in range(RES, SLOTS):
        mine = names == lax.axis_index("group") * SLOTS + slot
        groups.append(jnp.sum(jnp.where(mine, slots, 0.0)).astype(jnp.int32) // MIG)
    for slot, group in zip(range(RES, SLOTS), groups):
        sent[group, :HEADS] = asked_here[slot]
        sent[group, HEADS] = fresh_here[slot]


def split_kernel(moved, resident, *outs):
    here = place_of()
    for step, out in enumerate(outs):
        low, half = class_of(*swapped(step, *here))
        for place, pair in enumerate((2 * low + half, 6 - 2 * low + half)):
            for part in range(2):
                lanes = pl.ds(pl.multiple_of(pair * HD + part * FEATURES, HD), HD)
                columns = slice((part * PAIRS + place) * HD, (part * PAIRS + place + 1) * HD)
                out[:MIG, :, columns] = moved[:, :, lanes]
                out[MIG:, :, columns] = resident[:, :, lanes]


def spread_kernel(origin, arrived, kept, asking):
    for row in range(SLOTS):
        chunk = arrived.at[origin[row]] if row < MIG else kept.at[row - MIG]
        for peer in range(SIDE):
            asking[peer, row * HEADS : (row + 1) * HEADS] = chunk[:HEADS]
            asking[peer, SLOTS * HEADS + row] = chunk[HEADS]


def scores_of(left, right):
    return lax.dot_general(left, right, (((1,), (1,)), ((), ())), preferred_element_type=F32) * SCALE


def partial_kernel(lengths, asking, *rest):
    *blocks, payload, scores, weights, stats = rest
    column = lax.broadcasted_iota(jnp.int32, (1, HD), 1)
    y, x = swapped(column // STRIDE, *place_of())
    position = (y * SIDE + x) * STRIDE + column % STRIDE

    def stored(row, place):
        lanes = slice(place * HD, (place + 1) * HD)
        return jnp.concatenate([block[row, :, lanes] for block in blocks], 0)

    for row in range(SLOTS):
        usable = position < lengths[row]
        span = slice(row * QROWS, (row + 1) * QROWS)
        for pair in range(PAIRS):
            asked = jnp.concatenate([asking[2 * pair, span, :], asking[2 * pair + 1, span, :]], 0)
            found = jnp.where(usable, scores_of(asked, stored(row, pair)), FLOOR)
            scores[2 * pair, span, :] = found[:QROWS]
            scores[2 * pair + 1, span, :] = found[QROWS:]
    lane = lax.broadcasted_iota(jnp.int32, (ROWS, HD), 1)
    table = jnp.zeros((ROWS, HD), F32)
    for peer in range(SIDE):
        found = scores[peer]
        top = jnp.max(found, axis=1, keepdims=True)
        first = top.astype(BF).astype(F32)
        second = (top - first).astype(BF).astype(F32)
        weight = jnp.exp(found - (first + second))
        total = jnp.sum(weight, axis=1, keepdims=True)
        weights[peer] = weight.astype(BF)
        total_first = total.astype(BF).astype(F32)
        for place, value in enumerate((first, total_first, second, total - total_first)):
            table = jnp.where(lane == peer * 8 + place, value, table)
    stats[:ROWS, :] = table
    stats[ROWS:, :] = jnp.zeros((2 * HD - ROWS, HD), F32)
    low = stats[:HD, :].T
    high = stats[HD:, :].T
    for peer in range(SIDE):
        rows = slice(peer * 8, (peer + 1) * 8)
        payload[peer, ROWS:, :] = jnp.concatenate([low[rows], high[rows]], 0).astype(BF)
    for row in range(SLOTS):
        span = slice(row * QROWS, (row + 1) * QROWS)
        for pair in range(PAIRS):
            weight = jnp.concatenate([weights[2 * pair, span, :], weights[2 * pair + 1, span, :]], 0)
            blended = jnp.dot(weight, stored(row, PAIRS + pair), preferred_element_type=F32).astype(BF)
            payload[2 * pair, span, :] = blended[:QROWS]
            payload[2 * pair + 1, span, :] = blended[QROWS:]


def merge_kernel(origin, gathered, everyone, sent, kept):
    y, x = place_of()
    first = jnp.where(y > 1, 2, 0)
    asked = everyone[first + x % 2, :ROWS, :]
    keys = everyone[first, ROWS:, :]
    values = everyone[first + 1, ROWS:, :]
    row = lax.broadcasted_iota(jnp.int32, (ROWS, ENTRIES), 0)
    lane = lax.broadcasted_iota(jnp.int32, (ROWS, ENTRIES), 1)
    causal = (lane // STEPS == row // QROWS) & (lane % STEPS <= row % STEPS)
    fresh = jnp.where(causal, scores_of(asked, keys), FLOOR)
    fresh_top = jnp.max(fresh, axis=1, keepdims=True)

    tops = gathered[:, ROWS:, :].astype(F32)
    blank = jnp.zeros((HD - SIDE * 8, HD), F32)
    low = jnp.concatenate([tops[:, :8, :].reshape(SIDE * 8, HD), blank], 0).T
    high = jnp.concatenate([tops[:, 8:, :].reshape(SIDE * 8, HD), blank], 0).T[: ROWS - HD]
    pairs = jnp.concatenate([low, high], 0)
    both = pairs + pltpu.roll(pairs, HD - 2, 1)
    lane = lax.broadcasted_iota(jnp.int32, (ROWS, HD), 1)
    is_top = (lane % 8 == 0) & (lane < SIDE * 8)
    tops = jnp.where(is_top, both, FLOOR)
    sums = pltpu.roll(both, HD - 1, 1)
    highest = jnp.maximum(jnp.max(tops, axis=1, keepdims=True), fresh_top)
    factors = jnp.where(is_top, jnp.exp(tops - highest), 0.0)
    fresh_weights = jnp.where(causal, jnp.exp(fresh - highest), 0.0)
    totals = jnp.sum(jnp.where(is_top, factors * sums, 0.0), axis=1, keepdims=True)
    totals += jnp.sum(fresh_weights, axis=1, keepdims=True)
    blended = jnp.dot(fresh_weights.astype(BF), values, preferred_element_type=F32)
    for peer in range(SIDE):
        blended += factors[:, peer * 8 : peer * 8 + 1] * gathered[peer, :ROWS, :].astype(F32)
    result = (blended / totals).astype(BF)

    sent[...] = jnp.zeros_like(sent)
    for slot in range(MIG):
        sent[origin[slot]] = result[slot * QROWS : (slot + 1) * QROWS]
    for slot in range(RES):
        kept[slot] = result[(MIG + slot) * QROWS : (MIG + slot + 1) * QROWS]


def select_kernel(target, returned, kept, out):
    for slot in range(RES):
        out[slot] = kept[slot]
    for slot in range(MIG):
        out[RES + slot] = returned[target[slot]]


def body(
    queries,
    new_entries,
    resident_cache,
    prefill_cache,
    resident_kept,
    kept_tokens,
    prefill_slot,
    decode_slot,
):
    shape = jax.ShapeDtypeStruct
    whole = [(y, x) for y in range(SIDE) for x in range(SIDE)]
    peers = [[y * SIDE + x for y in (low, 3 - low) for x in (2 * half, 2 * half + 1)] for low in range(2) for half in range(2)]

    def across(array):
        return lax.all_to_all(array, "tensor", 0, 0, axis_index_groups=peers, tiled=True)

    asked = queries.reshape(SLOTS, STEPS, HEADS, HD).transpose(0, 2, 1, 3)
    sent, kept = call(
        pack_kernel,
        (shape((GROUPS, TILES, STEPS, HD), BF), shape((RES, TILES, STEPS, HD), BF)),
        [HB] * 4,
        scratch=[
            pltpu.VMEM((SLOTS, HEADS, STEPS, HD), BF),
            pltpu.VMEM((SLOTS, STEPS, HD), BF),
            pltpu.VMEM((2, HD), jnp.int32),
            pltpu.VMEM((2, HD), jnp.int32),
            pltpu.SemaphoreType.DMA((4,)),
        ],
        limit=FULL,
    )(decode_slot.reshape(2, HD), prefill_slot.reshape(2, HD), asked, new_entries)
    arrived = lax.all_to_all(sent, "group", 0, 0, tiled=True)

    later = (resident_kept, kept_tokens, prefill_slot, decode_slot, prefill_cache, resident_cache)
    later, kept = lax.optimization_barrier((later, kept))
    resident_kept, kept_tokens, prefill_slot, decode_slot, prefill_cache, resident_cache = later
    group = lax.axis_index("group")

    def looked_up(names, first, values):
        wanted = first + jnp.arange(MIG, dtype=jnp.int32)
        return jnp.sum(jnp.where(names[None, :] == wanted[:, None], values[None, :], 0), axis=1)

    target = looked_up(decode_slot, group * SLOTS + RES, prefill_slot) // MIG
    origin = looked_up(prefill_slot, group * MIG, decode_slot) // SLOTS
    moved_len = looked_up(prefill_slot, group * MIG, kept_tokens)
    resident_len = lax.dynamic_slice_in_dim(resident_kept, group * RES, RES)
    lengths = jnp.concatenate([moved_len, resident_len])

    split = call(
        split_kernel,
        (shape((SLOTS, STRIDE, 2 * PAIRS * HD), BF),) * SIDE,
        [VM, VM],
        moved=3 * 2**20,
    )(prefill_cache, resident_cache)
    blocks = [split[0]]
    for step in range(1, SIDE):
        steps = []
        for y, x in whole:
            other, side = swapped(step, y, x)
            steps.append((y * SIDE + x, other * SIDE + side))
        blocks.append(lax.ppermute(split[step], "tensor", steps))

    asking = call(
        spread_kernel, shape((SIDE, SLOTS * TILES, STEPS, HD), BF), [SM, VM, VM]
    )(origin, arrived, kept)
    everyone = across(asking).reshape(SIDE, ROWS + ENTRIES, HD)

    payload = call(
        partial_kernel,
        shape((SIDE, PAYLOAD, HD), BF),
        [SM] + [VM] * (1 + SIDE),
        flops=10**8,
        moved=3 * 2**20,
        scratch=[
            pltpu.VMEM((SIDE, ROWS, HD), F32),
            pltpu.VMEM((SIDE, ROWS, HD), BF),
            pltpu.VMEM((2 * HD, HD), F32),
        ],
    )(lengths, everyone, *blocks)
    gathered = across(payload)

    finished, here = call(
        merge_kernel,
        (shape((GROUPS, QROWS, HD), BF), shape((RES, QROWS, HD), BF)),
        [SM, VM, VM],
    )(origin, gathered, everyone)
    returned = lax.all_to_all(finished, "group", 0, 0, tiled=True)

    result = call(select_kernel, shape((SLOTS, QROWS, HD), BF), [SM, VM, VM])(target, returned, here)
    result = result.reshape(SLOTS, HEADS, STEPS, HD).transpose(0, 2, 1, 3)
    return result.reshape(SLOTS, STEPS, HEADS * HD)


def solution(mesh):
    in_specs = (
        P("group", None, "tensor"),
        P("group", None, None),
        P("group", "tensor", None),
        P("group", "tensor", None),
        P(),
        P(),
        P(),
        P(),
    )
    out_specs = P("group", None, "tensor")
    return jax.shard_map(body, mesh=mesh, in_specs=in_specs, out_specs=out_specs, check_vma=False)
```

```python
import math

import jax
import jax.numpy as jnp
from jax import lax
from jax.experimental import pallas as pl
from jax.experimental.pallas import tpu as pltpu
from jax.sharding import PartitionSpec as P

H = 64
KVH = 8
HD = 128
STEPS = 4
MIG = 8
RES = 4
SLOTS = MIG + RES
GROUPS = 32
SHARDS = 16
SIDE = 4
STRIDE = 32
HEADS = H // SHARDS
BLOCKS = 2
PEERS = SHARDS // BLOCKS
PAIRS = PEERS // 2
WIDE = BLOCKS * STRIDE
QROWS = HEADS * STEPS
ROWS = SLOTS * QROWS
FEATURES = KVH * HD
TILES = HEADS + 1
ENTRIES = SLOTS * STEPS
PAYLOAD = ROWS + 16
FLOOR = -(2.0**100)
SCALE = 1.0 / math.sqrt(HD)
LIMIT = 48 * 1024 * 1024
FULL = 63 * 1024 * 1024
BF = jnp.bfloat16
F32 = jnp.float32

VM = pl.BlockSpec(memory_space=pltpu.VMEM)
SM = pl.BlockSpec(memory_space=pltpu.SMEM)
HB = pl.BlockSpec(memory_space=pltpu.HBM)


def call(kernel, outs, specs, flops=0, moved=0, scratch=(), limit=LIMIT):
    return pl.pallas_call(
        kernel,
        out_shape=outs,
        in_specs=specs,
        out_specs=jax.tree.map(lambda _: VM, outs),
        scratch_shapes=scratch,
        compiler_params=pltpu.CompilerParams(vmem_limit_bytes=limit),
        cost_estimate=pl.CostEstimate(flops=flops, bytes_accessed=moved, transcendentals=0),
    )


def swapped(step, x):
    return x ^ (step * 3)


def place_of():
    shard = lax.axis_index("tensor")
    return shard // SIDE, shard % SIDE


def pack_kernel(named, holders, asked, fresh, sent, kept, asked_here, fresh_here, named_here, holders_here, sems):
    shard = lax.axis_index("tensor")
    first = pl.multiple_of(shard % 2 * FEATURES + shard // 2 * HD, HD)
    copies = [
        pltpu.make_async_copy(source, target, sems.at[n])
        for n, (source, target) in enumerate(
            (
                (named, named_here),
                (holders, holders_here),
                (asked, asked_here),
                (fresh.at[:, :, pl.ds(first, HD)], fresh_here),
            )
        )
    ]
    for copy in copies:
        copy.start()
    sent[...] = jnp.zeros_like(sent)
    for copy in copies:
        copy.wait()
    names = named_here[...]
    slots = holders_here[...].astype(F32)
    for slot in range(RES):
        kept[slot, :HEADS] = asked_here[slot]
        kept[slot, HEADS] = fresh_here[slot]
    groups = []
    for slot in range(RES, SLOTS):
        mine = names == lax.axis_index("group") * SLOTS + slot
        groups.append(jnp.sum(jnp.where(mine, slots, 0.0)).astype(jnp.int32) // MIG)
    for slot, group in zip(range(RES, SLOTS), groups):
        sent[group, :HEADS] = asked_here[slot]
        sent[group, HEADS] = fresh_here[slot]


def split_kernel(moved, resident, *outs):
    _, here = place_of()
    for step, out in enumerate(outs):
        half = swapped(step, here) // 2
        for place in range(PAIRS):
            for part in range(2):
                lanes = pl.ds(pl.multiple_of((2 * place + half) * HD + part * FEATURES, HD), HD)
                columns = slice((part * PAIRS + place) * HD, (part * PAIRS + place + 1) * HD)
                out[:MIG, :, columns] = moved[:, :, lanes]
                out[MIG:, :, columns] = resident[:, :, lanes]


def spread_kernel(origin, arrived, kept, asking):
    for row in range(SLOTS):
        chunk = arrived.at[origin[row]] if row < MIG else kept.at[row - MIG]
        for peer in range(PEERS):
            asking[peer, row * HEADS : (row + 1) * HEADS] = chunk[:HEADS]
            asking[peer, SLOTS * HEADS + row] = chunk[HEADS]


def scores_of(left, right):
    return lax.dot_general(left, right, (((1,), (1,)), ((), ())), preferred_element_type=F32) * SCALE


def partial_kernel(lengths, asking, *rest):
    *blocks, payload, scores, weights, stats = rest
    y, x = place_of()
    column = lax.broadcasted_iota(jnp.int32, (1, WIDE), 1)
    position = (y * SIDE + swapped(column // STRIDE, x)) * STRIDE + column % STRIDE

    def stored(row, place):
        lanes = slice(place * HD, (place + 1) * HD)
        return jnp.concatenate([block[row, :, lanes] for block in blocks], 0)

    for row in range(SLOTS):
        usable = position < lengths[row]
        span = slice(row * QROWS, (row + 1) * QROWS)
        for pair in range(PAIRS):
            asked = jnp.concatenate([asking[2 * pair, span, :], asking[2 * pair + 1, span, :]], 0)
            found = jnp.where(usable, scores_of(asked, stored(row, pair)), FLOOR)
            scores[2 * pair, span, :] = found[:QROWS]
            scores[2 * pair + 1, span, :] = found[QROWS:]
    lane = lax.broadcasted_iota(jnp.int32, (ROWS, HD), 1)
    table = jnp.zeros((ROWS, HD), F32)
    for peer in range(PEERS):
        found = scores[peer]
        top = jnp.max(found, axis=1, keepdims=True)
        first = top.astype(BF).astype(F32)
        second = (top - first).astype(BF).astype(F32)
        weight = jnp.exp(found - (first + second))
        total = jnp.sum(weight, axis=1, keepdims=True)
        weights[peer] = weight.astype(BF)
        total_first = total.astype(BF).astype(F32)
        for place, value in enumerate((first, total_first, second, total - total_first)):
            table = jnp.where(lane == peer * 8 + place, value, table)
    stats[:ROWS, :] = table
    stats[ROWS:, :] = jnp.zeros((2 * HD - ROWS, HD), F32)
    low = stats[:HD, :].T
    high = stats[HD:, :].T
    for peer in range(PEERS):
        rows = slice(peer * 8, (peer + 1) * 8)
        payload[peer, ROWS:, :] = jnp.concatenate([low[rows], high[rows]], 0).astype(BF)
    for row in range(SLOTS):
        span = slice(row * QROWS, (row + 1) * QROWS)
        for pair in range(PAIRS):
            weight = jnp.concatenate([weights[2 * pair, span, :], weights[2 * pair + 1, span, :]], 0)
            blended = jnp.dot(weight, stored(row, PAIRS + pair), preferred_element_type=F32).astype(BF)
            payload[2 * pair, span, :] = blended[:QROWS]
            payload[2 * pair + 1, span, :] = blended[QROWS:]


def merge_kernel(origin, gathered, everyone, sent, kept):
    y, x = place_of()
    first = 2 * y
    asked = everyone[first + x % 2, :ROWS, :]
    keys = everyone[first, ROWS:, :]
    values = everyone[first + 1, ROWS:, :]
    row = lax.broadcasted_iota(jnp.int32, (ROWS, ENTRIES), 0)
    lane = lax.broadcasted_iota(jnp.int32, (ROWS, ENTRIES), 1)
    causal = (lane // STEPS == row // QROWS) & (lane % STEPS <= row % STEPS)
    fresh = jnp.where(causal, scores_of(asked, keys), FLOOR)
    fresh_top = jnp.max(fresh, axis=1, keepdims=True)

    tops = gathered[:, ROWS:, :].astype(F32)
    blank = jnp.zeros((HD - PEERS * 8, HD), F32)
    low = jnp.concatenate([tops[:, :8, :].reshape(PEERS * 8, HD), blank], 0).T
    high = jnp.concatenate([tops[:, 8:, :].reshape(PEERS * 8, HD), blank], 0).T[: ROWS - HD]
    pairs = jnp.concatenate([low, high], 0)
    both = pairs + pltpu.roll(pairs, HD - 2, 1)
    lane = lax.broadcasted_iota(jnp.int32, (ROWS, HD), 1)
    is_top = (lane % 8 == 0) & (lane < PEERS * 8)
    tops = jnp.where(is_top, both, FLOOR)
    sums = pltpu.roll(both, HD - 1, 1)
    highest = jnp.maximum(jnp.max(tops, axis=1, keepdims=True), fresh_top)
    factors = jnp.where(is_top, jnp.exp(tops - highest), 0.0)
    fresh_weights = jnp.where(causal, jnp.exp(fresh - highest), 0.0)
    totals = jnp.sum(jnp.where(is_top, factors * sums, 0.0), axis=1, keepdims=True)
    totals += jnp.sum(fresh_weights, axis=1, keepdims=True)
    blended = jnp.dot(fresh_weights.astype(BF), values, preferred_element_type=F32)
    for peer in range(PEERS):
        blended += factors[:, peer * 8 : peer * 8 + 1] * gathered[peer, :ROWS, :].astype(F32)
    result = (blended / totals).astype(BF)

    sent[...] = jnp.zeros_like(sent)
    for slot in range(MIG):
        sent[origin[slot]] = result[slot * QROWS : (slot + 1) * QROWS]
    for slot in range(RES):
        kept[slot] = result[(MIG + slot) * QROWS : (MIG + slot + 1) * QROWS]


def select_kernel(target, returned, kept, out):
    for slot in range(RES):
        out[slot] = kept[slot]
    for slot in range(MIG):
        out[RES + slot] = returned[target[slot]]


def body(
    queries,
    new_entries,
    resident_cache,
    prefill_cache,
    resident_kept,
    kept_tokens,
    prefill_slot,
    decode_slot,
):
    shape = jax.ShapeDtypeStruct
    peers = [[y * SIDE + 2 * half + x for y in range(SIDE) for x in range(2)] for half in range(2)]

    def across(array):
        return lax.all_to_all(array, "tensor", 0, 0, axis_index_groups=peers, tiled=True)

    asked = queries.reshape(SLOTS, STEPS, HEADS, HD).transpose(0, 2, 1, 3)
    sent, kept = call(
        pack_kernel,
        (shape((GROUPS, TILES, STEPS, HD), BF), shape((RES, TILES, STEPS, HD), BF)),
        [HB] * 4,
        scratch=[
            pltpu.VMEM((SLOTS, HEADS, STEPS, HD), BF),
            pltpu.VMEM((SLOTS, STEPS, HD), BF),
            pltpu.VMEM((2, HD), jnp.int32),
            pltpu.VMEM((2, HD), jnp.int32),
            pltpu.SemaphoreType.DMA((4,)),
        ],
        limit=FULL,
    )(decode_slot.reshape(2, HD), prefill_slot.reshape(2, HD), asked, new_entries)
    arrived = lax.all_to_all(sent, "group", 0, 0, tiled=True)

    later = (resident_kept, kept_tokens, prefill_slot, decode_slot, prefill_cache, resident_cache)
    later, kept = lax.optimization_barrier((later, kept))
    resident_kept, kept_tokens, prefill_slot, decode_slot, prefill_cache, resident_cache = later
    group = lax.axis_index("group")

    def looked_up(names, first, values):
        wanted = first + jnp.arange(MIG, dtype=jnp.int32)
        return jnp.sum(jnp.where(names[None, :] == wanted[:, None], values[None, :], 0), axis=1)

    target = looked_up(decode_slot, group * SLOTS + RES, prefill_slot) // MIG
    origin = looked_up(prefill_slot, group * MIG, decode_slot) // SLOTS
    moved_len = looked_up(prefill_slot, group * MIG, kept_tokens)
    resident_len = lax.dynamic_slice_in_dim(resident_kept, group * RES, RES)
    lengths = jnp.concatenate([moved_len, resident_len])

    split = call(
        split_kernel,
        (shape((SLOTS, STRIDE, 2 * PAIRS * HD), BF),) * BLOCKS,
        [VM, VM],
        moved=3 * 2**20,
    )(prefill_cache, resident_cache)
    blocks = [split[0]]
    for step in range(1, BLOCKS):
        steps = [(t, t // SIDE * SIDE + swapped(step, t % SIDE)) for t in range(SHARDS)]
        blocks.append(lax.ppermute(split[step], "tensor", steps))

    asking = call(
        spread_kernel, shape((PEERS, SLOTS * TILES, STEPS, HD), BF), [SM, VM, VM]
    )(origin, arrived, kept)
    everyone = across(asking).reshape(PEERS, ROWS + ENTRIES, HD)

    payload = call(
        partial_kernel,
        shape((PEERS, PAYLOAD, HD), BF),
        [SM] + [VM] * (1 + BLOCKS),
        flops=10**8,
        moved=3 * 2**20,
        scratch=[
            pltpu.VMEM((PEERS, ROWS, WIDE), F32),
            pltpu.VMEM((PEERS, ROWS, WIDE), BF),
            pltpu.VMEM((2 * HD, HD), F32),
        ],
    )(lengths, everyone, *blocks)
    gathered = across(payload)

    finished, here = call(
        merge_kernel,
        (shape((GROUPS, QROWS, HD), BF), shape((RES, QROWS, HD), BF)),
        [SM, VM, VM],
    )(origin, gathered, everyone)
    returned = lax.all_to_all(finished, "group", 0, 0, tiled=True)

    result = call(select_kernel, shape((SLOTS, QROWS, HD), BF), [SM, VM, VM])(target, returned, here)
    result = result.reshape(SLOTS, HEADS, STEPS, HD).transpose(0, 2, 1, 3)
    return result.reshape(SLOTS, STEPS, HEADS * HD)


def solution(mesh):
    in_specs = (
        P("group", None, "tensor"),
        P("group", None, None),
        P("group", "tensor", None),
        P("group", "tensor", None),
        P(),
        P(),
        P(),
        P(),
    )
    out_specs = P("group", None, "tensor")
    return jax.shard_map(body, mesh=mesh, in_specs=in_specs, out_specs=out_specs, check_vma=False)
```

```python
import math

import jax
import jax.numpy as jnp
from jax import lax
from jax.experimental import pallas as pl
from jax.experimental.pallas import tpu as pltpu
from jax.sharding import PartitionSpec as P

H = 64
KVH = 8
HD = 128
STEPS = 4
MIG = 8
RES = 4
SLOTS = MIG + RES
GROUPS = 32
SHARDS = 16
SIDE = 4
STRIDE = 32
HEADS = H // SHARDS
PAIRS = KVH // SIDE
QROWS = HEADS * STEPS
ROWS = SLOTS * QROWS
FEATURES = KVH * HD
TILES = HEADS + 1
ENTRIES = SLOTS * STEPS
PAYLOAD = ROWS + 16
FLOOR = -(2.0**100)
SCALE = 1.0 / math.sqrt(HD)
LIMIT = 48 * 1024 * 1024
FULL = 63 * 1024 * 1024
BF = jnp.bfloat16
F32 = jnp.float32

VM = pl.BlockSpec(memory_space=pltpu.VMEM)
SM = pl.BlockSpec(memory_space=pltpu.SMEM)
HB = pl.BlockSpec(memory_space=pltpu.HBM)


def call(kernel, outs, specs, flops=0, moved=0, scratch=(), limit=LIMIT):
    return pl.pallas_call(
        kernel,
        out_shape=outs,
        in_specs=specs,
        out_specs=jax.tree.map(lambda _: VM, outs),
        scratch_shapes=scratch,
        compiler_params=pltpu.CompilerParams(vmem_limit_bytes=limit),
        cost_estimate=pl.CostEstimate(flops=flops, bytes_accessed=moved, transcendentals=0),
    )


def swapped(step, y, x):
    return y ^ (step % 2), x ^ (step // 2 * 3)


def class_of(y, x):
    return jnp.minimum(y, 3 - y), x // 2


def place_of():
    shard = lax.axis_index("tensor")
    return shard // SIDE, shard % SIDE


def pack_kernel(named, holders, asked, fresh, moved, resident, *rest):
    sent, kept, *blocks = rest[: 2 + SIDE]
    asked_here, fresh_here, named_here, holders_here, moved_here, resident_here, sems = rest[2 + SIDE :]
    shard = lax.axis_index("tensor")
    first = pl.multiple_of(shard % 2 * FEATURES + shard // 2 * HD, HD)
    pairs = (
        (named, named_here),
        (holders, holders_here),
        (asked, asked_here),
        (fresh.at[:, :, pl.ds(first, HD)], fresh_here),
        (moved, moved_here),
        (resident, resident_here),
    )
    copies = [pltpu.make_async_copy(*pair, sems.at[n]) for n, pair in enumerate(pairs)]
    for copy in copies:
        copy.start()
    sent[...] = jnp.zeros_like(sent)
    for copy in copies[:4]:
        copy.wait()
    names = named_here[...]
    slots = holders_here[...].astype(F32)
    for slot in range(RES):
        kept[slot, :HEADS] = asked_here[slot]
        kept[slot, HEADS] = fresh_here[slot]
    groups = []
    for slot in range(RES, SLOTS):
        mine = names == lax.axis_index("group") * SLOTS + slot
        groups.append(jnp.sum(jnp.where(mine, slots, 0.0)).astype(jnp.int32) // MIG)
    for slot, group in zip(range(RES, SLOTS), groups):
        sent[group, :HEADS] = asked_here[slot]
        sent[group, HEADS] = fresh_here[slot]
    for copy in copies[4:]:
        copy.wait()
    here = place_of()
    for step, block in enumerate(blocks):
        low, half = class_of(*swapped(step, *here))
        for place, pair in enumerate((2 * low + half, 6 - 2 * low + half)):
            for part in range(2):
                lanes = pl.ds(pl.multiple_of(pair * HD + part * FEATURES, HD), HD)
                columns = slice((part * PAIRS + place) * HD, (part * PAIRS + place + 1) * HD)
                block[:MIG, :, columns] = moved_here[:, :, lanes]
                block[MIG:, :, columns] = resident_here[:, :, lanes]


def spread_kernel(origin, arrived, kept, asking):
    core = lax.axis_index("group") % 2
    for row in range(SLOTS):
        if row < MIG:
            chunk = arrived.at[origin[row] % 2, origin[row] // 2, core]
        else:
            chunk = kept.at[row - MIG]
        for peer in range(SIDE):
            asking[peer, row * HEADS : (row + 1) * HEADS] = chunk[:HEADS]
            asking[peer, SLOTS * HEADS + row] = chunk[HEADS]


def scores_of(left, right):
    return lax.dot_general(left, right, (((1,), (1,)), ((), ())), preferred_element_type=F32) * SCALE


def partial_kernel(lengths, asking, *rest):
    *blocks, payload, scores, weights, stats = rest
    column = lax.broadcasted_iota(jnp.int32, (1, HD), 1)
    block = column // STRIDE
    y, x = swapped(jnp.where(block == 0, 0, (block + 1) % 3 + 1), *place_of())
    position = (y * SIDE + x) * STRIDE + column % STRIDE

    def stored(row, place):
        lanes = slice(place * HD, (place + 1) * HD)
        return jnp.concatenate([block[row, :, lanes] for block in blocks], 0)

    for row in range(SLOTS):
        usable = position < lengths[row]
        span = slice(row * QROWS, (row + 1) * QROWS)
        for pair in range(PAIRS):
            asked = jnp.concatenate([asking[2 * pair, span, :], asking[2 * pair + 1, span, :]], 0)
            found = jnp.where(usable, scores_of(asked, stored(row, pair)), FLOOR)
            scores[2 * pair, span, :] = found[:QROWS]
            scores[2 * pair + 1, span, :] = found[QROWS:]
    lane = lax.broadcasted_iota(jnp.int32, (ROWS, HD), 1)
    table = jnp.zeros((ROWS, HD), F32)
    for peer in range(SIDE):
        found = scores[peer]
        top = jnp.max(found, axis=1, keepdims=True)
        first = top.astype(BF).astype(F32)
        second = (top - first).astype(BF).astype(F32)
        weight = jnp.exp(found - (first + second))
        total = jnp.sum(weight, axis=1, keepdims=True)
        weights[peer] = weight.astype(BF)
        total_first = total.astype(BF).astype(F32)
        for place, value in enumerate((first, total_first, second, total - total_first)):
            table = jnp.where(lane == peer * 8 + place, value, table)
    stats[:ROWS, :] = table
    stats[ROWS:, :] = jnp.zeros((2 * HD - ROWS, HD), F32)
    low = stats[:HD, :].T
    high = stats[HD:, :].T
    for peer in range(SIDE):
        rows = slice(peer * 8, (peer + 1) * 8)
        payload[peer, ROWS:, :] = jnp.concatenate([low[rows], high[rows]], 0).astype(BF)
    for row in range(SLOTS):
        span = slice(row * QROWS, (row + 1) * QROWS)
        for pair in range(PAIRS):
            weight = jnp.concatenate([weights[2 * pair, span, :], weights[2 * pair + 1, span, :]], 0)
            blended = jnp.dot(weight, stored(row, PAIRS + pair), preferred_element_type=F32).astype(BF)
            payload[2 * pair, span, :] = blended[:QROWS]
            payload[2 * pair + 1, span, :] = blended[QROWS:]


def merge_kernel(origin, target, gathered, everyone, sent, kept):
    y, x = place_of()
    first = jnp.where(y > 1, 2, 0)
    asked = everyone[first + x % 2, :ROWS, :]
    keys = everyone[first, ROWS:, :]
    values = everyone[first + 1, ROWS:, :]
    row = lax.broadcasted_iota(jnp.int32, (ROWS, ENTRIES), 0)
    lane = lax.broadcasted_iota(jnp.int32, (ROWS, ENTRIES), 1)
    causal = (lane // STEPS == row // QROWS) & (lane % STEPS <= row % STEPS)
    fresh = jnp.where(causal, scores_of(asked, keys), FLOOR)
    fresh_top = jnp.max(fresh, axis=1, keepdims=True)

    tops = gathered[:, ROWS:, :].astype(F32)
    blank = jnp.zeros((HD - SIDE * 8, HD), F32)
    low = jnp.concatenate([tops[:, :8, :].reshape(SIDE * 8, HD), blank], 0).T
    high = jnp.concatenate([tops[:, 8:, :].reshape(SIDE * 8, HD), blank], 0).T[: ROWS - HD]
    pairs = jnp.concatenate([low, high], 0)
    both = pairs + pltpu.roll(pairs, HD - 2, 1)
    lane = lax.broadcasted_iota(jnp.int32, (ROWS, HD), 1)
    is_top = (lane % 8 == 0) & (lane < SIDE * 8)
    tops = jnp.where(is_top, both, FLOOR)
    sums = pltpu.roll(both, HD - 1, 1)
    highest = jnp.maximum(jnp.max(tops, axis=1, keepdims=True), fresh_top)
    factors = jnp.where(is_top, jnp.exp(tops - highest), 0.0)
    fresh_weights = jnp.where(causal, jnp.exp(fresh - highest), 0.0)
    totals = jnp.sum(jnp.where(is_top, factors * sums, 0.0), axis=1, keepdims=True)
    totals += jnp.sum(fresh_weights, axis=1, keepdims=True)
    blended = jnp.dot(fresh_weights.astype(BF), values, preferred_element_type=F32)
    for peer in range(SIDE):
        blended += factors[:, peer * 8 : peer * 8 + 1] * gathered[peer, :ROWS, :].astype(F32)
    result = (blended / totals).astype(BF)

    sent[...] = jnp.zeros_like(sent)
    for slot in range(MIG):
        sent[origin[slot]] = result[slot * QROWS : (slot + 1) * QROWS]
    for slot in range(RES):
        kept[slot] = result[(MIG + slot) * QROWS : (MIG + slot + 1) * QROWS]


def select_kernel(target, returned, kept, out):
    for slot in range(RES):
        out[slot] = kept[slot]
    for slot in range(MIG):
        out[RES + slot] = returned[target[slot]]


def body(
    queries,
    new_entries,
    resident_cache,
    prefill_cache,
    resident_kept,
    kept_tokens,
    prefill_slot,
    decode_slot,
):
    shape = jax.ShapeDtypeStruct
    whole = [(y, x) for y in range(SIDE) for x in range(SIDE)]
    peers = [[y * SIDE + x for y in (low, 3 - low) for x in (2 * half, 2 * half + 1)] for low in range(2) for half in range(2)]

    def across(array):
        return lax.all_to_all(array, "tensor", 0, 0, axis_index_groups=peers, tiled=True)

    asked = queries.reshape(SLOTS, STEPS, HEADS, HD).transpose(0, 2, 1, 3)
    sent, kept, *split = call(
        pack_kernel,
        (shape((GROUPS, TILES, STEPS, HD), BF), shape((RES, TILES, STEPS, HD), BF))
        + (shape((SLOTS, STRIDE, 2 * PAIRS * HD), BF),) * SIDE,
        [HB] * 6,
        moved=3 * 2**20,
        scratch=[
            pltpu.VMEM((SLOTS, HEADS, STEPS, HD), BF),
            pltpu.VMEM((SLOTS, STEPS, HD), BF),
            pltpu.VMEM((2, HD), jnp.int32),
            pltpu.VMEM((2, HD), jnp.int32),
            pltpu.VMEM((MIG, STRIDE, 2 * FEATURES), BF),
            pltpu.VMEM((RES, STRIDE, 2 * FEATURES), BF),
            pltpu.SemaphoreType.DMA((6,)),
        ],
        limit=FULL,
    )(decode_slot.reshape(2, HD), prefill_slot.reshape(2, HD), asked, new_entries, prefill_cache, resident_cache)
    layers = [[2 * z + core for z in range(GROUPS // 2)] for core in range(2)]
    chips = [[2 * z, 2 * z + 1] for z in range(GROUPS // 2)]
    sent = sent.reshape(GROUPS // 2, 2, TILES, STEPS, HD)
    arrived = lax.all_to_all(sent, "group", 0, 0, axis_index_groups=layers, tiled=True)
    arrived = lax.all_gather(arrived, "group", axis_index_groups=chips)

    later = (resident_kept, kept_tokens, prefill_slot, decode_slot)
    later, kept = lax.optimization_barrier((later, kept))
    resident_kept, kept_tokens, prefill_slot, decode_slot = later
    group = lax.axis_index("group")

    def looked_up(names, first, values):
        wanted = first + jnp.arange(MIG, dtype=jnp.int32)
        return jnp.sum(jnp.where(names[None, :] == wanted[:, None], values[None, :], 0), axis=1)

    target = looked_up(decode_slot, group * SLOTS + RES, prefill_slot) // MIG
    origin = looked_up(prefill_slot, group * MIG, decode_slot) // SLOTS
    moved_len = looked_up(prefill_slot, group * MIG, kept_tokens)
    resident_len = lax.dynamic_slice_in_dim(resident_kept, group * RES, RES)
    lengths = jnp.concatenate([moved_len, resident_len])

    blocks = [split[0]]
    for step in (3, 1, 2):
        steps = []
        for y, x in whole:
            other, side = swapped(step, y, x)
            steps.append((y * SIDE + x, other * SIDE + side))
        blocks.append(lax.ppermute(split[step], "tensor", steps))

    asking = call(
        spread_kernel, shape((SIDE, SLOTS * TILES, STEPS, HD), BF), [SM, VM, VM]
    )(origin, arrived, kept)
    everyone = across(asking).reshape(SIDE, ROWS + ENTRIES, HD)

    payload = call(
        partial_kernel,
        shape((SIDE, PAYLOAD, HD), BF),
        [SM] + [VM] * (1 + SIDE),
        flops=10**8,
        moved=3 * 2**20,
        scratch=[
            pltpu.VMEM((SIDE, ROWS, HD), F32),
            pltpu.VMEM((SIDE, ROWS, HD), BF),
            pltpu.VMEM((2 * HD, HD), F32),
        ],
    )(lengths, everyone, *blocks)
    gathered = across(payload)

    finished, here = call(
        merge_kernel,
        (shape((GROUPS, QROWS, HD), BF), shape((RES, QROWS, HD), BF)),
        [SM, SM, VM, VM],
    )(origin, target, gathered, everyone)
    returned = lax.all_to_all(finished, "group", 0, 0, tiled=True)

    result = call(select_kernel, shape((SLOTS, QROWS, HD), BF), [SM, VM, VM])(target, returned, here)
    result = result.reshape(SLOTS, HEADS, STEPS, HD).transpose(0, 2, 1, 3)
    return result.reshape(SLOTS, STEPS, HEADS * HD)


def solution(mesh):
    in_specs = (
        P("group", None, "tensor"),
        P("group", None, None),
        P("group", "tensor", None),
        P("group", "tensor", None),
        P(),
        P(),
        P(),
        P(),
    )
    out_specs = P("group", None, "tensor")
    return jax.shard_map(body, mesh=mesh, in_specs=in_specs, out_specs=out_specs, check_vma=False)
```

```python
import math

import jax
import jax.numpy as jnp
from jax import lax
from jax.experimental import pallas as pl
from jax.experimental.pallas import tpu as pltpu
from jax.sharding import PartitionSpec as P

H = 64
KVH = 8
HD = 128
STEPS = 4
MIG = 8
RES = 4
SLOTS = MIG + RES
GROUPS = 32
SHARDS = 16
SIDE = 4
STRIDE = 32
HEADS = H // SHARDS
BLOCKS = 2
PEERS = SHARDS // BLOCKS
PAIRS = PEERS // 2
WIDE = BLOCKS * STRIDE
QROWS = HEADS * STEPS
ROWS = SLOTS * QROWS
FEATURES = KVH * HD
TILES = HEADS + 1
ENTRIES = SLOTS * STEPS
PAYLOAD = ROWS + 16
FLOOR = -(2.0**100)
SCALE = 1.0 / math.sqrt(HD)
LIMIT = 48 * 1024 * 1024
FULL = 63 * 1024 * 1024
BF = jnp.bfloat16
F32 = jnp.float32

VM = pl.BlockSpec(memory_space=pltpu.VMEM)
SM = pl.BlockSpec(memory_space=pltpu.SMEM)
HB = pl.BlockSpec(memory_space=pltpu.HBM)


ANY = pl.BlockSpec(memory_space=pl.ANY)
TARGET, ORIGIN, LENGTH = 0, MIG, 2 * MIG


def call(kernel, outs, specs, flops=0, moved=0, scratch=(), limit=LIMIT, places=None):
    return pl.pallas_call(
        kernel,
        out_shape=outs,
        in_specs=specs,
        out_specs=jax.tree.map(lambda _: VM, outs) if places is None else places,
        scratch_shapes=scratch,
        compiler_params=pltpu.CompilerParams(vmem_limit_bytes=limit),
        cost_estimate=pl.CostEstimate(flops=flops, bytes_accessed=moved, transcendentals=0),
    )


def swapped(step, x):
    return x ^ (step * 3)


def place_of():
    shard = lax.axis_index("tensor")
    return shard // SIDE, shard % SIDE


def pack_kernel(*refs):
    n = BLOCKS
    given, refs = refs[:8], refs[8:]
    plan, outs, refs = refs[0], refs[1 : 3 + n], refs[3 + n :]
    inside, (sent, kept, *blocks), (come, go) = refs[:8], refs[8 : 10 + n], refs[10 + n :]
    shard, group = lax.axis_index("tensor"), lax.axis_index("group")
    first = pl.multiple_of(shard % 2 * FEATURES + shard // 2 * HD, HD)
    given = list(given)
    given[5] = given[5].at[:, :, pl.ds(first, HD)]
    copies = [pltpu.make_async_copy(p, q, come.at[k]) for k, (p, q) in enumerate(zip(given, inside))]
    for copy in copies:
        copy.start()
    sent[...] = jnp.zeros_like(sent)
    for copy in copies[:6]:
        copy.wait()
    names, holders, tokens, residents = (ref[...].astype(F32) for ref in inside[:4])
    asked, fresh, moved, resident = inside[4:]

    def found(where, name, values):
        return jnp.sum(jnp.where(where == name, values, 0.0)).astype(jnp.int32)

    for slot in range(RES):
        kept[slot, :HEADS] = asked[slot]
        kept[slot, HEADS] = fresh[slot]
    for slot in range(MIG):
        name = (group * SLOTS + RES + slot).astype(F32)
        to = lax.div(found(names, name, holders), MIG)
        plan[TARGET + slot] = to
        sent[to, :HEADS] = asked[RES + slot]
        sent[to, HEADS] = fresh[RES + slot]
    writes = [pltpu.make_async_copy(p, q, go.at[k]) for k, (p, q) in enumerate(zip((sent, kept, *blocks), outs))]
    writes[0].start()
    writes[1].start()
    for slot in range(MIG):
        name = (group * MIG + slot).astype(F32)
        plan[ORIGIN + slot] = lax.div(found(holders, name, names), SLOTS)
        plan[LENGTH + slot] = found(holders, name, tokens)
    lane = lax.broadcasted_iota(jnp.int32, (1, HD), 1)
    for slot in range(RES):
        plan[LENGTH + MIG + slot] = found(lane, group * RES + slot, residents)
    for copy in copies[6:]:
        copy.wait()
    y, x = place_of()
    for step in (*range(1, n), 0):
        block = blocks[step]
        half = swapped(step, x) // 2
        heads = [2 * place + half for place in range(PAIRS)]
        for place, pair in enumerate(heads):
            for part in range(2):
                lanes = pl.ds(pl.multiple_of(pair * HD + part * FEATURES, HD), HD)
                columns = slice((part * PAIRS + place) * HD, (part * PAIRS + place + 1) * HD)
                block[:MIG, :, columns] = moved[:, :, lanes]
                block[MIG:, :, columns] = resident[:, :, lanes]
        writes[2 + step].start()
    for write in writes:
        write.wait()


def spread_kernel(plan, arrived, kept, asking):
    for row in range(SLOTS):
        chunk = arrived.at[plan[ORIGIN + row]] if row < MIG else kept.at[row - MIG]
        for peer in range(PEERS):
            asking[peer, row * HEADS : (row + 1) * HEADS] = chunk[:HEADS]
            asking[peer, SLOTS * HEADS + row] = chunk[HEADS]


def scores_of(left, right):
    return lax.dot_general(left, right, (((1,), (1,)), ((), ())), preferred_element_type=F32) * SCALE


def partial_kernel(plan, asking, *rest):
    *blocks, payload, scores, weights, stats = rest
    y, x = place_of()
    column = lax.broadcasted_iota(jnp.int32, (1, WIDE), 1)
    position = (y * SIDE + swapped(column // STRIDE, x)) * STRIDE + column % STRIDE

    def stored(row, place):
        lanes = slice(place * HD, (place + 1) * HD)
        return jnp.concatenate([block[row, :, lanes] for block in blocks], 0)

    for row in range(SLOTS):
        usable = position < plan[LENGTH + row]
        span = slice(row * QROWS, (row + 1) * QROWS)
        for pair in range(PAIRS):
            asked = jnp.concatenate([asking[2 * pair, span, :], asking[2 * pair + 1, span, :]], 0)
            found = jnp.where(usable, scores_of(asked, stored(row, pair)), FLOOR)
            scores[2 * pair, span, :] = found[:QROWS]
            scores[2 * pair + 1, span, :] = found[QROWS:]
    lane = lax.broadcasted_iota(jnp.int32, (ROWS, HD), 1)
    table = jnp.zeros((ROWS, HD), F32)
    for peer in range(PEERS):
        found = scores[peer]
        top = jnp.max(found, axis=1, keepdims=True)
        first = top.astype(BF).astype(F32)
        second = (top - first).astype(BF).astype(F32)
        weight = jnp.exp(found - (first + second))
        total = jnp.sum(weight, axis=1, keepdims=True)
        weights[peer] = weight.astype(BF)
        total_first = total.astype(BF).astype(F32)
        for place, value in enumerate((first, total_first, second, total - total_first)):
            table = jnp.where(lane == peer * 8 + place, value, table)
    stats[:ROWS, :] = table
    stats[ROWS:, :] = jnp.zeros((2 * HD - ROWS, HD), F32)
    low = stats[:HD, :].T
    high = stats[HD:, :].T
    for peer in range(PEERS):
        rows = slice(peer * 8, (peer + 1) * 8)
        payload[peer, ROWS:, :] = jnp.concatenate([low[rows], high[rows]], 0).astype(BF)
    for row in range(SLOTS):
        span = slice(row * QROWS, (row + 1) * QROWS)
        for pair in range(PAIRS):
            weight = jnp.concatenate([weights[2 * pair, span, :], weights[2 * pair + 1, span, :]], 0)
            blended = jnp.dot(weight, stored(row, PAIRS + pair), preferred_element_type=F32).astype(BF)
            payload[2 * pair, span, :] = blended[:QROWS]
            payload[2 * pair + 1, span, :] = blended[QROWS:]


def merge_kernel(plan, gathered, everyone, sent, kept):
    y, x = place_of()
    first = 2 * y
    asked = everyone[first + x % 2, :ROWS, :]
    keys = everyone[first, ROWS:, :]
    values = everyone[first + 1, ROWS:, :]
    row = lax.broadcasted_iota(jnp.int32, (ROWS, ENTRIES), 0)
    lane = lax.broadcasted_iota(jnp.int32, (ROWS, ENTRIES), 1)
    causal = (lane // STEPS == row // QROWS) & (lane % STEPS <= row % STEPS)
    fresh = jnp.where(causal, scores_of(asked, keys), FLOOR)
    fresh_top = jnp.max(fresh, axis=1, keepdims=True)

    tops = gathered[:, ROWS:, :].astype(F32)
    blank = jnp.zeros((HD - PEERS * 8, HD), F32)
    low = jnp.concatenate([tops[:, :8, :].reshape(PEERS * 8, HD), blank], 0).T
    high = jnp.concatenate([tops[:, 8:, :].reshape(PEERS * 8, HD), blank], 0).T[: ROWS - HD]
    pairs = jnp.concatenate([low, high], 0)
    both = pairs + pltpu.roll(pairs, HD - 2, 1)
    lane = lax.broadcasted_iota(jnp.int32, (ROWS, HD), 1)
    is_top = (lane % 8 == 0) & (lane < PEERS * 8)
    tops = jnp.where(is_top, both, FLOOR)
    sums = pltpu.roll(both, HD - 1, 1)
    highest = jnp.maximum(jnp.max(tops, axis=1, keepdims=True), fresh_top)
    factors = jnp.where(is_top, jnp.exp(tops - highest), 0.0)
    fresh_weights = jnp.where(causal, jnp.exp(fresh - highest), 0.0)
    totals = jnp.sum(jnp.where(is_top, factors * sums, 0.0), axis=1, keepdims=True)
    totals += jnp.sum(fresh_weights, axis=1, keepdims=True)
    blended = jnp.dot(fresh_weights.astype(BF), values, preferred_element_type=F32)
    for peer in range(PEERS):
        blended += factors[:, peer * 8 : peer * 8 + 1] * gathered[peer, :ROWS, :].astype(F32)
    result = (blended / totals).astype(BF)

    sent[...] = jnp.zeros_like(sent)
    for slot in range(MIG):
        sent[plan[ORIGIN + slot]] = result[slot * QROWS : (slot + 1) * QROWS]
    for slot in range(RES):
        kept[slot] = result[(MIG + slot) * QROWS : (MIG + slot + 1) * QROWS]


def select_kernel(plan, returned, kept, out):
    for slot in range(RES):
        out[slot] = kept[slot]
    for slot in range(MIG):
        out[RES + slot] = returned[plan[TARGET + slot]]


def body(
    queries,
    new_entries,
    resident_cache,
    prefill_cache,
    resident_kept,
    kept_tokens,
    prefill_slot,
    decode_slot,
):
    shape = jax.ShapeDtypeStruct
    peers = [[y * SIDE + 2 * half + x for y in range(SIDE) for x in range(2)] for half in range(2)]

    def across(array):
        return lax.all_to_all(array, "tensor", 0, 0, axis_index_groups=peers, tiled=True)

    asked = queries.reshape(SLOTS, STEPS, HEADS, HD).transpose(0, 2, 1, 3)
    tile = (SLOTS, STRIDE, 2 * PAIRS * HD)
    held = [
        ((GROUPS, TILES, STEPS, HD), BF),
        ((RES, TILES, STEPS, HD), BF),
        *([(tile, BF)] * BLOCKS),
    ]
    taken = [
        *([((2, HD), jnp.int32)] * 3),
        ((1, HD), jnp.int32),
        ((SLOTS, HEADS, STEPS, HD), BF),
        ((SLOTS, STEPS, HD), BF),
        (prefill_cache.shape, BF),
        (resident_cache.shape, BF),
    ]
    plan, sent, kept, *split = call(
        pack_kernel,
        (shape((2 * MIG + SLOTS,), jnp.int32), *(shape(*one) for one in held)),
        [HB] * 8,
        moved=3 * 2**20,
        scratch=[pltpu.VMEM(*one) for one in taken + held]
        + [pltpu.SemaphoreType.DMA((8,)), pltpu.SemaphoreType.DMA((len(held),))],
        limit=FULL,
        places=(SM, *([ANY] * len(held))),
    )(
        decode_slot.reshape(2, HD),
        prefill_slot.reshape(2, HD),
        kept_tokens.reshape(2, HD),
        resident_kept.reshape(1, HD),
        asked,
        new_entries,
        prefill_cache,
        resident_cache,
    )
    arrived = lax.all_to_all(sent, "group", 0, 0, tiled=True)

    blocks = [split[0]]
    for step in range(1, BLOCKS):
        steps = [(t, t // SIDE * SIDE + swapped(step, t % SIDE)) for t in range(SHARDS)]
        blocks.append(lax.ppermute(split[step], "tensor", steps))

    asking = call(
        spread_kernel, shape((PEERS, SLOTS * TILES, STEPS, HD), BF), [SM, VM, VM]
    )(plan, arrived, kept)
    everyone = across(asking).reshape(PEERS, ROWS + ENTRIES, HD)

    payload = call(
        partial_kernel,
        shape((PEERS, PAYLOAD, HD), BF),
        [SM] + [VM] * (1 + BLOCKS),
        flops=10**8,
        moved=3 * 2**20,
        scratch=[
            pltpu.VMEM((PEERS, ROWS, WIDE), F32),
            pltpu.VMEM((PEERS, ROWS, WIDE), BF),
            pltpu.VMEM((2 * HD, HD), F32),
        ],
    )(plan, everyone, *blocks)
    gathered = across(payload)

    finished, here = call(
        merge_kernel,
        (shape((GROUPS, QROWS, HD), BF), shape((RES, QROWS, HD), BF)),
        [SM, VM, VM],
    )(plan, gathered, everyone)
    returned = lax.all_to_all(finished, "group", 0, 0, tiled=True)

    result = call(select_kernel, shape((SLOTS, QROWS, HD), BF), [SM, VM, VM])(plan, returned, here)
    result = result.reshape(SLOTS, HEADS, STEPS, HD).transpose(0, 2, 1, 3)
    return result.reshape(SLOTS, STEPS, HEADS * HD)


def solution(mesh):
    in_specs = (
        P("group", None, "tensor"),
        P("group", None, None),
        P("group", "tensor", None),
        P("group", "tensor", None),
        P(),
        P(),
        P(),
        P(),
    )
    out_specs = P("group", None, "tensor")
    return jax.shard_map(body, mesh=mesh, in_specs=in_specs, out_specs=out_specs, check_vma=False)
```

```python
import math

import jax
import jax.numpy as jnp
from jax import lax
from jax.experimental import pallas as pl
from jax.experimental.pallas import tpu as pltpu
from jax.sharding import PartitionSpec as P

H = 64
KVH = 8
HD = 128
STEPS = 4
MIG = 8
RES = 4
SLOTS = MIG + RES
GROUPS = 32
SHARDS = 16
SIDE = 4
STRIDE = 32
HEADS = H // SHARDS
PAIRS = KVH // SIDE
QROWS = HEADS * STEPS
ROWS = SLOTS * QROWS
FEATURES = KVH * HD
TILES = HEADS + 1
ENTRIES = SLOTS * STEPS
PAYLOAD = ROWS + 16
FLOOR = -(2.0**100)
SCALE = 1.0 / math.sqrt(HD)
LIMIT = 48 * 1024 * 1024
FULL = 62 * 1024 * 1024
BF = jnp.bfloat16
F32 = jnp.float32

VM = pl.BlockSpec(memory_space=pltpu.VMEM)
SM = pl.BlockSpec(memory_space=pltpu.SMEM)
HB = pl.BlockSpec(memory_space=pltpu.HBM)


ANY = pl.BlockSpec(memory_space=pl.ANY)
TARGET, ORIGIN, LENGTH = 0, MIG, 2 * MIG


def call(kernel, outs, specs, flops=0, moved=0, scratch=(), limit=LIMIT, places=None):
    return pl.pallas_call(
        kernel,
        out_shape=outs,
        in_specs=specs,
        out_specs=jax.tree.map(lambda _: VM, outs) if places is None else places,
        scratch_shapes=scratch,
        compiler_params=pltpu.CompilerParams(vmem_limit_bytes=limit),
        cost_estimate=pl.CostEstimate(flops=flops, bytes_accessed=moved, transcendentals=0),
    )


def swapped(step, y, x):
    return y ^ (step % 2), x ^ (step // 2 * 3)


def class_of(y, x):
    return jnp.minimum(y, 3 - y), x // 2


def place_of():
    shard = lax.axis_index("tensor")
    return shard // SIDE, shard % SIDE


def pack_kernel(*refs):
    given, plan, outs, refs = refs[:6], refs[6], refs[7:9], refs[9:]
    inside, (sent, kept), (come, go) = refs[:6], refs[6:8], refs[8:]
    shard, group = lax.axis_index("tensor"), lax.axis_index("group")
    first = pl.multiple_of(shard % 2 * FEATURES + shard // 2 * HD, HD)
    given = list(given)
    given[5] = given[5].at[:, :, pl.ds(first, HD)]
    copies = [pltpu.make_async_copy(p, q, come.at[k]) for k, (p, q) in enumerate(zip(given, inside))]
    for copy in copies:
        copy.start()
    sent[...] = jnp.zeros_like(sent)
    for copy in copies:
        copy.wait()
    names, holders, tokens, residents = (ref[...].astype(F32) for ref in inside[:4])
    asked, fresh = inside[4:]

    def found(where, name, values):
        return jnp.sum(jnp.where(where == name, values, 0.0)).astype(jnp.int32)

    for slot in range(RES):
        kept[slot, :HEADS] = asked[slot]
        kept[slot, HEADS] = fresh[slot]
    for slot in range(MIG):
        name = (group * SLOTS + RES + slot).astype(F32)
        to = lax.div(found(names, name, holders), MIG)
        plan[TARGET + slot] = to
        sent[to, :HEADS] = asked[RES + slot]
        sent[to, HEADS] = fresh[RES + slot]
    writes = [pltpu.make_async_copy(p, q, go.at[k]) for k, (p, q) in enumerate(zip((sent, kept), outs))]
    writes[0].start()
    writes[1].start()
    for slot in range(MIG):
        name = (group * MIG + slot).astype(F32)
        plan[ORIGIN + slot] = lax.div(found(holders, name, names), SLOTS)
        plan[LENGTH + slot] = found(holders, name, tokens)
    lane = lax.broadcasted_iota(jnp.int32, (1, HD), 1)
    for slot in range(RES):
        plan[LENGTH + MIG + slot] = found(lane, group * RES + slot, residents)
    for write in writes:
        write.wait()


def split_kernel(moved, resident, *outs):
    y, x = place_of()
    for step, out in enumerate(outs):
        low, half = class_of(*swapped(step, y, x))
        for place, pair in enumerate((2 * low + half, 6 - 2 * low + half)):
            for part in range(2):
                lanes = pl.ds(pl.multiple_of(pair * HD + part * FEATURES, HD), HD)
                columns = slice((part * PAIRS + place) * HD, (part * PAIRS + place + 1) * HD)
                out[:MIG, :, columns] = moved[:, :, lanes]
                out[MIG:, :, columns] = resident[:, :, lanes]


def spread_kernel(plan, arrived, kept, asking):
    for row in range(SLOTS):
        chunk = arrived.at[plan[ORIGIN + row]] if row < MIG else kept.at[row - MIG]
        for peer in range(SIDE):
            asking[peer, row * HEADS : (row + 1) * HEADS] = chunk[:HEADS]
            asking[peer, SLOTS * HEADS + row] = chunk[HEADS]


def scores_of(left, right):
    return lax.dot_general(left, right, (((1,), (1,)), ((), ())), preferred_element_type=F32) * SCALE


def partial_kernel(plan, asking, *rest):
    *blocks, payload, scores, weights, stats = rest
    column = lax.broadcasted_iota(jnp.int32, (1, HD), 1)
    block = column // STRIDE
    y, x = swapped(jnp.where(block == 0, 0, (block + 1) % 3 + 1), *place_of())
    position = (y * SIDE + x) * STRIDE + column % STRIDE

    def stored(row, place):
        lanes = slice(place * HD, (place + 1) * HD)
        return jnp.concatenate([block[row, :, lanes] for block in blocks], 0)

    for row in range(SLOTS):
        usable = position < plan[LENGTH + row]
        span = slice(row * QROWS, (row + 1) * QROWS)
        for pair in range(PAIRS):
            asked = jnp.concatenate([asking[2 * pair, span, :], asking[2 * pair + 1, span, :]], 0)
            found = jnp.where(usable, scores_of(asked, stored(row, pair)), FLOOR)
            scores[2 * pair, span, :] = found[:QROWS]
            scores[2 * pair + 1, span, :] = found[QROWS:]
    lane = lax.broadcasted_iota(jnp.int32, (ROWS, HD), 1)
    table = jnp.zeros((ROWS, HD), F32)
    for peer in range(SIDE):
        found = scores[peer]
        top = jnp.max(found, axis=1, keepdims=True)
        first = top.astype(BF).astype(F32)
        second = (top - first).astype(BF).astype(F32)
        weight = jnp.exp(found - (first + second))
        total = jnp.sum(weight, axis=1, keepdims=True)
        weights[peer] = weight.astype(BF)
        total_first = total.astype(BF).astype(F32)
        for place, value in enumerate((first, total_first, second, total - total_first)):
            table = jnp.where(lane == peer * 8 + place, value, table)
    stats[:ROWS, :] = table
    stats[ROWS:, :] = jnp.zeros((2 * HD - ROWS, HD), F32)
    low = stats[:HD, :].T
    high = stats[HD:, :].T
    for peer in range(SIDE):
        rows = slice(peer * 8, (peer + 1) * 8)
        payload[peer, ROWS:, :] = jnp.concatenate([low[rows], high[rows]], 0).astype(BF)
    for row in range(SLOTS):
        span = slice(row * QROWS, (row + 1) * QROWS)
        for pair in range(PAIRS):
            weight = jnp.concatenate([weights[2 * pair, span, :], weights[2 * pair + 1, span, :]], 0)
            blended = jnp.dot(weight, stored(row, PAIRS + pair), preferred_element_type=F32).astype(BF)
            payload[2 * pair, span, :] = blended[:QROWS]
            payload[2 * pair + 1, span, :] = blended[QROWS:]


def merge_kernel(plan, gathered, everyone, sent, kept):
    y, x = place_of()
    first = jnp.where(y > 1, 2, 0)
    asked = everyone[first + x % 2, :ROWS, :]
    keys = everyone[first, ROWS:, :]
    values = everyone[first + 1, ROWS:, :]
    row = lax.broadcasted_iota(jnp.int32, (ROWS, ENTRIES), 0)
    lane = lax.broadcasted_iota(jnp.int32, (ROWS, ENTRIES), 1)
    causal = (lane // STEPS == row // QROWS) & (lane % STEPS <= row % STEPS)
    fresh = jnp.where(causal, scores_of(asked, keys), FLOOR)
    fresh_top = jnp.max(fresh, axis=1, keepdims=True)

    tops = gathered[:, ROWS:, :].astype(F32)
    blank = jnp.zeros((HD - SIDE * 8, HD), F32)
    low = jnp.concatenate([tops[:, :8, :].reshape(SIDE * 8, HD), blank], 0).T
    high = jnp.concatenate([tops[:, 8:, :].reshape(SIDE * 8, HD), blank], 0).T[: ROWS - HD]
    pairs = jnp.concatenate([low, high], 0)
    both = pairs + pltpu.roll(pairs, HD - 2, 1)
    lane = lax.broadcasted_iota(jnp.int32, (ROWS, HD), 1)
    is_top = (lane % 8 == 0) & (lane < SIDE * 8)
    tops = jnp.where(is_top, both, FLOOR)
    sums = pltpu.roll(both, HD - 1, 1)
    highest = jnp.maximum(jnp.max(tops, axis=1, keepdims=True), fresh_top)
    factors = jnp.where(is_top, jnp.exp(tops - highest), 0.0)
    fresh_weights = jnp.where(causal, jnp.exp(fresh - highest), 0.0)
    totals = jnp.sum(jnp.where(is_top, factors * sums, 0.0), axis=1, keepdims=True)
    totals += jnp.sum(fresh_weights, axis=1, keepdims=True)
    blended = jnp.dot(fresh_weights.astype(BF), values, preferred_element_type=F32)
    for peer in range(SIDE):
        blended += factors[:, peer * 8 : peer * 8 + 1] * gathered[peer, :ROWS, :].astype(F32)
    result = (blended / totals).astype(BF)

    sent[...] = jnp.zeros_like(sent)
    for slot in range(MIG):
        sent[plan[ORIGIN + slot]] = result[slot * QROWS : (slot + 1) * QROWS]
    for slot in range(RES):
        kept[slot] = result[(MIG + slot) * QROWS : (MIG + slot + 1) * QROWS]


def select_kernel(plan, returned, kept, out):
    for slot in range(RES):
        out[slot] = kept[slot]
    for slot in range(MIG):
        out[RES + slot] = returned[plan[TARGET + slot]]


def body(
    queries,
    new_entries,
    resident_cache,
    prefill_cache,
    resident_kept,
    kept_tokens,
    prefill_slot,
    decode_slot,
):
    shape = jax.ShapeDtypeStruct
    whole = [(y, x) for y in range(SIDE) for x in range(SIDE)]
    peers = [[y * SIDE + x for y in (low, 3 - low) for x in (2 * half, 2 * half + 1)] for low in range(2) for half in range(2)]

    def across(array):
        return lax.all_to_all(array, "tensor", 0, 0, axis_index_groups=peers, tiled=True)

    asked = queries.reshape(SLOTS, STEPS, HEADS, HD).transpose(0, 2, 1, 3)
    held = [
        ((GROUPS, TILES, STEPS, HD), BF),
        ((RES, TILES, STEPS, HD), BF),
    ]
    taken = [
        *([((2, HD), jnp.int32)] * 3),
        ((1, HD), jnp.int32),
        ((SLOTS, HEADS, STEPS, HD), BF),
        ((SLOTS, STEPS, HD), BF),
    ]
    plan, sent, kept = call(
        pack_kernel,
        (shape((2 * MIG + SLOTS,), jnp.int32), *(shape(*one) for one in held)),
        [HB] * 6,
        scratch=[pltpu.VMEM(*one) for one in taken + held]
        + [pltpu.SemaphoreType.DMA((6,)), pltpu.SemaphoreType.DMA((len(held),))],
        limit=FULL,
        places=(SM, *([ANY] * len(held))),
    )(
        decode_slot.reshape(2, HD),
        prefill_slot.reshape(2, HD),
        kept_tokens.reshape(2, HD),
        resident_kept.reshape(1, HD),
        asked,
        new_entries,
    )
    arrived = lax.all_to_all(sent, "group", 0, 0, tiled=True)

    split = call(
        split_kernel,
        (shape((SLOTS, STRIDE, 2 * PAIRS * HD), BF),) * SIDE,
        [VM, VM],
        moved=3 * 2**20,
    )(prefill_cache, resident_cache)
    blocks = [split[0]]
    for step in (3, 1, 2):
        steps = []
        for y, x in whole:
            other, side = swapped(step, y, x)
            steps.append((y * SIDE + x, other * SIDE + side))
        blocks.append(lax.ppermute(split[step], "tensor", steps))

    asking = call(
        spread_kernel, shape((SIDE, SLOTS * TILES, STEPS, HD), BF), [SM, VM, VM]
    )(plan, arrived, kept)
    everyone = across(asking).reshape(SIDE, ROWS + ENTRIES, HD)

    payload = call(
        partial_kernel,
        shape((SIDE, PAYLOAD, HD), BF),
        [SM] + [VM] * (1 + SIDE),
        flops=10**8,
        moved=3 * 2**20,
        scratch=[
            pltpu.VMEM((SIDE, ROWS, HD), F32),
            pltpu.VMEM((SIDE, ROWS, HD), BF),
            pltpu.VMEM((2 * HD, HD), F32),
        ],
    )(plan, everyone, *blocks)
    gathered = across(payload)

    finished, here = call(
        merge_kernel,
        (shape((GROUPS, QROWS, HD), BF), shape((RES, QROWS, HD), BF)),
        [SM, VM, VM],
    )(plan, gathered, everyone)
    returned = lax.all_to_all(finished, "group", 0, 0, tiled=True)

    result = call(select_kernel, shape((SLOTS, QROWS, HD), BF), [SM, VM, VM])(plan, returned, here)
    result = result.reshape(SLOTS, HEADS, STEPS, HD).transpose(0, 2, 1, 3)
    return result.reshape(SLOTS, STEPS, HEADS * HD)


def solution(mesh):
    in_specs = (
        P("group", None, "tensor"),
        P("group", None, None),
        P("group", "tensor", None),
        P("group", "tensor", None),
        P(),
        P(),
        P(),
        P(),
    )
    out_specs = P("group", None, "tensor")
    return jax.shard_map(body, mesh=mesh, in_specs=in_specs, out_specs=out_specs, check_vma=False)
```

```python
import math

import jax
import jax.numpy as jnp
from jax import lax
from jax.experimental import pallas as pl
from jax.experimental.pallas import tpu as pltpu
from jax.sharding import PartitionSpec as P

H = 64
KVH = 8
HD = 128
STEPS = 4
MIG = 8
RES = 4
SLOTS = MIG + RES
GROUPS = 32
TURN = 16
SHARDS = 16
SIDE = 4
STRIDE = 32
HEADS = H // SHARDS
PAIRS = KVH // SIDE
QROWS = HEADS * STEPS
ROWS = SLOTS * QROWS
FEATURES = KVH * HD
TILES = HEADS + 1
ENTRIES = SLOTS * STEPS
PAYLOAD = ROWS + 16
FLOOR = -(2.0**100)
SCALE = 1.0 / math.sqrt(HD)
LIMIT = 48 * 1024 * 1024
FULL = 62 * 1024 * 1024
BF = jnp.bfloat16
F32 = jnp.float32

VM = pl.BlockSpec(memory_space=pltpu.VMEM)
SM = pl.BlockSpec(memory_space=pltpu.SMEM)
HB = pl.BlockSpec(memory_space=pltpu.HBM)


ANY = pl.BlockSpec(memory_space=pl.ANY)
TARGET, ORIGIN, LENGTH = 0, MIG, 2 * MIG


def call(kernel, outs, specs, flops=0, moved=0, scratch=(), limit=LIMIT, places=None):
    return pl.pallas_call(
        kernel,
        out_shape=outs,
        in_specs=specs,
        out_specs=jax.tree.map(lambda _: VM, outs) if places is None else places,
        scratch_shapes=scratch,
        compiler_params=pltpu.CompilerParams(vmem_limit_bytes=limit),
        cost_estimate=pl.CostEstimate(flops=flops, bytes_accessed=moved, transcendentals=0),
    )


def swapped(step, y, x):
    return y ^ (step % 2), x ^ (step // 2 * 3)


def class_of(y, x):
    return jnp.minimum(y, 3 - y), x // 2


def place_of():
    shard = lax.axis_index("tensor")
    return shard // SIDE, shard % SIDE


def pack_kernel(*refs):
    given, plan, outs, refs = refs[:6], refs[6], refs[7:9], refs[9:]
    inside, (sent, kept), (come, go) = refs[:6], refs[6:8], refs[8:]
    shard, group = lax.axis_index("tensor"), lax.axis_index("group")
    first = pl.multiple_of(shard % 2 * FEATURES + shard // 2 * HD, HD)
    given = list(given)
    given[5] = given[5].at[:, :, pl.ds(first, HD)]
    copies = [pltpu.make_async_copy(p, q, come.at[k]) for k, (p, q) in enumerate(zip(given, inside))]
    for copy in copies:
        copy.start()
    sent[...] = jnp.zeros_like(sent)
    for copy in copies:
        copy.wait()
    names, holders, tokens, residents = (ref[...].astype(F32) for ref in inside[:4])
    asked, fresh = inside[4:]

    def found(where, name, values):
        return jnp.sum(jnp.where(where == name, values, 0.0)).astype(jnp.int32)

    for slot in range(RES):
        kept[slot, :HEADS] = asked[slot]
        kept[slot, HEADS] = fresh[slot]
    for slot in range(MIG):
        name = (group * SLOTS + RES + slot).astype(F32)
        to = lax.div(found(names, name, holders), MIG)
        plan[TARGET + slot] = to
        sent[to ^ TURN, :HEADS] = asked[RES + slot]
        sent[to ^ TURN, HEADS] = fresh[RES + slot]
    writes = [pltpu.make_async_copy(p, q, go.at[k]) for k, (p, q) in enumerate(zip((sent, kept), outs))]
    writes[0].start()
    writes[1].start()
    for slot in range(MIG):
        name = (group * MIG + slot).astype(F32)
        plan[ORIGIN + slot] = lax.div(found(holders, name, names), SLOTS)
        plan[LENGTH + slot] = found(holders, name, tokens)
    lane = lax.broadcasted_iota(jnp.int32, (1, HD), 1)
    for slot in range(RES):
        plan[LENGTH + MIG + slot] = found(lane, group * RES + slot, residents)
    for write in writes:
        write.wait()


def split_kernel(moved, resident, *outs):
    y, x = place_of()
    for step, out in enumerate(outs):
        low, half = class_of(*swapped(step, y, x))
        for place, pair in enumerate((2 * low + half, 6 - 2 * low + half)):
            for part in range(2):
                lanes = pl.ds(pl.multiple_of(pair * HD + part * FEATURES, HD), HD)
                columns = slice((part * PAIRS + place) * HD, (part * PAIRS + place + 1) * HD)
                out[:MIG, :, columns] = moved[:, :, lanes]
                out[MIG:, :, columns] = resident[:, :, lanes]


def spread_kernel(plan, arrived, kept, asking):
    for row in range(SLOTS):
        chunk = arrived.at[plan[ORIGIN + row] ^ TURN] if row < MIG else kept.at[row - MIG]
        for peer in range(SIDE):
            asking[peer, row * HEADS : (row + 1) * HEADS] = chunk[:HEADS]
            asking[peer, SLOTS * HEADS + row] = chunk[HEADS]


def scores_of(left, right):
    return lax.dot_general(left, right, (((1,), (1,)), ((), ())), preferred_element_type=F32) * SCALE


def partial_kernel(plan, asking, *rest):
    *blocks, payload, scores, weights, stats = rest
    column = lax.broadcasted_iota(jnp.int32, (1, HD), 1)
    block = column // STRIDE
    y, x = swapped(jnp.where(block == 0, 0, (block + 1) % 3 + 1), *place_of())
    position = (y * SIDE + x) * STRIDE + column % STRIDE

    def stored(row, place):
        lanes = slice(place * HD, (place + 1) * HD)
        return jnp.concatenate([block[row, :, lanes] for block in blocks], 0)

    for row in range(SLOTS):
        usable = position < plan[LENGTH + row]
        span = slice(row * QROWS, (row + 1) * QROWS)
        for pair in range(PAIRS):
            asked = jnp.concatenate([asking[2 * pair, span, :], asking[2 * pair + 1, span, :]], 0)
            found = jnp.where(usable, scores_of(asked, stored(row, pair)), FLOOR)
            scores[2 * pair, span, :] = found[:QROWS]
            scores[2 * pair + 1, span, :] = found[QROWS:]
    lane = lax.broadcasted_iota(jnp.int32, (ROWS, HD), 1)
    table = jnp.zeros((ROWS, HD), F32)
    for peer in range(SIDE):
        found = scores[peer]
        top = jnp.max(found, axis=1, keepdims=True)
        first = top.astype(BF).astype(F32)
        second = (top - first).astype(BF).astype(F32)
        weight = jnp.exp(found - (first + second))
        total = jnp.sum(weight, axis=1, keepdims=True)
        weights[peer] = weight.astype(BF)
        total_first = total.astype(BF).astype(F32)
        for place, value in enumerate((first, total_first, second, total - total_first)):
            table = jnp.where(lane == peer * 8 + place, value, table)
    stats[:ROWS, :] = table
    stats[ROWS:, :] = jnp.zeros((2 * HD - ROWS, HD), F32)
    low = stats[:HD, :].T
    high = stats[HD:, :].T
    for peer in range(SIDE):
        rows = slice(peer * 8, (peer + 1) * 8)
        payload[peer, ROWS:, :] = jnp.concatenate([low[rows], high[rows]], 0).astype(BF)
    for row in range(SLOTS):
        span = slice(row * QROWS, (row + 1) * QROWS)
        for pair in range(PAIRS):
            weight = jnp.concatenate([weights[2 * pair, span, :], weights[2 * pair + 1, span, :]], 0)
            blended = jnp.dot(weight, stored(row, PAIRS + pair), preferred_element_type=F32).astype(BF)
            payload[2 * pair, span, :] = blended[:QROWS]
            payload[2 * pair + 1, span, :] = blended[QROWS:]


def merge_kernel(plan, gathered, everyone, sent, kept):
    y, x = place_of()
    first = jnp.where(y > 1, 2, 0)
    asked = everyone[first + x % 2, :ROWS, :]
    keys = everyone[first, ROWS:, :]
    values = everyone[first + 1, ROWS:, :]
    row = lax.broadcasted_iota(jnp.int32, (ROWS, ENTRIES), 0)
    lane = lax.broadcasted_iota(jnp.int32, (ROWS, ENTRIES), 1)
    causal = (lane // STEPS == row // QROWS) & (lane % STEPS <= row % STEPS)
    fresh = jnp.where(causal, scores_of(asked, keys), FLOOR)
    fresh_top = jnp.max(fresh, axis=1, keepdims=True)

    tops = gathered[:, ROWS:, :].astype(F32)
    blank = jnp.zeros((HD - SIDE * 8, HD), F32)
    low = jnp.concatenate([tops[:, :8, :].reshape(SIDE * 8, HD), blank], 0).T
    high = jnp.concatenate([tops[:, 8:, :].reshape(SIDE * 8, HD), blank], 0).T[: ROWS - HD]
    pairs = jnp.concatenate([low, high], 0)
    both = pairs + pltpu.roll(pairs, HD - 2, 1)
    lane = lax.broadcasted_iota(jnp.int32, (ROWS, HD), 1)
    is_top = (lane % 8 == 0) & (lane < SIDE * 8)
    tops = jnp.where(is_top, both, FLOOR)
    sums = pltpu.roll(both, HD - 1, 1)
    highest = jnp.maximum(jnp.max(tops, axis=1, keepdims=True), fresh_top)
    factors = jnp.where(is_top, jnp.exp(tops - highest), 0.0)
    fresh_weights = jnp.where(causal, jnp.exp(fresh - highest), 0.0)
    totals = jnp.sum(jnp.where(is_top, factors * sums, 0.0), axis=1, keepdims=True)
    totals += jnp.sum(fresh_weights, axis=1, keepdims=True)
    blended = jnp.dot(fresh_weights.astype(BF), values, preferred_element_type=F32)
    for peer in range(SIDE):
        blended += factors[:, peer * 8 : peer * 8 + 1] * gathered[peer, :ROWS, :].astype(F32)
    result = (blended / totals).astype(BF)

    sent[...] = jnp.zeros_like(sent)
    for slot in range(MIG):
        sent[plan[ORIGIN + slot] ^ TURN] = result[slot * QROWS : (slot + 1) * QROWS]
    for slot in range(RES):
        kept[slot] = result[(MIG + slot) * QROWS : (MIG + slot + 1) * QROWS]


def select_kernel(plan, returned, kept, out):
    for slot in range(RES):
        out[slot] = kept[slot]
    for slot in range(MIG):
        out[RES + slot] = returned[plan[TARGET + slot] ^ TURN]


def body(
    queries,
    new_entries,
    resident_cache,
    prefill_cache,
    resident_kept,
    kept_tokens,
    prefill_slot,
    decode_slot,
):
    shape = jax.ShapeDtypeStruct
    whole = [(y, x) for y in range(SIDE) for x in range(SIDE)]
    peers = [[y * SIDE + x for y in (low, 3 - low) for x in (2 * half, 2 * half + 1)] for low in range(2) for half in range(2)]

    turned = [[group ^ TURN for group in range(GROUPS)]]

    def around(array):
        return lax.all_to_all(array, "group", 0, 0, axis_index_groups=turned, tiled=True)

    def across(array):
        return lax.all_to_all(array, "tensor", 0, 0, axis_index_groups=peers, tiled=True)

    asked = queries.reshape(SLOTS, STEPS, HEADS, HD).transpose(0, 2, 1, 3)
    held = [
        ((GROUPS, TILES, STEPS, HD), BF),
        ((RES, TILES, STEPS, HD), BF),
    ]
    taken = [
        *([((2, HD), jnp.int32)] * 3),
        ((1, HD), jnp.int32),
        ((SLOTS, HEADS, STEPS, HD), BF),
        ((SLOTS, STEPS, HD), BF),
    ]
    plan, sent, kept = call(
        pack_kernel,
        (shape((2 * MIG + SLOTS,), jnp.int32), *(shape(*one) for one in held)),
        [HB] * 6,
        scratch=[pltpu.VMEM(*one) for one in taken + held]
        + [pltpu.SemaphoreType.DMA((6,)), pltpu.SemaphoreType.DMA((len(held),))],
        limit=FULL,
        places=(SM, *([ANY] * len(held))),
    )(
        decode_slot.reshape(2, HD),
        prefill_slot.reshape(2, HD),
        kept_tokens.reshape(2, HD),
        resident_kept.reshape(1, HD),
        asked,
        new_entries,
    )
    arrived = around(sent)

    split = call(
        split_kernel,
        (shape((SLOTS, STRIDE, 2 * PAIRS * HD), BF),) * SIDE,
        [VM, VM],
        moved=3 * 2**20,
    )(prefill_cache, resident_cache)
    blocks = [split[0]]
    for step in (3, 1, 2):
        steps = []
        for y, x in whole:
            other, side = swapped(step, y, x)
            steps.append((y * SIDE + x, other * SIDE + side))
        blocks.append(lax.ppermute(split[step], "tensor", steps))

    asking = call(
        spread_kernel, shape((SIDE, SLOTS * TILES, STEPS, HD), BF), [SM, VM, VM]
    )(plan, arrived, kept)
    everyone = across(asking).reshape(SIDE, ROWS + ENTRIES, HD)

    payload = call(
        partial_kernel,
        shape((SIDE, PAYLOAD, HD), BF),
        [SM] + [VM] * (1 + SIDE),
        flops=10**8,
        moved=3 * 2**20,
        scratch=[
            pltpu.VMEM((SIDE, ROWS, HD), F32),
            pltpu.VMEM((SIDE, ROWS, HD), BF),
            pltpu.VMEM((2 * HD, HD), F32),
        ],
    )(plan, everyone, *blocks)
    gathered = across(payload)

    finished, here = call(
        merge_kernel,
        (shape((GROUPS, QROWS, HD), BF), shape((RES, QROWS, HD), BF)),
        [SM, VM, VM],
    )(plan, gathered, everyone)
    returned = around(finished)

    result = call(select_kernel, shape((SLOTS, QROWS, HD), BF), [SM, VM, VM])(plan, returned, here)
    result = result.reshape(SLOTS, HEADS, STEPS, HD).transpose(0, 2, 1, 3)
    return result.reshape(SLOTS, STEPS, HEADS * HD)


def solution(mesh):
    in_specs = (
        P("group", None, "tensor"),
        P("group", None, None),
        P("group", "tensor", None),
        P("group", "tensor", None),
        P(),
        P(),
        P(),
        P(),
    )
    out_specs = P("group", None, "tensor")
    return jax.shard_map(body, mesh=mesh, in_specs=in_specs, out_specs=out_specs, check_vma=False)
```

```python
import math

import jax
import jax.numpy as jnp
from jax import lax
from jax.experimental import pallas as pl
from jax.experimental.pallas import tpu as pltpu
from jax.sharding import PartitionSpec as P

H = 64
KVH = 8
HD = 128
STEPS = 4
MIG = 8
RES = 4
SLOTS = MIG + RES
GROUPS = 32
TURN = 16
SHARDS = 16
SIDE = 4
STRIDE = 32
HEADS = H // SHARDS
PAIRS = KVH // SIDE
QROWS = HEADS * STEPS
ROWS = SLOTS * QROWS
FEATURES = KVH * HD
TILES = HEADS + 1
ENTRIES = SLOTS * STEPS
PAYLOAD = ROWS + 16
FLOOR = -(2.0**100)
SCALE = 1.0 / math.sqrt(HD)
LIMIT = 48 * 1024 * 1024
FULL = 62 * 1024 * 1024
BF = jnp.bfloat16
F32 = jnp.float32

VM = pl.BlockSpec(memory_space=pltpu.VMEM)
SM = pl.BlockSpec(memory_space=pltpu.SMEM)
HB = pl.BlockSpec(memory_space=pltpu.HBM)


ANY = pl.BlockSpec(memory_space=pl.ANY)
TARGET, ORIGIN, LENGTH = 0, MIG, 2 * MIG


def call(kernel, outs, specs, flops=0, moved=0, scratch=(), limit=LIMIT, places=None):
    return pl.pallas_call(
        kernel,
        out_shape=outs,
        in_specs=specs,
        out_specs=jax.tree.map(lambda _: VM, outs) if places is None else places,
        scratch_shapes=scratch,
        compiler_params=pltpu.CompilerParams(vmem_limit_bytes=limit),
        cost_estimate=pl.CostEstimate(flops=flops, bytes_accessed=moved, transcendentals=0),
    )


def swapped(step, y, x):
    return y ^ (step % 2), x ^ (step // 2 * 3)


def class_of(y, x):
    return jnp.minimum(y, 3 - y), x // 2


def place_of():
    shard = lax.axis_index("tensor")
    return shard // SIDE, shard % SIDE


def pack_kernel(*refs):
    given, plan, outs, refs = refs[:6], refs[6], refs[7:9], refs[9:]
    inside, (sent, kept), (come, go) = refs[:6], refs[6:8], refs[8:]
    shard, group = lax.axis_index("tensor"), lax.axis_index("group")
    first = pl.multiple_of(shard % 2 * FEATURES + shard // 2 * HD, HD)
    given = list(given)
    given[5] = given[5].at[:, :, pl.ds(first, HD)]
    copies = [pltpu.make_async_copy(p, q, come.at[k]) for k, (p, q) in enumerate(zip(given, inside))]
    for copy in copies:
        copy.start()
    sent[...] = jnp.zeros_like(sent)
    for copy in copies:
        copy.wait()
    names, holders, tokens, residents = (ref[...].astype(F32) for ref in inside[:4])
    asked, fresh = inside[4:]

    def found(where, name, values):
        return jnp.sum(jnp.where(where == name, values, 0.0)).astype(jnp.int32)

    for slot in range(RES):
        kept[slot, :HEADS] = asked[slot]
        kept[slot, HEADS] = fresh[slot]
    for slot in range(MIG):
        name = (group * SLOTS + RES + slot).astype(F32)
        to = lax.div(found(names, name, holders), MIG)
        plan[TARGET + slot] = to
        sent[to ^ TURN, :HEADS] = asked[RES + slot]
        sent[to ^ TURN, HEADS] = fresh[RES + slot]
    writes = [pltpu.make_async_copy(p, q, go.at[k]) for k, (p, q) in enumerate(zip((sent, kept), outs))]
    writes[0].start()
    writes[1].start()
    for slot in range(MIG):
        name = (group * MIG + slot).astype(F32)
        plan[ORIGIN + slot] = lax.div(found(holders, name, names), SLOTS)
        plan[LENGTH + slot] = found(holders, name, tokens)
    lane = lax.broadcasted_iota(jnp.int32, (1, HD), 1)
    for slot in range(RES):
        plan[LENGTH + MIG + slot] = found(lane, group * RES + slot, residents)
    for write in writes:
        write.wait()


def split_kernel(moved, resident, *outs):
    y, x = place_of()
    for step, out in enumerate(outs):
        low, half = class_of(*swapped(step, y, x))
        for place, pair in enumerate((2 * low + half, 6 - 2 * low + half)):
            for part in range(2):
                lanes = pl.ds(pl.multiple_of(pair * HD + part * FEATURES, HD), HD)
                columns = slice((part * PAIRS + place) * HD, (part * PAIRS + place + 1) * HD)
                out[:MIG, :, columns] = moved[:, :, lanes]
                out[MIG:, :, columns] = resident[:, :, lanes]


def spread_kernel(plan, arrived, kept, asking):
    for row in range(SLOTS):
        chunk = arrived.at[plan[ORIGIN + row] ^ TURN] if row < MIG else kept.at[row - MIG]
        for peer in range(SIDE):
            asking[peer, row * HEADS : (row + 1) * HEADS] = chunk[:HEADS]
            asking[peer, SLOTS * HEADS + row] = chunk[HEADS]


def scores_of(left, right):
    return lax.dot_general(left, right, (((1,), (1,)), ((), ())), preferred_element_type=F32) * SCALE


def partial_kernel(plan, asking, *rest):
    *blocks, payload, scores, weights, stats = rest
    column = lax.broadcasted_iota(jnp.int32, (1, HD), 1)
    block = column // STRIDE
    y, x = swapped(jnp.where(block == 0, 0, (block + 1) % 3 + 1), *place_of())
    position = (y * SIDE + x) * STRIDE + column % STRIDE

    def stored(row, place):
        lanes = slice(place * HD, (place + 1) * HD)
        return jnp.concatenate([block[row, :, lanes] for block in blocks], 0)

    for row in range(SLOTS):
        usable = position < plan[LENGTH + row]
        span = slice(row * QROWS, (row + 1) * QROWS)
        for pair in range(PAIRS):
            asked = jnp.concatenate([asking[2 * pair, span, :], asking[2 * pair + 1, span, :]], 0)
            found = jnp.where(usable, scores_of(asked, stored(row, pair)), FLOOR)
            scores[2 * pair, span, :] = found[:QROWS]
            scores[2 * pair + 1, span, :] = found[QROWS:]
    lane = lax.broadcasted_iota(jnp.int32, (ROWS, HD), 1)
    table = jnp.zeros((ROWS, HD), F32)
    for peer in range(SIDE):
        found = scores[peer]
        top = jnp.max(found, axis=1, keepdims=True)
        first = top.astype(BF).astype(F32)
        second = (top - first).astype(BF).astype(F32)
        weight = jnp.exp(found - (first + second))
        total = jnp.sum(weight, axis=1, keepdims=True)
        weights[peer] = weight.astype(BF)
        total_first = total.astype(BF).astype(F32)
        for place, value in enumerate((first, total_first, second, total - total_first)):
            table = jnp.where(lane == peer * 8 + place, value, table)
    stats[:ROWS, :] = table
    stats[ROWS:, :] = jnp.zeros((2 * HD - ROWS, HD), F32)
    low = stats[:HD, :].T
    high = stats[HD:, :].T
    for peer in range(SIDE):
        rows = slice(peer * 8, (peer + 1) * 8)
        payload[peer, ROWS:, :] = jnp.concatenate([low[rows], high[rows]], 0).astype(BF)
    for row in range(SLOTS):
        span = slice(row * QROWS, (row + 1) * QROWS)
        for pair in range(PAIRS):
            weight = jnp.concatenate([weights[2 * pair, span, :], weights[2 * pair + 1, span, :]], 0)
            blended = jnp.dot(weight, stored(row, PAIRS + pair), preferred_element_type=F32).astype(BF)
            payload[2 * pair, span, :] = blended[:QROWS]
            payload[2 * pair + 1, span, :] = blended[QROWS:]


def merge_kernel(plan, gathered, everyone, sent, kept):
    y, x = place_of()
    first = jnp.where(y > 1, 2, 0)
    asked = everyone[first + x % 2, :ROWS, :]
    keys = everyone[first, ROWS:, :]
    values = everyone[first + 1, ROWS:, :]
    row = lax.broadcasted_iota(jnp.int32, (ROWS, ENTRIES), 0)
    lane = lax.broadcasted_iota(jnp.int32, (ROWS, ENTRIES), 1)
    causal = (lane // STEPS == row // QROWS) & (lane % STEPS <= row % STEPS)
    fresh = jnp.where(causal, scores_of(asked, keys), FLOOR)
    fresh_top = jnp.max(fresh, axis=1, keepdims=True)

    tops = gathered[:, ROWS:, :].astype(F32)
    blank = jnp.zeros((HD - SIDE * 8, HD), F32)
    low = jnp.concatenate([tops[:, :8, :].reshape(SIDE * 8, HD), blank], 0).T
    high = jnp.concatenate([tops[:, 8:, :].reshape(SIDE * 8, HD), blank], 0).T[: ROWS - HD]
    pairs = jnp.concatenate([low, high], 0)
    both = pairs + pltpu.roll(pairs, HD - 2, 1)
    lane = lax.broadcasted_iota(jnp.int32, (ROWS, HD), 1)
    is_top = (lane % 8 == 0) & (lane < SIDE * 8)
    tops = jnp.where(is_top, both, FLOOR)
    sums = pltpu.roll(both, HD - 1, 1)
    highest = jnp.maximum(jnp.max(tops, axis=1, keepdims=True), fresh_top)
    factors = jnp.where(is_top, jnp.exp(tops - highest), 0.0)
    fresh_weights = jnp.where(causal, jnp.exp(fresh - highest), 0.0)
    totals = jnp.sum(jnp.where(is_top, factors * sums, 0.0), axis=1, keepdims=True)
    totals += jnp.sum(fresh_weights, axis=1, keepdims=True)
    blended = jnp.dot(fresh_weights.astype(BF), values, preferred_element_type=F32)
    for peer in range(SIDE):
        blended += factors[:, peer * 8 : peer * 8 + 1] * gathered[peer, :ROWS, :].astype(F32)
    result = (blended / totals).astype(BF)

    sent[...] = jnp.zeros_like(sent)
    for slot in range(MIG):
        sent[plan[ORIGIN + slot]] = result[slot * QROWS : (slot + 1) * QROWS]
    for slot in range(RES):
        kept[slot] = result[(MIG + slot) * QROWS : (MIG + slot + 1) * QROWS]


def select_kernel(plan, returned, kept, out):
    for slot in range(RES):
        out[slot] = kept[slot]
    for slot in range(MIG):
        out[RES + slot] = returned[plan[TARGET + slot]]


def body(
    queries,
    new_entries,
    resident_cache,
    prefill_cache,
    resident_kept,
    kept_tokens,
    prefill_slot,
    decode_slot,
):
    shape = jax.ShapeDtypeStruct
    whole = [(y, x) for y in range(SIDE) for x in range(SIDE)]
    peers = [[y * SIDE + x for y in (low, 3 - low) for x in (2 * half, 2 * half + 1)] for low in range(2) for half in range(2)]

    turned = [[group ^ TURN for group in range(GROUPS)]]

    def across(array):
        return lax.all_to_all(array, "tensor", 0, 0, axis_index_groups=peers, tiled=True)

    asked = queries.reshape(SLOTS, STEPS, HEADS, HD).transpose(0, 2, 1, 3)
    held = [
        ((GROUPS, TILES, STEPS, HD), BF),
        ((RES, TILES, STEPS, HD), BF),
    ]
    taken = [
        *([((2, HD), jnp.int32)] * 3),
        ((1, HD), jnp.int32),
        ((SLOTS, HEADS, STEPS, HD), BF),
        ((SLOTS, STEPS, HD), BF),
    ]
    plan, sent, kept = call(
        pack_kernel,
        (shape((2 * MIG + SLOTS,), jnp.int32), *(shape(*one) for one in held)),
        [HB] * 6,
        scratch=[pltpu.VMEM(*one) for one in taken + held]
        + [pltpu.SemaphoreType.DMA((6,)), pltpu.SemaphoreType.DMA((len(held),))],
        limit=FULL,
        places=(SM, *([ANY] * len(held))),
    )(
        decode_slot.reshape(2, HD),
        prefill_slot.reshape(2, HD),
        kept_tokens.reshape(2, HD),
        resident_kept.reshape(1, HD),
        asked,
        new_entries,
    )
    arrived = lax.all_to_all(sent, "group", 0, 0, axis_index_groups=turned, tiled=True)

    split = call(
        split_kernel,
        (shape((SLOTS, STRIDE, 2 * PAIRS * HD), BF),) * SIDE,
        [VM, VM],
        moved=3 * 2**20,
    )(prefill_cache, resident_cache)
    blocks = [split[0]]
    for step in (3, 1, 2):
        steps = []
        for y, x in whole:
            other, side = swapped(step, y, x)
            steps.append((y * SIDE + x, other * SIDE + side))
        blocks.append(lax.ppermute(split[step], "tensor", steps))

    asking = call(
        spread_kernel, shape((SIDE, SLOTS * TILES, STEPS, HD), BF), [SM, VM, VM]
    )(plan, arrived, kept)
    everyone = across(asking).reshape(SIDE, ROWS + ENTRIES, HD)

    payload = call(
        partial_kernel,
        shape((SIDE, PAYLOAD, HD), BF),
        [SM] + [VM] * (1 + SIDE),
        flops=10**8,
        moved=3 * 2**20,
        scratch=[
            pltpu.VMEM((SIDE, ROWS, HD), F32),
            pltpu.VMEM((SIDE, ROWS, HD), BF),
            pltpu.VMEM((2 * HD, HD), F32),
        ],
    )(plan, everyone, *blocks)
    gathered = across(payload)

    finished, here = call(
        merge_kernel,
        (shape((GROUPS, QROWS, HD), BF), shape((RES, QROWS, HD), BF)),
        [SM, VM, VM],
    )(plan, gathered, everyone)
    returned = lax.all_to_all(finished, "group", 0, 0, tiled=True)

    result = call(select_kernel, shape((SLOTS, QROWS, HD), BF), [SM, VM, VM])(plan, returned, here)
    result = result.reshape(SLOTS, HEADS, STEPS, HD).transpose(0, 2, 1, 3)
    return result.reshape(SLOTS, STEPS, HEADS * HD)


def solution(mesh):
    in_specs = (
        P("group", None, "tensor"),
        P("group", None, None),
        P("group", "tensor", None),
        P("group", "tensor", None),
        P(),
        P(),
        P(),
        P(),
    )
    out_specs = P("group", None, "tensor")
    return jax.shard_map(body, mesh=mesh, in_specs=in_specs, out_specs=out_specs, check_vma=False)
```

```python
import math

import jax
import jax.numpy as jnp
from jax import lax
from jax.experimental import pallas as pl
from jax.experimental.pallas import tpu as pltpu
from jax.sharding import PartitionSpec as P

H = 64
KVH = 8
HD = 128
STEPS = 4
MIG = 8
RES = 4
SLOTS = MIG + RES
GROUPS = 32
FIRST_G, STRIDE_G = 16, 15
SHARDS = 16
SIDE = 4
STRIDE = 32
HEADS = H // SHARDS
PAIRS = KVH // SIDE
QROWS = HEADS * STEPS
ROWS = SLOTS * QROWS
FEATURES = KVH * HD
TILES = HEADS + 1
ENTRIES = SLOTS * STEPS
PAYLOAD = ROWS + 16
FLOOR = -(2.0**100)
SCALE = 1.0 / math.sqrt(HD)
LIMIT = 48 * 1024 * 1024
FULL = 62 * 1024 * 1024
BF = jnp.bfloat16
F32 = jnp.float32

VM = pl.BlockSpec(memory_space=pltpu.VMEM)
SM = pl.BlockSpec(memory_space=pltpu.SMEM)
HB = pl.BlockSpec(memory_space=pltpu.HBM)


ANY = pl.BlockSpec(memory_space=pl.ANY)
TARGET, ORIGIN, LENGTH = 0, MIG, 2 * MIG


def call(kernel, outs, specs, flops=0, moved=0, scratch=(), limit=LIMIT, places=None):
    return pl.pallas_call(
        kernel,
        out_shape=outs,
        in_specs=specs,
        out_specs=jax.tree.map(lambda _: VM, outs) if places is None else places,
        scratch_shapes=scratch,
        compiler_params=pltpu.CompilerParams(vmem_limit_bytes=limit),
        cost_estimate=pl.CostEstimate(flops=flops, bytes_accessed=moved, transcendentals=0),
    )


def swapped(step, y, x):
    return y ^ (step % 2), x ^ (step // 2 * 3)


def class_of(y, x):
    return jnp.minimum(y, 3 - y), x // 2


def place_of():
    shard = lax.axis_index("tensor")
    return shard // SIDE, shard % SIDE


def listed(group):
    return (group * STRIDE_G + FIRST_G) % GROUPS


def pack_kernel(*refs):
    given, plan, outs, refs = refs[:6], refs[6], refs[7:9], refs[9:]
    inside, (sent, kept), (come, go) = refs[:6], refs[6:8], refs[8:]
    shard, group = lax.axis_index("tensor"), lax.axis_index("group")
    first = pl.multiple_of(shard % 2 * FEATURES + shard // 2 * HD, HD)
    given = list(given)
    given[5] = given[5].at[:, :, pl.ds(first, HD)]
    copies = [pltpu.make_async_copy(p, q, come.at[k]) for k, (p, q) in enumerate(zip(given, inside))]
    for copy in copies:
        copy.start()
    sent[...] = jnp.zeros_like(sent)
    for copy in copies:
        copy.wait()
    names, holders, tokens, residents = (ref[...].astype(F32) for ref in inside[:4])
    asked, fresh = inside[4:]

    def found(where, name, values):
        return jnp.sum(jnp.where(where == name, values, 0.0)).astype(jnp.int32)

    for slot in range(RES):
        kept[slot, :HEADS] = asked[slot]
        kept[slot, HEADS] = fresh[slot]
    for slot in range(MIG):
        name = (group * SLOTS + RES + slot).astype(F32)
        to = lax.div(found(names, name, holders), MIG)
        plan[TARGET + slot] = to
        sent[listed(to), :HEADS] = asked[RES + slot]
        sent[listed(to), HEADS] = fresh[RES + slot]
    writes = [pltpu.make_async_copy(p, q, go.at[k]) for k, (p, q) in enumerate(zip((sent, kept), outs))]
    writes[0].start()
    writes[1].start()
    for slot in range(MIG):
        name = (group * MIG + slot).astype(F32)
        plan[ORIGIN + slot] = lax.div(found(holders, name, names), SLOTS)
        plan[LENGTH + slot] = found(holders, name, tokens)
    lane = lax.broadcasted_iota(jnp.int32, (1, HD), 1)
    for slot in range(RES):
        plan[LENGTH + MIG + slot] = found(lane, group * RES + slot, residents)
    for write in writes:
        write.wait()


def split_kernel(moved, resident, *outs):
    y, x = place_of()
    for step, out in enumerate(outs):
        low, half = class_of(*swapped(step, y, x))
        for place, pair in enumerate((2 * low + half, 6 - 2 * low + half)):
            for part in range(2):
                lanes = pl.ds(pl.multiple_of(pair * HD + part * FEATURES, HD), HD)
                columns = slice((part * PAIRS + place) * HD, (part * PAIRS + place + 1) * HD)
                out[:MIG, :, columns] = moved[:, :, lanes]
                out[MIG:, :, columns] = resident[:, :, lanes]


def spread_kernel(plan, arrived, kept, asking):
    for row in range(SLOTS):
        chunk = arrived.at[listed(plan[ORIGIN + row])] if row < MIG else kept.at[row - MIG]
        for peer in range(SIDE):
            asking[peer, row * HEADS : (row + 1) * HEADS] = chunk[:HEADS]
            asking[peer, SLOTS * HEADS + row] = chunk[HEADS]


def scores_of(left, right):
    return lax.dot_general(left, right, (((1,), (1,)), ((), ())), preferred_element_type=F32) * SCALE


def partial_kernel(plan, asking, *rest):
    *blocks, payload, scores, weights, stats = rest
    column = lax.broadcasted_iota(jnp.int32, (1, HD), 1)
    block = column // STRIDE
    y, x = swapped(jnp.where(block == 0, 0, (block + 1) % 3 + 1), *place_of())
    position = (y * SIDE + x) * STRIDE + column % STRIDE

    def stored(row, place):
        lanes = slice(place * HD, (place + 1) * HD)
        return jnp.concatenate([block[row, :, lanes] for block in blocks], 0)

    for row in range(SLOTS):
        usable = position < plan[LENGTH + row]
        span = slice(row * QROWS, (row + 1) * QROWS)
        for pair in range(PAIRS):
            asked = jnp.concatenate([asking[2 * pair, span, :], asking[2 * pair + 1, span, :]], 0)
            found = jnp.where(usable, scores_of(asked, stored(row, pair)), FLOOR)
            scores[2 * pair, span, :] = found[:QROWS]
            scores[2 * pair + 1, span, :] = found[QROWS:]
    lane = lax.broadcasted_iota(jnp.int32, (ROWS, HD), 1)
    table = jnp.zeros((ROWS, HD), F32)
    for peer in range(SIDE):
        found = scores[peer]
        top = jnp.max(found, axis=1, keepdims=True)
        first = top.astype(BF).astype(F32)
        second = (top - first).astype(BF).astype(F32)
        weight = jnp.exp(found - (first + second))
        total = jnp.sum(weight, axis=1, keepdims=True)
        weights[peer] = weight.astype(BF)
        total_first = total.astype(BF).astype(F32)
        for place, value in enumerate((first, total_first, second, total - total_first)):
            table = jnp.where(lane == peer * 8 + place, value, table)
    stats[:ROWS, :] = table
    stats[ROWS:, :] = jnp.zeros((2 * HD - ROWS, HD), F32)
    low = stats[:HD, :].T
    high = stats[HD:, :].T
    for peer in range(SIDE):
        rows = slice(peer * 8, (peer + 1) * 8)
        payload[peer, ROWS:, :] = jnp.concatenate([low[rows], high[rows]], 0).astype(BF)
    for row in range(SLOTS):
        span = slice(row * QROWS, (row + 1) * QROWS)
        for pair in range(PAIRS):
            weight = jnp.concatenate([weights[2 * pair, span, :], weights[2 * pair + 1, span, :]], 0)
            blended = jnp.dot(weight, stored(row, PAIRS + pair), preferred_element_type=F32).astype(BF)
            payload[2 * pair, span, :] = blended[:QROWS]
            payload[2 * pair + 1, span, :] = blended[QROWS:]


def merge_kernel(plan, gathered, everyone, sent, kept):
    y, x = place_of()
    first = jnp.where(y > 1, 2, 0)
    asked = everyone[first + x % 2, :ROWS, :]
    keys = everyone[first, ROWS:, :]
    values = everyone[first + 1, ROWS:, :]
    row = lax.broadcasted_iota(jnp.int32, (ROWS, ENTRIES), 0)
    lane = lax.broadcasted_iota(jnp.int32, (ROWS, ENTRIES), 1)
    causal = (lane // STEPS == row // QROWS) & (lane % STEPS <= row % STEPS)
    fresh = jnp.where(causal, scores_of(asked, keys), FLOOR)
    fresh_top = jnp.max(fresh, axis=1, keepdims=True)

    tops = gathered[:, ROWS:, :].astype(F32)
    blank = jnp.zeros((HD - SIDE * 8, HD), F32)
    low = jnp.concatenate([tops[:, :8, :].reshape(SIDE * 8, HD), blank], 0).T
    high = jnp.concatenate([tops[:, 8:, :].reshape(SIDE * 8, HD), blank], 0).T[: ROWS - HD]
    pairs = jnp.concatenate([low, high], 0)
    both = pairs + pltpu.roll(pairs, HD - 2, 1)
    lane = lax.broadcasted_iota(jnp.int32, (ROWS, HD), 1)
    is_top = (lane % 8 == 0) & (lane < SIDE * 8)
    tops = jnp.where(is_top, both, FLOOR)
    sums = pltpu.roll(both, HD - 1, 1)
    highest = jnp.maximum(jnp.max(tops, axis=1, keepdims=True), fresh_top)
    factors = jnp.where(is_top, jnp.exp(tops - highest), 0.0)
    fresh_weights = jnp.where(causal, jnp.exp(fresh - highest), 0.0)
    totals = jnp.sum(jnp.where(is_top, factors * sums, 0.0), axis=1, keepdims=True)
    totals += jnp.sum(fresh_weights, axis=1, keepdims=True)
    blended = jnp.dot(fresh_weights.astype(BF), values, preferred_element_type=F32)
    for peer in range(SIDE):
        blended += factors[:, peer * 8 : peer * 8 + 1] * gathered[peer, :ROWS, :].astype(F32)
    result = (blended / totals).astype(BF)

    sent[...] = jnp.zeros_like(sent)
    for slot in range(MIG):
        sent[listed(plan[ORIGIN + slot])] = result[slot * QROWS : (slot + 1) * QROWS]
    for slot in range(RES):
        kept[slot] = result[(MIG + slot) * QROWS : (MIG + slot + 1) * QROWS]


def select_kernel(plan, returned, kept, out):
    for slot in range(RES):
        out[slot] = kept[slot]
    for slot in range(MIG):
        out[RES + slot] = returned[listed(plan[TARGET + slot])]


def body(
    queries,
    new_entries,
    resident_cache,
    prefill_cache,
    resident_kept,
    kept_tokens,
    prefill_slot,
    decode_slot,
):
    shape = jax.ShapeDtypeStruct
    whole = [(y, x) for y in range(SIDE) for x in range(SIDE)]
    peers = [[y * SIDE + x for y in (low, 3 - low) for x in (2 * half, 2 * half + 1)] for low in range(2) for half in range(2)]

    turned = [[listed(place) for place in range(GROUPS)]]

    def around(array):
        return lax.all_to_all(array, "group", 0, 0, axis_index_groups=turned, tiled=True)

    def across(array):
        return lax.all_to_all(array, "tensor", 0, 0, axis_index_groups=peers, tiled=True)

    asked = queries.reshape(SLOTS, STEPS, HEADS, HD).transpose(0, 2, 1, 3)
    held = [
        ((GROUPS, TILES, STEPS, HD), BF),
        ((RES, TILES, STEPS, HD), BF),
    ]
    taken = [
        *([((2, HD), jnp.int32)] * 3),
        ((1, HD), jnp.int32),
        ((SLOTS, HEADS, STEPS, HD), BF),
        ((SLOTS, STEPS, HD), BF),
    ]
    plan, sent, kept = call(
        pack_kernel,
        (shape((2 * MIG + SLOTS,), jnp.int32), *(shape(*one) for one in held)),
        [HB] * 6,
        scratch=[pltpu.VMEM(*one) for one in taken + held]
        + [pltpu.SemaphoreType.DMA((6,)), pltpu.SemaphoreType.DMA((len(held),))],
        limit=FULL,
        places=(SM, *([ANY] * len(held))),
    )(
        decode_slot.reshape(2, HD),
        prefill_slot.reshape(2, HD),
        kept_tokens.reshape(2, HD),
        resident_kept.reshape(1, HD),
        asked,
        new_entries,
    )
    arrived = around(sent)

    split = call(
        split_kernel,
        (shape((SLOTS, STRIDE, 2 * PAIRS * HD), BF),) * SIDE,
        [VM, VM],
        moved=3 * 2**20,
    )(prefill_cache, resident_cache)
    blocks = [split[0]]
    for step in (3, 1, 2):
        steps = []
        for y, x in whole:
            other, side = swapped(step, y, x)
            steps.append((y * SIDE + x, other * SIDE + side))
        blocks.append(lax.ppermute(split[step], "tensor", steps))

    asking = call(
        spread_kernel, shape((SIDE, SLOTS * TILES, STEPS, HD), BF), [SM, VM, VM]
    )(plan, arrived, kept)
    everyone = across(asking).reshape(SIDE, ROWS + ENTRIES, HD)

    payload = call(
        partial_kernel,
        shape((SIDE, PAYLOAD, HD), BF),
        [SM] + [VM] * (1 + SIDE),
        flops=10**8,
        moved=3 * 2**20,
        scratch=[
            pltpu.VMEM((SIDE, ROWS, HD), F32),
            pltpu.VMEM((SIDE, ROWS, HD), BF),
            pltpu.VMEM((2 * HD, HD), F32),
        ],
    )(plan, everyone, *blocks)
    gathered = across(payload)

    finished, here = call(
        merge_kernel,
        (shape((GROUPS, QROWS, HD), BF), shape((RES, QROWS, HD), BF)),
        [SM, VM, VM],
    )(plan, gathered, everyone)
    returned = around(finished)

    result = call(select_kernel, shape((SLOTS, QROWS, HD), BF), [SM, VM, VM])(plan, returned, here)
    result = result.reshape(SLOTS, HEADS, STEPS, HD).transpose(0, 2, 1, 3)
    return result.reshape(SLOTS, STEPS, HEADS * HD)


def solution(mesh):
    in_specs = (
        P("group", None, "tensor"),
        P("group", None, None),
        P("group", "tensor", None),
        P("group", "tensor", None),
        P(),
        P(),
        P(),
        P(),
    )
    out_specs = P("group", None, "tensor")
    return jax.shard_map(body, mesh=mesh, in_specs=in_specs, out_specs=out_specs, check_vma=False)
```

```python
import math

import jax
import jax.numpy as jnp
from jax import lax
from jax.experimental import pallas as pl
from jax.experimental.pallas import tpu as pltpu
from jax.sharding import PartitionSpec as P

H = 64
KVH = 8
HD = 128
STEPS = 4
MIG = 8
RES = 4
SLOTS = MIG + RES
GROUPS = 32
FIRST_G, STRIDE_G = 16, 15
SHARDS = 16
SIDE = 4
STRIDE = 32
HEADS = H // SHARDS
PAIRS = KVH // SIDE
QROWS = HEADS * STEPS
ROWS = SLOTS * QROWS
FEATURES = KVH * HD
TILES = HEADS + 1
ENTRIES = SLOTS * STEPS
PAYLOAD = ROWS + 16
FLOOR = -(2.0**100)
SCALE = 1.0 / math.sqrt(HD)
LIMIT = 48 * 1024 * 1024
FULL = 60 * 1024 * 1024
BF = jnp.bfloat16
F32 = jnp.float32

VM = pl.BlockSpec(memory_space=pltpu.VMEM)
SM = pl.BlockSpec(memory_space=pltpu.SMEM)
HB = pl.BlockSpec(memory_space=pltpu.HBM)


ANY = pl.BlockSpec(memory_space=pl.ANY)

def call(kernel, outs, specs, flops=0, moved=0, scratch=(), limit=LIMIT, places=None):
    return pl.pallas_call(
        kernel,
        out_shape=outs,
        in_specs=specs,
        out_specs=jax.tree.map(lambda _: VM, outs) if places is None else places,
        scratch_shapes=scratch,
        compiler_params=pltpu.CompilerParams(vmem_limit_bytes=limit),
        cost_estimate=pl.CostEstimate(flops=flops, bytes_accessed=moved, transcendentals=0),
    )


def swapped(step, y, x):
    return y ^ (step % 2), x ^ (step // 2 * 3)


def class_of(y, x):
    return jnp.minimum(y, 3 - y), x // 2


def place_of():
    shard = lax.axis_index("tensor")
    return shard // SIDE, shard % SIDE


def listed(group):
    return (group * STRIDE_G + FIRST_G) % GROUPS


def pack_kernel(named, holders, asked, fresh, sent, kept, asked_here, fresh_here, named_here, holders_here, sems):
    shard = lax.axis_index("tensor")
    first = pl.multiple_of(shard % 2 * FEATURES + shard // 2 * HD, HD)
    copies = [
        pltpu.make_async_copy(source, target, sems.at[n])
        for n, (source, target) in enumerate(
            (
                (named, named_here),
                (holders, holders_here),
                (asked, asked_here),
                (fresh.at[:, :, pl.ds(first, HD)], fresh_here),
            )
        )
    ]
    for copy in copies:
        copy.start()
    sent[...] = jnp.zeros_like(sent)
    for copy in copies:
        copy.wait()
    names = named_here[...]
    slots = holders_here[...].astype(F32)
    for slot in range(RES):
        kept[slot, :HEADS] = asked_here[slot]
        kept[slot, HEADS] = fresh_here[slot]
    groups = []
    for slot in range(RES, SLOTS):
        mine = names == lax.axis_index("group") * SLOTS + slot
        groups.append(jnp.sum(jnp.where(mine, slots, 0.0)).astype(jnp.int32) >> 3)
    for slot, group in zip(range(RES, SLOTS), groups):
        sent[listed(group), :HEADS] = asked_here[slot]
        sent[listed(group), HEADS] = fresh_here[slot]


def split_kernel(moved, resident, *outs):
    y, x = place_of()
    for step, out in enumerate(outs):
        low, half = class_of(*swapped(step, y, x))
        for place, pair in enumerate((2 * low + half, 6 - 2 * low + half)):
            for part in range(2):
                lanes = pl.ds(pl.multiple_of(pair * HD + part * FEATURES, HD), HD)
                columns = slice((part * PAIRS + place) * HD, (part * PAIRS + place + 1) * HD)
                out[:MIG, :, columns] = moved[:, :, lanes]
                out[MIG:, :, columns] = resident[:, :, lanes]


def spread_kernel(origin, arrived, kept, asking):
    for row in range(SLOTS):
        chunk = arrived.at[listed(origin[row])] if row < MIG else kept.at[row - MIG]
        for peer in range(SIDE):
            asking[peer, row * HEADS : (row + 1) * HEADS] = chunk[:HEADS]
            asking[peer, SLOTS * HEADS + row] = chunk[HEADS]


def scores_of(left, right):
    return lax.dot_general(left, right, (((1,), (1,)), ((), ())), preferred_element_type=F32) * SCALE


def partial_kernel(lengths, asking, *rest):
    *blocks, payload, scores, weights, stats = rest
    column = lax.broadcasted_iota(jnp.int32, (1, HD), 1)
    block = column // STRIDE
    y, x = swapped(jnp.where(block == 0, 0, (block + 1) % 3 + 1), *place_of())
    position = (y * SIDE + x) * STRIDE + column % STRIDE

    def stored(row, place):
        lanes = slice(place * HD, (place + 1) * HD)
        return jnp.concatenate([block[row, :, lanes] for block in blocks], 0)

    for row in range(SLOTS):
        usable = position < lengths[row]
        span = slice(row * QROWS, (row + 1) * QROWS)
        for pair in range(PAIRS):
            asked = jnp.concatenate([asking[2 * pair, span, :], asking[2 * pair + 1, span, :]], 0)
            found = jnp.where(usable, scores_of(asked, stored(row, pair)), FLOOR)
            scores[2 * pair, span, :] = found[:QROWS]
            scores[2 * pair + 1, span, :] = found[QROWS:]
    lane = lax.broadcasted_iota(jnp.int32, (ROWS, HD), 1)
    table = jnp.zeros((ROWS, HD), F32)
    for peer in range(SIDE):
        found = scores[peer]
        top = jnp.max(found, axis=1, keepdims=True)
        first = top.astype(BF).astype(F32)
        second = (top - first).astype(BF).astype(F32)
        weight = jnp.exp(found - (first + second))
        total = jnp.sum(weight, axis=1, keepdims=True)
        weights[peer] = weight.astype(BF)
        total_first = total.astype(BF).astype(F32)
        for place, value in enumerate((first, total_first, second, total - total_first)):
            table = jnp.where(lane == peer * 8 + place, value, table)
    stats[:ROWS, :] = table
    stats[ROWS:, :] = jnp.zeros((2 * HD - ROWS, HD), F32)
    low = stats[:HD, :].T
    high = stats[HD:, :].T
    for peer in range(SIDE):
        rows = slice(peer * 8, (peer + 1) * 8)
        payload[peer, ROWS:, :] = jnp.concatenate([low[rows], high[rows]], 0).astype(BF)
    for row in range(SLOTS):
        span = slice(row * QROWS, (row + 1) * QROWS)
        for pair in range(PAIRS):
            weight = jnp.concatenate([weights[2 * pair, span, :], weights[2 * pair + 1, span, :]], 0)
            blended = jnp.dot(weight, stored(row, PAIRS + pair), preferred_element_type=F32).astype(BF)
            payload[2 * pair, span, :] = blended[:QROWS]
            payload[2 * pair + 1, span, :] = blended[QROWS:]


def merge_kernel(origin, target, gathered, everyone, sent, kept):
    y, x = place_of()
    first = jnp.where(y > 1, 2, 0)
    asked = everyone[first + x % 2, :ROWS, :]
    keys = everyone[first, ROWS:, :]
    values = everyone[first + 1, ROWS:, :]
    row = lax.broadcasted_iota(jnp.int32, (ROWS, ENTRIES), 0)
    lane = lax.broadcasted_iota(jnp.int32, (ROWS, ENTRIES), 1)
    causal = (lane // STEPS == row // QROWS) & (lane % STEPS <= row % STEPS)
    fresh = jnp.where(causal, scores_of(asked, keys), FLOOR)
    fresh_top = jnp.max(fresh, axis=1, keepdims=True)

    tops = gathered[:, ROWS:, :].astype(F32)
    blank = jnp.zeros((HD - SIDE * 8, HD), F32)
    low = jnp.concatenate([tops[:, :8, :].reshape(SIDE * 8, HD), blank], 0).T
    high = jnp.concatenate([tops[:, 8:, :].reshape(SIDE * 8, HD), blank], 0).T[: ROWS - HD]
    pairs = jnp.concatenate([low, high], 0)
    both = pairs + pltpu.roll(pairs, HD - 2, 1)
    lane = lax.broadcasted_iota(jnp.int32, (ROWS, HD), 1)
    is_top = (lane % 8 == 0) & (lane < SIDE * 8)
    tops = jnp.where(is_top, both, FLOOR)
    sums = pltpu.roll(both, HD - 1, 1)
    highest = jnp.maximum(jnp.max(tops, axis=1, keepdims=True), fresh_top)
    factors = jnp.where(is_top, jnp.exp(tops - highest), 0.0)
    fresh_weights = jnp.where(causal, jnp.exp(fresh - highest), 0.0)
    totals = jnp.sum(jnp.where(is_top, factors * sums, 0.0), axis=1, keepdims=True)
    totals += jnp.sum(fresh_weights, axis=1, keepdims=True)
    blended = jnp.dot(fresh_weights.astype(BF), values, preferred_element_type=F32)
    for peer in range(SIDE):
        blended += factors[:, peer * 8 : peer * 8 + 1] * gathered[peer, :ROWS, :].astype(F32)
    result = (blended / totals).astype(BF)

    sent[...] = jnp.zeros_like(sent)
    for slot in range(MIG):
        sent[listed(origin[slot])] = result[slot * QROWS : (slot + 1) * QROWS]
    for slot in range(RES):
        kept[slot] = result[(MIG + slot) * QROWS : (MIG + slot + 1) * QROWS]


def select_kernel(target, returned, kept, out):
    for slot in range(RES):
        out[slot] = kept[slot]
    for slot in range(MIG):
        out[RES + slot] = returned[listed(target[slot])]


def body(
    queries,
    new_entries,
    resident_cache,
    prefill_cache,
    resident_kept,
    kept_tokens,
    prefill_slot,
    decode_slot,
):
    shape = jax.ShapeDtypeStruct
    whole = [(y, x) for y in range(SIDE) for x in range(SIDE)]
    peers = [[y * SIDE + x for y in (low, 3 - low) for x in (2 * half, 2 * half + 1)] for low in range(2) for half in range(2)]

    turned = [[listed(place) for place in range(GROUPS)]]

    def around(array):
        return lax.all_to_all(array, "group", 0, 0, axis_index_groups=turned, tiled=True)

    def across(array):
        return lax.all_to_all(array, "tensor", 0, 0, axis_index_groups=peers, tiled=True)

    asked = queries.reshape(SLOTS, STEPS, HEADS, HD).transpose(0, 2, 1, 3)
    sent, kept = call(
        pack_kernel,
        (shape((GROUPS, TILES, STEPS, HD), BF), shape((RES, TILES, STEPS, HD), BF)),
        [HB] * 4,
        scratch=[
            pltpu.VMEM((SLOTS, HEADS, STEPS, HD), BF),
            pltpu.VMEM((SLOTS, STEPS, HD), BF),
            pltpu.VMEM((2, HD), jnp.int32),
            pltpu.VMEM((2, HD), jnp.int32),
            pltpu.SemaphoreType.DMA((4,)),
        ],
        limit=FULL,
    )(decode_slot.reshape(2, HD), prefill_slot.reshape(2, HD), asked, new_entries)
    arrived = around(sent)

    later = (resident_kept, kept_tokens, prefill_slot, decode_slot)
    later, kept = lax.optimization_barrier((later, kept))
    resident_kept, kept_tokens, prefill_slot, decode_slot = later
    group = lax.axis_index("group")

    def looked_up(names, first, values):
        wanted = first + jnp.arange(MIG, dtype=jnp.int32)
        return jnp.sum(jnp.where(names[None, :] == wanted[:, None], values[None, :], 0), axis=1)

    target = looked_up(decode_slot, group * SLOTS + RES, prefill_slot) // MIG
    origin = looked_up(prefill_slot, group * MIG, decode_slot) // SLOTS
    moved_len = looked_up(prefill_slot, group * MIG, kept_tokens)
    resident_len = lax.dynamic_slice_in_dim(resident_kept, group * RES, RES)
    lengths = jnp.concatenate([moved_len, resident_len])

    split = call(
        split_kernel,
        (shape((SLOTS, STRIDE, 2 * PAIRS * HD), BF),) * SIDE,
        [VM, VM],
        moved=3 * 2**20,
    )(prefill_cache, resident_cache)
    blocks = [split[0]]
    for step in (3, 1, 2):
        steps = []
        for y, x in whole:
            other, side = swapped(step, y, x)
            steps.append((y * SIDE + x, other * SIDE + side))
        blocks.append(lax.ppermute(split[step], "tensor", steps))

    asking = call(
        spread_kernel, shape((SIDE, SLOTS * TILES, STEPS, HD), BF), [SM, VM, VM]
    )(origin, arrived, kept)
    everyone = across(asking).reshape(SIDE, ROWS + ENTRIES, HD)

    payload = call(
        partial_kernel,
        shape((SIDE, PAYLOAD, HD), BF),
        [SM] + [VM] * (1 + SIDE),
        flops=10**8,
        moved=3 * 2**20,
        scratch=[
            pltpu.VMEM((SIDE, ROWS, HD), F32),
            pltpu.VMEM((SIDE, ROWS, HD), BF),
            pltpu.VMEM((2 * HD, HD), F32),
        ],
    )(lengths, everyone, *blocks)
    gathered = across(payload)

    finished, here = call(
        merge_kernel,
        (shape((GROUPS, QROWS, HD), BF), shape((RES, QROWS, HD), BF)),
        [SM, SM, VM, VM],
    )(origin, target, gathered, everyone)
    returned = around(finished)

    result = call(select_kernel, shape((SLOTS, QROWS, HD), BF), [SM, VM, VM])(target, returned, here)
    result = result.reshape(SLOTS, HEADS, STEPS, HD).transpose(0, 2, 1, 3)
    return result.reshape(SLOTS, STEPS, HEADS * HD)


def solution(mesh):
    in_specs = (
        P("group", None, "tensor"),
        P("group", None, None),
        P("group", "tensor", None),
        P("group", "tensor", None),
        P(),
        P(),
        P(),
        P(),
    )
    out_specs = P("group", None, "tensor")
    return jax.shard_map(body, mesh=mesh, in_specs=in_specs, out_specs=out_specs, check_vma=False)
```

```python
import math

import jax
import jax.numpy as jnp
from jax import lax
from jax.experimental import pallas as pl
from jax.experimental.pallas import tpu as pltpu
from jax.sharding import PartitionSpec as P

H = 64
KVH = 8
HD = 128
STEPS = 4
MIG = 8
RES = 4
SLOTS = MIG + RES
GROUPS = 32
FIRST_G, STRIDE_G = 16, 15
SHARDS = 16
SIDE = 4
STRIDE = 32
HEADS = H // SHARDS
PAIRS = KVH // SIDE
QROWS = HEADS * STEPS
ROWS = SLOTS * QROWS
FEATURES = KVH * HD
TILES = HEADS + 1
ENTRIES = SLOTS * STEPS
PAYLOAD = ROWS + 16
FLOOR = -(2.0**100)
SCALE = 1.0 / math.sqrt(HD)
LIMIT = 48 * 1024 * 1024
FULL = 60 * 1024 * 1024
BF = jnp.bfloat16
F32 = jnp.float32

VM = pl.BlockSpec(memory_space=pltpu.VMEM)
SM = pl.BlockSpec(memory_space=pltpu.SMEM)
HB = pl.BlockSpec(memory_space=pltpu.HBM)


ANY = pl.BlockSpec(memory_space=pl.ANY)

def call(kernel, outs, specs, flops=0, moved=0, scratch=(), limit=LIMIT, places=None):
    return pl.pallas_call(
        kernel,
        out_shape=outs,
        in_specs=specs,
        out_specs=jax.tree.map(lambda _: VM, outs) if places is None else places,
        scratch_shapes=scratch,
        compiler_params=pltpu.CompilerParams(vmem_limit_bytes=limit),
        cost_estimate=pl.CostEstimate(flops=flops, bytes_accessed=moved, transcendentals=0),
    )


def swapped(step, y, x):
    return y ^ (step % 2), x ^ (step // 2 * 3)


def class_of(y, x):
    return jnp.minimum(y, 3 - y), x // 2


def place_of():
    shard = lax.axis_index("tensor")
    return shard // SIDE, shard % SIDE


def listed(group):
    return (group * STRIDE_G + FIRST_G) % GROUPS


def pack_kernel(named, holders, asked, fresh, sent, kept, asked_here, fresh_here, named_here, holders_here, sems):
    shard = lax.axis_index("tensor")
    first = pl.multiple_of(shard % 2 * FEATURES + shard // 2 * HD, HD)
    copies = [
        pltpu.make_async_copy(source, target, sems.at[n])
        for n, (source, target) in enumerate(
            (
                (named, named_here),
                (holders, holders_here),
                (asked, asked_here),
                (fresh.at[:, :, pl.ds(first, HD)], fresh_here),
            )
        )
    ]
    for copy in copies:
        copy.start()
    sent[...] = jnp.zeros_like(sent)
    for copy in copies:
        copy.wait()
    names = named_here[...]
    slots = holders_here[...].astype(F32)
    for slot in range(RES):
        kept[slot, :HEADS] = asked_here[slot]
        kept[slot, HEADS] = fresh_here[slot]
    groups = []
    for slot in range(RES, SLOTS):
        mine = names == lax.axis_index("group") * SLOTS + slot
        groups.append(jnp.sum(jnp.where(mine, slots, 0.0)).astype(jnp.int32) >> 3)
    for slot, group in zip(range(RES, SLOTS), groups):
        sent[listed(group), :HEADS] = asked_here[slot]
        sent[listed(group), HEADS] = fresh_here[slot]


def split_kernel(moved, resident, *outs):
    y, x = place_of()
    for step, out in enumerate(outs):
        low, half = class_of(*swapped(step, y, x))
        for place, pair in enumerate((2 * low + half, 6 - 2 * low + half)):
            for part in range(2):
                lanes = pl.ds(pl.multiple_of(pair * HD + part * FEATURES, HD), HD)
                columns = slice((part * PAIRS + place) * HD, (part * PAIRS + place + 1) * HD)
                out[:MIG, :, columns] = moved[:, :, lanes]
                out[MIG:, :, columns] = resident[:, :, lanes]


def spread_kernel(origin, arrived, kept, asking):
    for row in range(SLOTS):
        chunk = arrived.at[listed(origin[row])] if row < MIG else kept.at[row - MIG]
        for peer in range(SIDE):
            asking[peer, row * HEADS : (row + 1) * HEADS] = chunk[:HEADS]
            asking[peer, SLOTS * HEADS + row] = chunk[HEADS]


def scores_of(left, right):
    return lax.dot_general(left, right, (((1,), (1,)), ((), ())), preferred_element_type=F32) * SCALE


def partial_kernel(lengths, target, asking, *rest):
    *blocks, payload, scores, weights, stats = rest
    column = lax.broadcasted_iota(jnp.int32, (1, HD), 1)
    block = column // STRIDE
    y, x = swapped(jnp.where(block == 0, 0, (block + 1) % 3 + 1), *place_of())
    position = (y * SIDE + x) * STRIDE + column % STRIDE

    def stored(row, place):
        lanes = slice(place * HD, (place + 1) * HD)
        return jnp.concatenate([block[row, :, lanes] for block in blocks], 0)

    for row in range(SLOTS):
        usable = position < lengths[row]
        span = slice(row * QROWS, (row + 1) * QROWS)
        for pair in range(PAIRS):
            asked = jnp.concatenate([asking[2 * pair, span, :], asking[2 * pair + 1, span, :]], 0)
            found = jnp.where(usable, scores_of(asked, stored(row, pair)), FLOOR)
            scores[2 * pair, span, :] = found[:QROWS]
            scores[2 * pair + 1, span, :] = found[QROWS:]
    lane = lax.broadcasted_iota(jnp.int32, (ROWS, HD), 1)
    table = jnp.zeros((ROWS, HD), F32)
    for peer in range(SIDE):
        found = scores[peer]
        top = jnp.max(found, axis=1, keepdims=True)
        first = top.astype(BF).astype(F32)
        second = (top - first).astype(BF).astype(F32)
        weight = jnp.exp(found - (first + second))
        total = jnp.sum(weight, axis=1, keepdims=True)
        weights[peer] = weight.astype(BF)
        total_first = total.astype(BF).astype(F32)
        for place, value in enumerate((first, total_first, second, total - total_first)):
            table = jnp.where(lane == peer * 8 + place, value, table)
    stats[:ROWS, :] = table
    stats[ROWS:, :] = jnp.zeros((2 * HD - ROWS, HD), F32)
    low = stats[:HD, :].T
    high = stats[HD:, :].T
    for peer in range(SIDE):
        rows = slice(peer * 8, (peer + 1) * 8)
        payload[peer, ROWS:, :] = jnp.concatenate([low[rows], high[rows]], 0).astype(BF)
    for row in range(SLOTS):
        span = slice(row * QROWS, (row + 1) * QROWS)
        for pair in range(PAIRS):
            weight = jnp.concatenate([weights[2 * pair, span, :], weights[2 * pair + 1, span, :]], 0)
            blended = jnp.dot(weight, stored(row, PAIRS + pair), preferred_element_type=F32).astype(BF)
            payload[2 * pair, span, :] = blended[:QROWS]
            payload[2 * pair + 1, span, :] = blended[QROWS:]


def merge_kernel(origin, target, gathered, everyone, sent, kept):
    y, x = place_of()
    first = jnp.where(y > 1, 2, 0)
    asked = everyone[first + x % 2, :ROWS, :]
    keys = everyone[first, ROWS:, :]
    values = everyone[first + 1, ROWS:, :]
    row = lax.broadcasted_iota(jnp.int32, (ROWS, ENTRIES), 0)
    lane = lax.broadcasted_iota(jnp.int32, (ROWS, ENTRIES), 1)
    causal = (lane // STEPS == row // QROWS) & (lane % STEPS <= row % STEPS)
    fresh = jnp.where(causal, scores_of(asked, keys), FLOOR)
    fresh_top = jnp.max(fresh, axis=1, keepdims=True)

    tops = gathered[:, ROWS:, :].astype(F32)
    blank = jnp.zeros((HD - SIDE * 8, HD), F32)
    low = jnp.concatenate([tops[:, :8, :].reshape(SIDE * 8, HD), blank], 0).T
    high = jnp.concatenate([tops[:, 8:, :].reshape(SIDE * 8, HD), blank], 0).T[: ROWS - HD]
    pairs = jnp.concatenate([low, high], 0)
    both = pairs + pltpu.roll(pairs, HD - 2, 1)
    lane = lax.broadcasted_iota(jnp.int32, (ROWS, HD), 1)
    is_top = (lane % 8 == 0) & (lane < SIDE * 8)
    tops = jnp.where(is_top, both, FLOOR)
    sums = pltpu.roll(both, HD - 1, 1)
    highest = jnp.maximum(jnp.max(tops, axis=1, keepdims=True), fresh_top)
    factors = jnp.where(is_top, jnp.exp(tops - highest), 0.0)
    fresh_weights = jnp.where(causal, jnp.exp(fresh - highest), 0.0)
    totals = jnp.sum(jnp.where(is_top, factors * sums, 0.0), axis=1, keepdims=True)
    totals += jnp.sum(fresh_weights, axis=1, keepdims=True)
    blended = jnp.dot(fresh_weights.astype(BF), values, preferred_element_type=F32)
    for peer in range(SIDE):
        blended += factors[:, peer * 8 : peer * 8 + 1] * gathered[peer, :ROWS, :].astype(F32)
    result = (blended / totals).astype(BF)

    sent[...] = jnp.zeros_like(sent)
    for slot in range(MIG):
        sent[listed(origin[slot])] = result[slot * QROWS : (slot + 1) * QROWS]
    for slot in range(RES):
        kept[slot] = result[(MIG + slot) * QROWS : (MIG + slot + 1) * QROWS]


def select_kernel(target, returned, kept, out):
    for slot in range(RES):
        out[slot] = kept[slot]
    for slot in range(MIG):
        out[RES + slot] = returned[listed(target[slot])]


def body(
    queries,
    new_entries,
    resident_cache,
    prefill_cache,
    resident_kept,
    kept_tokens,
    prefill_slot,
    decode_slot,
):
    shape = jax.ShapeDtypeStruct
    whole = [(y, x) for y in range(SIDE) for x in range(SIDE)]
    peers = [[y * SIDE + x for y in (low, 3 - low) for x in (2 * half, 2 * half + 1)] for low in range(2) for half in range(2)]

    turned = [[listed(place) for place in range(GROUPS)]]

    def around(array):
        return lax.all_to_all(array, "group", 0, 0, axis_index_groups=turned, tiled=True)

    def across(array):
        return lax.all_to_all(array, "tensor", 0, 0, axis_index_groups=peers, tiled=True)

    asked = queries.reshape(SLOTS, STEPS, HEADS, HD).transpose(0, 2, 1, 3)
    sent, kept = call(
        pack_kernel,
        (shape((GROUPS, TILES, STEPS, HD), BF), shape((RES, TILES, STEPS, HD), BF)),
        [HB] * 4,
        scratch=[
            pltpu.VMEM((SLOTS, HEADS, STEPS, HD), BF),
            pltpu.VMEM((SLOTS, STEPS, HD), BF),
            pltpu.VMEM((2, HD), jnp.int32),
            pltpu.VMEM((2, HD), jnp.int32),
            pltpu.SemaphoreType.DMA((4,)),
        ],
        limit=FULL,
    )(decode_slot.reshape(2, HD), prefill_slot.reshape(2, HD), asked, new_entries)
    arrived = around(sent)

    later = (resident_kept, kept_tokens, prefill_slot, decode_slot)
    later, kept = lax.optimization_barrier((later, kept))
    resident_kept, kept_tokens, prefill_slot, decode_slot = later
    group = lax.axis_index("group")

    def looked_up(names, first, values):
        wanted = first + jnp.arange(MIG, dtype=jnp.int32)
        return jnp.sum(jnp.where(names[None, :] == wanted[:, None], values[None, :], 0), axis=1)

    target = looked_up(decode_slot, group * SLOTS + RES, prefill_slot) // MIG
    origin = looked_up(prefill_slot, group * MIG, decode_slot) // SLOTS
    moved_len = looked_up(prefill_slot, group * MIG, kept_tokens)
    resident_len = lax.dynamic_slice_in_dim(resident_kept, group * RES, RES)
    lengths = jnp.concatenate([moved_len, resident_len])

    split = call(
        split_kernel,
        (shape((SLOTS, STRIDE, 2 * PAIRS * HD), BF),) * SIDE,
        [VM, VM],
        moved=3 * 2**20,
    )(prefill_cache, resident_cache)
    blocks = [split[0]]
    for step in (3, 1, 2):
        steps = []
        for y, x in whole:
            other, side = swapped(step, y, x)
            steps.append((y * SIDE + x, other * SIDE + side))
        blocks.append(lax.ppermute(split[step], "tensor", steps))

    asking = call(
        spread_kernel, shape((SIDE, SLOTS * TILES, STEPS, HD), BF), [SM, VM, VM]
    )(origin, arrived, kept)
    everyone = across(asking).reshape(SIDE, ROWS + ENTRIES, HD)

    payload = call(
        partial_kernel,
        shape((SIDE, PAYLOAD, HD), BF),
        [SM, SM] + [VM] * (1 + SIDE),
        flops=10**8,
        moved=3 * 2**20,
        scratch=[
            pltpu.VMEM((SIDE, ROWS, HD), F32),
            pltpu.VMEM((SIDE, ROWS, HD), BF),
            pltpu.VMEM((2 * HD, HD), F32),
        ],
    )(lengths, target, everyone, *blocks)
    gathered = across(payload)

    finished, here = call(
        merge_kernel,
        (shape((GROUPS, QROWS, HD), BF), shape((RES, QROWS, HD), BF)),
        [SM, SM, VM, VM],
    )(origin, target, gathered, everyone)
    returned = around(finished)

    result = call(select_kernel, shape((SLOTS, QROWS, HD), BF), [SM, VM, VM])(target, returned, here)
    result = result.reshape(SLOTS, HEADS, STEPS, HD).transpose(0, 2, 1, 3)
    return result.reshape(SLOTS, STEPS, HEADS * HD)


def solution(mesh):
    in_specs = (
        P("group", None, "tensor"),
        P("group", None, None),
        P("group", "tensor", None),
        P("group", "tensor", None),
        P(),
        P(),
        P(),
        P(),
    )
    out_specs = P("group", None, "tensor")
    return jax.shard_map(body, mesh=mesh, in_specs=in_specs, out_specs=out_specs, check_vma=False)
```

```python
import math

import jax
import jax.numpy as jnp
from jax import lax
from jax.experimental import pallas as pl
from jax.experimental.pallas import tpu as pltpu
from jax.sharding import PartitionSpec as P

H = 64
KVH = 8
HD = 128
STEPS = 4
MIG = 8
RES = 4
SLOTS = MIG + RES
GROUPS = 32
FIRST_G, STRIDE_G = 16, 15
SHARDS = 16
SIDE = 4
STRIDE = 32
HEADS = H // SHARDS
PAIRS = KVH // SIDE
QROWS = HEADS * STEPS
ROWS = SLOTS * QROWS
FEATURES = KVH * HD
TILES = HEADS + 1
ENTRIES = SLOTS * STEPS
PAYLOAD = ROWS + 16
FLOOR = -(2.0**100)
SCALE = 1.0 / math.sqrt(HD)
LIMIT = 48 * 1024 * 1024
FULL = 60 * 1024 * 1024
BF = jnp.bfloat16
F32 = jnp.float32

VM = pl.BlockSpec(memory_space=pltpu.VMEM)
SM = pl.BlockSpec(memory_space=pltpu.SMEM)
HB = pl.BlockSpec(memory_space=pltpu.HBM)


ANY = pl.BlockSpec(memory_space=pl.ANY)

def call(kernel, outs, specs, flops=0, moved=0, scratch=(), limit=LIMIT, places=None):
    return pl.pallas_call(
        kernel,
        out_shape=outs,
        in_specs=specs,
        out_specs=jax.tree.map(lambda _: VM, outs) if places is None else places,
        scratch_shapes=scratch,
        compiler_params=pltpu.CompilerParams(vmem_limit_bytes=limit),
        cost_estimate=pl.CostEstimate(flops=flops, bytes_accessed=moved, transcendentals=0),
    )


def swapped(step, y, x):
    return y ^ (step % 2), x ^ (step // 2 * 3)


def class_of(y, x):
    return jnp.minimum(y, 3 - y), x // 2


def place_of():
    shard = lax.axis_index("tensor")
    return shard // SIDE, shard % SIDE


def listed(group):
    return (group * STRIDE_G + FIRST_G) % GROUPS


def pack_kernel(named, holders, asked, fresh, sent, kept, asked_here, fresh_here, named_here, holders_here, sems):
    shard = lax.axis_index("tensor")
    first = pl.multiple_of(shard % 2 * FEATURES + shard // 2 * HD, HD)
    copies = [
        pltpu.make_async_copy(source, target, sems.at[n])
        for n, (source, target) in enumerate(
            (
                (named, named_here),
                (holders, holders_here),
                (asked, asked_here),
                (fresh.at[:, :, pl.ds(first, HD)], fresh_here),
            )
        )
    ]
    for copy in copies:
        copy.start()
    sent[...] = jnp.zeros_like(sent)
    for copy in copies:
        copy.wait()
    names = named_here[...]
    slots = holders_here[...].astype(F32)
    for slot in range(RES):
        kept[slot, :HEADS] = asked_here[slot]
        kept[slot, HEADS] = fresh_here[slot]
    groups = []
    for slot in range(RES, SLOTS):
        mine = names == lax.axis_index("group") * SLOTS + slot
        groups.append(jnp.sum(jnp.where(mine, slots, 0.0)).astype(jnp.int32) >> 3)
    for slot, group in zip(range(RES, SLOTS), groups):
        sent[group, :HEADS] = asked_here[slot]
        sent[group, HEADS] = fresh_here[slot]


def split_kernel(moved, resident, *outs):
    y, x = place_of()
    for step, out in enumerate(outs):
        low, half = class_of(*swapped(step, y, x))
        for place, pair in enumerate((2 * low + half, 6 - 2 * low + half)):
            for part in range(2):
                lanes = pl.ds(pl.multiple_of(pair * HD + part * FEATURES, HD), HD)
                columns = slice((part * PAIRS + place) * HD, (part * PAIRS + place + 1) * HD)
                out[:MIG, :, columns] = moved[:, :, lanes]
                out[MIG:, :, columns] = resident[:, :, lanes]


def spread_kernel(origin, arrived, kept, asking):
    for row in range(SLOTS):
        chunk = arrived.at[origin[row]] if row < MIG else kept.at[row - MIG]
        for peer in range(SIDE):
            asking[peer, row * HEADS : (row + 1) * HEADS] = chunk[:HEADS]
            asking[peer, SLOTS * HEADS + row] = chunk[HEADS]


def scores_of(left, right):
    return lax.dot_general(left, right, (((1,), (1,)), ((), ())), preferred_element_type=F32) * SCALE


def partial_kernel(lengths, target, asking, *rest):
    *blocks, payload, scores, weights, stats = rest
    column = lax.broadcasted_iota(jnp.int32, (1, HD), 1)
    block = column // STRIDE
    y, x = swapped(jnp.where(block == 0, 0, (block + 1) % 3 + 1), *place_of())
    position = (y * SIDE + x) * STRIDE + column % STRIDE

    def stored(row, place):
        lanes = slice(place * HD, (place + 1) * HD)
        return jnp.concatenate([block[row, :, lanes] for block in blocks], 0)

    for row in range(SLOTS):
        usable = position < lengths[row]
        span = slice(row * QROWS, (row + 1) * QROWS)
        for pair in range(PAIRS):
            asked = jnp.concatenate([asking[2 * pair, span, :], asking[2 * pair + 1, span, :]], 0)
            found = jnp.where(usable, scores_of(asked, stored(row, pair)), FLOOR)
            scores[2 * pair, span, :] = found[:QROWS]
            scores[2 * pair + 1, span, :] = found[QROWS:]
    lane = lax.broadcasted_iota(jnp.int32, (ROWS, HD), 1)
    table = jnp.zeros((ROWS, HD), F32)
    for peer in range(SIDE):
        found = scores[peer]
        top = jnp.max(found, axis=1, keepdims=True)
        first = top.astype(BF).astype(F32)
        second = (top - first).astype(BF).astype(F32)
        weight = jnp.exp(found - (first + second))
        total = jnp.sum(weight, axis=1, keepdims=True)
        weights[peer] = weight.astype(BF)
        total_first = total.astype(BF).astype(F32)
        for place, value in enumerate((first, total_first, second, total - total_first)):
            table = jnp.where(lane == peer * 8 + place, value, table)
    stats[:ROWS, :] = table
    stats[ROWS:, :] = jnp.zeros((2 * HD - ROWS, HD), F32)
    low = stats[:HD, :].T
    high = stats[HD:, :].T
    for peer in range(SIDE):
        rows = slice(peer * 8, (peer + 1) * 8)
        payload[peer, ROWS:, :] = jnp.concatenate([low[rows], high[rows]], 0).astype(BF)
    for row in range(SLOTS):
        span = slice(row * QROWS, (row + 1) * QROWS)
        for pair in range(PAIRS):
            weight = jnp.concatenate([weights[2 * pair, span, :], weights[2 * pair + 1, span, :]], 0)
            blended = jnp.dot(weight, stored(row, PAIRS + pair), preferred_element_type=F32).astype(BF)
            payload[2 * pair, span, :] = blended[:QROWS]
            payload[2 * pair + 1, span, :] = blended[QROWS:]


def merge_kernel(origin, target, gathered, everyone, sent, kept):
    y, x = place_of()
    first = jnp.where(y > 1, 2, 0)
    asked = everyone[first + x % 2, :ROWS, :]
    keys = everyone[first, ROWS:, :]
    values = everyone[first + 1, ROWS:, :]
    row = lax.broadcasted_iota(jnp.int32, (ROWS, ENTRIES), 0)
    lane = lax.broadcasted_iota(jnp.int32, (ROWS, ENTRIES), 1)
    causal = (lane // STEPS == row // QROWS) & (lane % STEPS <= row % STEPS)
    fresh = jnp.where(causal, scores_of(asked, keys), FLOOR)
    fresh_top = jnp.max(fresh, axis=1, keepdims=True)

    tops = gathered[:, ROWS:, :].astype(F32)
    blank = jnp.zeros((HD - SIDE * 8, HD), F32)
    low = jnp.concatenate([tops[:, :8, :].reshape(SIDE * 8, HD), blank], 0).T
    high = jnp.concatenate([tops[:, 8:, :].reshape(SIDE * 8, HD), blank], 0).T[: ROWS - HD]
    pairs = jnp.concatenate([low, high], 0)
    both = pairs + pltpu.roll(pairs, HD - 2, 1)
    lane = lax.broadcasted_iota(jnp.int32, (ROWS, HD), 1)
    is_top = (lane % 8 == 0) & (lane < SIDE * 8)
    tops = jnp.where(is_top, both, FLOOR)
    sums = pltpu.roll(both, HD - 1, 1)
    highest = jnp.maximum(jnp.max(tops, axis=1, keepdims=True), fresh_top)
    factors = jnp.where(is_top, jnp.exp(tops - highest), 0.0)
    fresh_weights = jnp.where(causal, jnp.exp(fresh - highest), 0.0)
    totals = jnp.sum(jnp.where(is_top, factors * sums, 0.0), axis=1, keepdims=True)
    totals += jnp.sum(fresh_weights, axis=1, keepdims=True)
    blended = jnp.dot(fresh_weights.astype(BF), values, preferred_element_type=F32)
    for peer in range(SIDE):
        blended += factors[:, peer * 8 : peer * 8 + 1] * gathered[peer, :ROWS, :].astype(F32)
    result = (blended / totals).astype(BF)

    sent[...] = jnp.zeros_like(sent)
    for slot in range(MIG):
        sent[listed(origin[slot])] = result[slot * QROWS : (slot + 1) * QROWS]
    for slot in range(RES):
        kept[slot] = result[(MIG + slot) * QROWS : (MIG + slot + 1) * QROWS]


def select_kernel(target, returned, kept, out):
    for slot in range(RES):
        out[slot] = kept[slot]
    for slot in range(MIG):
        out[RES + slot] = returned[listed(target[slot])]


def body(
    queries,
    new_entries,
    resident_cache,
    prefill_cache,
    resident_kept,
    kept_tokens,
    prefill_slot,
    decode_slot,
):
    shape = jax.ShapeDtypeStruct
    whole = [(y, x) for y in range(SIDE) for x in range(SIDE)]
    peers = [[y * SIDE + x for y in (low, 3 - low) for x in (2 * half, 2 * half + 1)] for low in range(2) for half in range(2)]

    turned = [[listed(place) for place in range(GROUPS)]]

    def across(array):
        return lax.all_to_all(array, "tensor", 0, 0, axis_index_groups=peers, tiled=True)

    asked = queries.reshape(SLOTS, STEPS, HEADS, HD).transpose(0, 2, 1, 3)
    sent, kept = call(
        pack_kernel,
        (shape((GROUPS, TILES, STEPS, HD), BF), shape((RES, TILES, STEPS, HD), BF)),
        [HB] * 4,
        scratch=[
            pltpu.VMEM((SLOTS, HEADS, STEPS, HD), BF),
            pltpu.VMEM((SLOTS, STEPS, HD), BF),
            pltpu.VMEM((2, HD), jnp.int32),
            pltpu.VMEM((2, HD), jnp.int32),
            pltpu.SemaphoreType.DMA((4,)),
        ],
        limit=FULL,
    )(decode_slot.reshape(2, HD), prefill_slot.reshape(2, HD), asked, new_entries)
    arrived = lax.all_to_all(sent, "group", 0, 0, tiled=True)

    later = (resident_kept, kept_tokens, prefill_slot, decode_slot)
    later, kept = lax.optimization_barrier((later, kept))
    resident_kept, kept_tokens, prefill_slot, decode_slot = later
    group = lax.axis_index("group")

    def looked_up(names, first, values):
        wanted = first + jnp.arange(MIG, dtype=jnp.int32)
        return jnp.sum(jnp.where(names[None, :] == wanted[:, None], values[None, :], 0), axis=1)

    target = looked_up(decode_slot, group * SLOTS + RES, prefill_slot) // MIG
    origin = looked_up(prefill_slot, group * MIG, decode_slot) // SLOTS
    moved_len = looked_up(prefill_slot, group * MIG, kept_tokens)
    resident_len = lax.dynamic_slice_in_dim(resident_kept, group * RES, RES)
    lengths = jnp.concatenate([moved_len, resident_len])

    split = call(
        split_kernel,
        (shape((SLOTS, STRIDE, 2 * PAIRS * HD), BF),) * SIDE,
        [VM, VM],
        moved=3 * 2**20,
    )(prefill_cache, resident_cache)
    blocks = [split[0]]
    for step in (3, 1, 2):
        steps = []
        for y, x in whole:
            other, side = swapped(step, y, x)
            steps.append((y * SIDE + x, other * SIDE + side))
        blocks.append(lax.ppermute(split[step], "tensor", steps))

    asking = call(
        spread_kernel, shape((SIDE, SLOTS * TILES, STEPS, HD), BF), [SM, VM, VM]
    )(origin, arrived, kept)
    everyone = across(asking).reshape(SIDE, ROWS + ENTRIES, HD)

    payload = call(
        partial_kernel,
        shape((SIDE, PAYLOAD, HD), BF),
        [SM, SM] + [VM] * (1 + SIDE),
        flops=10**8,
        moved=3 * 2**20,
        scratch=[
            pltpu.VMEM((SIDE, ROWS, HD), F32),
            pltpu.VMEM((SIDE, ROWS, HD), BF),
            pltpu.VMEM((2 * HD, HD), F32),
        ],
    )(lengths, target, everyone, *blocks)
    gathered = across(payload)

    finished, here = call(
        merge_kernel,
        (shape((GROUPS, QROWS, HD), BF), shape((RES, QROWS, HD), BF)),
        [SM, SM, VM, VM],
    )(origin, target, gathered, everyone)
    returned = lax.all_to_all(finished, "group", 0, 0, axis_index_groups=turned, tiled=True)

    result = call(select_kernel, shape((SLOTS, QROWS, HD), BF), [SM, VM, VM])(target, returned, here)
    result = result.reshape(SLOTS, HEADS, STEPS, HD).transpose(0, 2, 1, 3)
    return result.reshape(SLOTS, STEPS, HEADS * HD)


def solution(mesh):
    in_specs = (
        P("group", None, "tensor"),
        P("group", None, None),
        P("group", "tensor", None),
        P("group", "tensor", None),
        P(),
        P(),
        P(),
        P(),
    )
    out_specs = P("group", None, "tensor")
    return jax.shard_map(body, mesh=mesh, in_specs=in_specs, out_specs=out_specs, check_vma=False)
```

```python
import math

import jax
import jax.numpy as jnp
from jax import lax
from jax.experimental import pallas as pl
from jax.experimental.pallas import tpu as pltpu
from jax.sharding import PartitionSpec as P

H = 64
KVH = 8
HD = 128
STEPS = 4
MIG = 8
RES = 4
SLOTS = MIG + RES
GROUPS = 32
FIRST_G, STRIDE_G = 16, 15
SHARDS = 16
SIDE = 4
STRIDE = 32
HEADS = H // SHARDS
BLOCKS = 2
PEERS = SHARDS // BLOCKS
PAIRS = PEERS // 2
WIDE = BLOCKS * STRIDE
QROWS = HEADS * STEPS
ROWS = SLOTS * QROWS
FEATURES = KVH * HD
TILES = HEADS + 1
ENTRIES = SLOTS * STEPS
PAYLOAD = ROWS + 16
FLOOR = -(2.0**100)
SCALE = 1.0 / math.sqrt(HD)
LIMIT = 48 * 1024 * 1024
FULL = 60 * 1024 * 1024
BF = jnp.bfloat16
F32 = jnp.float32

VM = pl.BlockSpec(memory_space=pltpu.VMEM)
SM = pl.BlockSpec(memory_space=pltpu.SMEM)
HB = pl.BlockSpec(memory_space=pltpu.HBM)


ANY = pl.BlockSpec(memory_space=pl.ANY)

def call(kernel, outs, specs, flops=0, moved=0, scratch=(), limit=LIMIT, places=None):
    return pl.pallas_call(
        kernel,
        out_shape=outs,
        in_specs=specs,
        out_specs=jax.tree.map(lambda _: VM, outs) if places is None else places,
        scratch_shapes=scratch,
        compiler_params=pltpu.CompilerParams(vmem_limit_bytes=limit),
        cost_estimate=pl.CostEstimate(flops=flops, bytes_accessed=moved, transcendentals=0),
    )


def swapped(step, x):
    return x ^ (step * 3)


def place_of():
    shard = lax.axis_index("tensor")
    return shard // SIDE, shard % SIDE


def listed(group):
    return (group * STRIDE_G + FIRST_G) % GROUPS


def pack_kernel(named, holders, asked, fresh, sent, kept, asked_here, fresh_here, named_here, holders_here, sems):
    shard = lax.axis_index("tensor")
    first = pl.multiple_of(shard % 2 * FEATURES + shard // 2 * HD, HD)
    copies = [
        pltpu.make_async_copy(source, target, sems.at[n])
        for n, (source, target) in enumerate(
            (
                (named, named_here),
                (holders, holders_here),
                (asked, asked_here),
                (fresh.at[:, :, pl.ds(first, HD)], fresh_here),
            )
        )
    ]
    for copy in copies:
        copy.start()
    sent[...] = jnp.zeros_like(sent)
    for copy in copies:
        copy.wait()
    names = named_here[...]
    slots = holders_here[...].astype(F32)
    for slot in range(RES):
        kept[slot, :HEADS] = asked_here[slot]
        kept[slot, HEADS] = fresh_here[slot]
    groups = []
    for slot in range(RES, SLOTS):
        mine = names == lax.axis_index("group") * SLOTS + slot
        groups.append(jnp.sum(jnp.where(mine, slots, 0.0)).astype(jnp.int32) >> 3)
    for slot, group in zip(range(RES, SLOTS), groups):
        sent[listed(group), :HEADS] = asked_here[slot]
        sent[listed(group), HEADS] = fresh_here[slot]


def split_kernel(moved, resident, *outs):
    _, here = place_of()
    for step, out in enumerate(outs):
        half = swapped(step, here) // 2
        for place in range(PAIRS):
            for part in range(2):
                lanes = pl.ds(pl.multiple_of((2 * place + half) * HD + part * FEATURES, HD), HD)
                columns = slice((part * PAIRS + place) * HD, (part * PAIRS + place + 1) * HD)
                out[:MIG, :, columns] = moved[:, :, lanes]
                out[MIG:, :, columns] = resident[:, :, lanes]


def spread_kernel(origin, arrived, kept, asking):
    for row in range(SLOTS):
        chunk = arrived.at[listed(origin[row])] if row < MIG else kept.at[row - MIG]
        for peer in range(PEERS):
            asking[peer, row * HEADS : (row + 1) * HEADS] = chunk[:HEADS]
            asking[peer, SLOTS * HEADS + row] = chunk[HEADS]


def scores_of(left, right):
    return lax.dot_general(left, right, (((1,), (1,)), ((), ())), preferred_element_type=F32) * SCALE


def partial_kernel(lengths, target, asking, *rest):
    *blocks, payload, scores, weights, stats = rest
    y, x = place_of()
    column = lax.broadcasted_iota(jnp.int32, (1, WIDE), 1)
    position = (y * SIDE + swapped(column // STRIDE, x)) * STRIDE + column % STRIDE

    def stored(row, place):
        lanes = slice(place * HD, (place + 1) * HD)
        return jnp.concatenate([block[row, :, lanes] for block in blocks], 0)

    for row in range(SLOTS):
        usable = position < lengths[row]
        span = slice(row * QROWS, (row + 1) * QROWS)
        for pair in range(PAIRS):
            asked = jnp.concatenate([asking[2 * pair, span, :], asking[2 * pair + 1, span, :]], 0)
            found = jnp.where(usable, scores_of(asked, stored(row, pair)), FLOOR)
            scores[2 * pair, span, :] = found[:QROWS]
            scores[2 * pair + 1, span, :] = found[QROWS:]
    lane = lax.broadcasted_iota(jnp.int32, (ROWS, HD), 1)
    table = jnp.zeros((ROWS, HD), F32)
    for peer in range(PEERS):
        found = scores[peer]
        top = jnp.max(found, axis=1, keepdims=True)
        first = top.astype(BF).astype(F32)
        second = (top - first).astype(BF).astype(F32)
        weight = jnp.exp(found - (first + second))
        total = jnp.sum(weight, axis=1, keepdims=True)
        weights[peer] = weight.astype(BF)
        total_first = total.astype(BF).astype(F32)
        for place, value in enumerate((first, total_first, second, total - total_first)):
            table = jnp.where(lane == peer * 8 + place, value, table)
    stats[:ROWS, :] = table
    stats[ROWS:, :] = jnp.zeros((2 * HD - ROWS, HD), F32)
    low = stats[:HD, :].T
    high = stats[HD:, :].T
    for peer in range(PEERS):
        rows = slice(peer * 8, (peer + 1) * 8)
        payload[peer, ROWS:, :] = jnp.concatenate([low[rows], high[rows]], 0).astype(BF)
    for row in range(SLOTS):
        span = slice(row * QROWS, (row + 1) * QROWS)
        for pair in range(PAIRS):
            weight = jnp.concatenate([weights[2 * pair, span, :], weights[2 * pair + 1, span, :]], 0)
            blended = jnp.dot(weight, stored(row, PAIRS + pair), preferred_element_type=F32).astype(BF)
            payload[2 * pair, span, :] = blended[:QROWS]
            payload[2 * pair + 1, span, :] = blended[QROWS:]


def merge_kernel(origin, target, gathered, everyone, sent, kept):
    y, x = place_of()
    first = 2 * y
    asked = everyone[first + x % 2, :ROWS, :]
    keys = everyone[first, ROWS:, :]
    values = everyone[first + 1, ROWS:, :]
    row = lax.broadcasted_iota(jnp.int32, (ROWS, ENTRIES), 0)
    lane = lax.broadcasted_iota(jnp.int32, (ROWS, ENTRIES), 1)
    causal = (lane // STEPS == row // QROWS) & (lane % STEPS <= row % STEPS)
    fresh = jnp.where(causal, scores_of(asked, keys), FLOOR)
    fresh_top = jnp.max(fresh, axis=1, keepdims=True)

    tops = gathered[:, ROWS:, :].astype(F32)
    blank = jnp.zeros((HD - PEERS * 8, HD), F32)
    low = jnp.concatenate([tops[:, :8, :].reshape(PEERS * 8, HD), blank], 0).T
    high = jnp.concatenate([tops[:, 8:, :].reshape(PEERS * 8, HD), blank], 0).T[: ROWS - HD]
    pairs = jnp.concatenate([low, high], 0)
    both = pairs + pltpu.roll(pairs, HD - 2, 1)
    lane = lax.broadcasted_iota(jnp.int32, (ROWS, HD), 1)
    is_top = (lane % 8 == 0) & (lane < PEERS * 8)
    tops = jnp.where(is_top, both, FLOOR)
    sums = pltpu.roll(both, HD - 1, 1)
    highest = jnp.maximum(jnp.max(tops, axis=1, keepdims=True), fresh_top)
    factors = jnp.where(is_top, jnp.exp(tops - highest), 0.0)
    fresh_weights = jnp.where(causal, jnp.exp(fresh - highest), 0.0)
    totals = jnp.sum(jnp.where(is_top, factors * sums, 0.0), axis=1, keepdims=True)
    totals += jnp.sum(fresh_weights, axis=1, keepdims=True)
    blended = jnp.dot(fresh_weights.astype(BF), values, preferred_element_type=F32)
    for peer in range(PEERS):
        blended += factors[:, peer * 8 : peer * 8 + 1] * gathered[peer, :ROWS, :].astype(F32)
    result = (blended / totals).astype(BF)

    sent[...] = jnp.zeros_like(sent)
    for slot in range(MIG):
        sent[listed(origin[slot])] = result[slot * QROWS : (slot + 1) * QROWS]
    for slot in range(RES):
        kept[slot] = result[(MIG + slot) * QROWS : (MIG + slot + 1) * QROWS]


def select_kernel(target, returned, kept, out):
    for slot in range(RES):
        out[slot] = kept[slot]
    for slot in range(MIG):
        out[RES + slot] = returned[listed(target[slot])]


def body(
    queries,
    new_entries,
    resident_cache,
    prefill_cache,
    resident_kept,
    kept_tokens,
    prefill_slot,
    decode_slot,
):
    shape = jax.ShapeDtypeStruct
    peers = [[y * SIDE + 2 * half + x for y in range(SIDE) for x in range(2)] for half in range(2)]
    turned = [[listed(place) for place in range(GROUPS)]]

    def around(array):
        return lax.all_to_all(array, "group", 0, 0, axis_index_groups=turned, tiled=True)

    def across(array):
        return lax.all_to_all(array, "tensor", 0, 0, axis_index_groups=peers, tiled=True)

    asked = queries.reshape(SLOTS, STEPS, HEADS, HD).transpose(0, 2, 1, 3)
    sent, kept = call(
        pack_kernel,
        (shape((GROUPS, TILES, STEPS, HD), BF), shape((RES, TILES, STEPS, HD), BF)),
        [HB] * 4,
        scratch=[
            pltpu.VMEM((SLOTS, HEADS, STEPS, HD), BF),
            pltpu.VMEM((SLOTS, STEPS, HD), BF),
            pltpu.VMEM((2, HD), jnp.int32),
            pltpu.VMEM((2, HD), jnp.int32),
            pltpu.SemaphoreType.DMA((4,)),
        ],
        limit=FULL,
    )(decode_slot.reshape(2, HD), prefill_slot.reshape(2, HD), asked, new_entries)
    arrived = around(sent)

    later = (resident_kept, kept_tokens, prefill_slot, decode_slot)
    later, kept = lax.optimization_barrier((later, kept))
    resident_kept, kept_tokens, prefill_slot, decode_slot = later
    group = lax.axis_index("group")

    def looked_up(names, first, values):
        wanted = first + jnp.arange(MIG, dtype=jnp.int32)
        return jnp.sum(jnp.where(names[None, :] == wanted[:, None], values[None, :], 0), axis=1)

    target = looked_up(decode_slot, group * SLOTS + RES, prefill_slot) // MIG
    origin = looked_up(prefill_slot, group * MIG, decode_slot) // SLOTS
    moved_len = looked_up(prefill_slot, group * MIG, kept_tokens)
    resident_len = lax.dynamic_slice_in_dim(resident_kept, group * RES, RES)
    lengths = jnp.concatenate([moved_len, resident_len])

    split = call(
        split_kernel,
        (shape((SLOTS, STRIDE, 2 * PAIRS * HD), BF),) * BLOCKS,
        [VM, VM],
        moved=3 * 2**20,
    )(prefill_cache, resident_cache)
    blocks = [split[0]]
    for step in range(1, BLOCKS):
        steps = [(t, t // SIDE * SIDE + swapped(step, t % SIDE)) for t in range(SHARDS)]
        blocks.append(lax.ppermute(split[step], "tensor", steps))

    asking = call(
        spread_kernel, shape((PEERS, SLOTS * TILES, STEPS, HD), BF), [SM, VM, VM]
    )(origin, arrived, kept)
    everyone = across(asking).reshape(PEERS, ROWS + ENTRIES, HD)

    payload = call(
        partial_kernel,
        shape((PEERS, PAYLOAD, HD), BF),
        [SM, SM] + [VM] * (1 + BLOCKS),
        flops=10**8,
        moved=3 * 2**20,
        scratch=[
            pltpu.VMEM((PEERS, ROWS, WIDE), F32),
            pltpu.VMEM((PEERS, ROWS, WIDE), BF),
            pltpu.VMEM((2 * HD, HD), F32),
        ],
    )(lengths, target, everyone, *blocks)
    gathered = across(payload)

    finished, here = call(
        merge_kernel,
        (shape((GROUPS, QROWS, HD), BF), shape((RES, QROWS, HD), BF)),
        [SM, SM, VM, VM],
    )(origin, target, gathered, everyone)
    returned = around(finished)

    result = call(select_kernel, shape((SLOTS, QROWS, HD), BF), [SM, VM, VM])(target, returned, here)
    result = result.reshape(SLOTS, HEADS, STEPS, HD).transpose(0, 2, 1, 3)
    return result.reshape(SLOTS, STEPS, HEADS * HD)


def solution(mesh):
    in_specs = (
        P("group", None, "tensor"),
        P("group", None, None),
        P("group", "tensor", None),
        P("group", "tensor", None),
        P(),
        P(),
        P(),
        P(),
    )
    out_specs = P("group", None, "tensor")
    return jax.shard_map(body, mesh=mesh, in_specs=in_specs, out_specs=out_specs, check_vma=False)
```

```python
import math

import jax
import jax.numpy as jnp
from jax import lax
from jax.experimental import pallas as pl
from jax.experimental.pallas import tpu as pltpu
from jax.sharding import PartitionSpec as P

H = 64
KVH = 8
HD = 128
STEPS = 4
MIG = 8
RES = 4
SLOTS = MIG + RES
GROUPS = 32
FIRST_G, STRIDE_G = 16, 15
SHARDS = 16
SIDE = 4
STRIDE = 32
HEADS = H // SHARDS
PAIRS = KVH // SIDE
QROWS = HEADS * STEPS
ROWS = SLOTS * QROWS
FEATURES = KVH * HD
TILES = HEADS + 1
ENTRIES = SLOTS * STEPS
PAYLOAD = ROWS + 16
FLOOR = -(2.0**100)
SCALE = 1.0 / math.sqrt(HD)
LIMIT = 48 * 1024 * 1024
FULL = 60 * 1024 * 1024
BF = jnp.bfloat16
F32 = jnp.float32

VM = pl.BlockSpec(memory_space=pltpu.VMEM)
SM = pl.BlockSpec(memory_space=pltpu.SMEM)
HB = pl.BlockSpec(memory_space=pltpu.HBM)


ANY = pl.BlockSpec(memory_space=pl.ANY)

def call(kernel, outs, specs, flops=0, moved=0, scratch=(), limit=LIMIT, places=None):
    return pl.pallas_call(
        kernel,
        out_shape=outs,
        in_specs=specs,
        out_specs=jax.tree.map(lambda _: VM, outs) if places is None else places,
        scratch_shapes=scratch,
        compiler_params=pltpu.CompilerParams(vmem_limit_bytes=limit),
        cost_estimate=pl.CostEstimate(flops=flops, bytes_accessed=moved, transcendentals=0),
    )


def shifted(y, step):
    return (y + step) & (SIDE - 1)


def place_of():
    shard = lax.axis_index("tensor")
    return shard // SIDE, shard % SIDE


def listed(group):
    return (group * STRIDE_G + FIRST_G) % GROUPS


def pack_kernel(named, holders, asked, fresh, sent, kept, asked_here, fresh_here, named_here, holders_here, sems):
    shard = lax.axis_index("tensor")
    first = pl.multiple_of(shard % 2 * FEATURES + shard // 2 * HD, HD)
    copies = [
        pltpu.make_async_copy(source, target, sems.at[n])
        for n, (source, target) in enumerate(
            (
                (named, named_here),
                (holders, holders_here),
                (asked, asked_here),
                (fresh.at[:, :, pl.ds(first, HD)], fresh_here),
            )
        )
    ]
    for copy in copies:
        copy.start()
    sent[...] = jnp.zeros_like(sent)
    for copy in copies:
        copy.wait()
    names = named_here[...]
    slots = holders_here[...].astype(F32)
    for slot in range(RES):
        kept[slot, :HEADS] = asked_here[slot]
        kept[slot, HEADS] = fresh_here[slot]
    groups = []
    for slot in range(RES, SLOTS):
        mine = names == lax.axis_index("group") * SLOTS + slot
        groups.append(jnp.sum(jnp.where(mine, slots, 0.0)).astype(jnp.int32) >> 3)
    for slot, group in zip(range(RES, SLOTS), groups):
        sent[listed(group), :HEADS] = asked_here[slot]
        sent[listed(group), HEADS] = fresh_here[slot]


def split_kernel(moved, resident, *outs):
    y, _ = place_of()
    for step, out in enumerate(outs):
        for part in range(2):
            first = shifted(y, step) * PAIRS * HD + part * FEATURES
            lanes = pl.ds(pl.multiple_of(first, PAIRS * HD), PAIRS * HD)
            columns = slice(part * PAIRS * HD, (part + 1) * PAIRS * HD)
            out[:MIG, :, columns] = moved[:, :, lanes]
            out[MIG:, :, columns] = resident[:, :, lanes]


def spread_kernel(origin, arrived, kept, asking):
    for row in range(SLOTS):
        chunk = arrived.at[listed(origin[row])] if row < MIG else kept.at[row - MIG]
        for peer in range(SIDE):
            asking[peer, row * HEADS : (row + 1) * HEADS] = chunk[:HEADS]
            asking[peer, SLOTS * HEADS + row] = chunk[HEADS]


def scores_of(left, right):
    return lax.dot_general(left, right, (((1,), (1,)), ((), ())), preferred_element_type=F32) * SCALE


def partial_kernel(lengths, target, asking, *rest):
    *blocks, payload, scores, weights, stats = rest
    column = lax.broadcasted_iota(jnp.int32, (1, HD), 1)
    block = column // STRIDE
    y, x = place_of()
    y = shifted(y, -jnp.where((block == 1) | (block == 2), 3 - block, block))
    position = (y * SIDE + x) * STRIDE + column % STRIDE

    def stored(row, place):
        lanes = slice(place * HD, (place + 1) * HD)
        return jnp.concatenate([block[row, :, lanes] for block in blocks], 0)

    for row in range(SLOTS):
        usable = position < lengths[row]
        span = slice(row * QROWS, (row + 1) * QROWS)
        for pair in range(PAIRS):
            asked = jnp.concatenate([asking[2 * pair, span, :], asking[2 * pair + 1, span, :]], 0)
            found = jnp.where(usable, scores_of(asked, stored(row, pair)), FLOOR)
            scores[2 * pair, span, :] = found[:QROWS]
            scores[2 * pair + 1, span, :] = found[QROWS:]
    lane = lax.broadcasted_iota(jnp.int32, (ROWS, HD), 1)
    table = jnp.zeros((ROWS, HD), F32)
    for peer in range(SIDE):
        found = scores[peer]
        top = jnp.max(found, axis=1, keepdims=True)
        first = top.astype(BF).astype(F32)
        second = (top - first).astype(BF).astype(F32)
        weight = jnp.exp(found - (first + second))
        total = jnp.sum(weight, axis=1, keepdims=True)
        weights[peer] = weight.astype(BF)
        total_first = total.astype(BF).astype(F32)
        for place, value in enumerate((first, total_first, second, total - total_first)):
            table = jnp.where(lane == peer * 8 + place, value, table)
    stats[:ROWS, :] = table
    stats[ROWS:, :] = jnp.zeros((2 * HD - ROWS, HD), F32)
    low = stats[:HD, :].T
    high = stats[HD:, :].T
    for peer in range(SIDE):
        rows = slice(peer * 8, (peer + 1) * 8)
        payload[peer, ROWS:, :] = jnp.concatenate([low[rows], high[rows]], 0).astype(BF)
    for row in range(SLOTS):
        span = slice(row * QROWS, (row + 1) * QROWS)
        for pair in range(PAIRS):
            weight = jnp.concatenate([weights[2 * pair, span, :], weights[2 * pair + 1, span, :]], 0)
            blended = jnp.dot(weight, stored(row, PAIRS + pair), preferred_element_type=F32).astype(BF)
            payload[2 * pair, span, :] = blended[:QROWS]
            payload[2 * pair + 1, span, :] = blended[QROWS:]


def merge_kernel(origin, target, gathered, everyone, sent, kept):
    _, x = place_of()
    first = x // 2 * 2
    asked = everyone[first + x % 2, :ROWS, :]
    keys = everyone[first, ROWS:, :]
    values = everyone[first + 1, ROWS:, :]
    row = lax.broadcasted_iota(jnp.int32, (ROWS, ENTRIES), 0)
    lane = lax.broadcasted_iota(jnp.int32, (ROWS, ENTRIES), 1)
    causal = (lane // STEPS == row // QROWS) & (lane % STEPS <= row % STEPS)
    fresh = jnp.where(causal, scores_of(asked, keys), FLOOR)
    fresh_top = jnp.max(fresh, axis=1, keepdims=True)

    tops = gathered[:, ROWS:, :].astype(F32)
    blank = jnp.zeros((HD - SIDE * 8, HD), F32)
    low = jnp.concatenate([tops[:, :8, :].reshape(SIDE * 8, HD), blank], 0).T
    high = jnp.concatenate([tops[:, 8:, :].reshape(SIDE * 8, HD), blank], 0).T[: ROWS - HD]
    pairs = jnp.concatenate([low, high], 0)
    both = pairs + pltpu.roll(pairs, HD - 2, 1)
    lane = lax.broadcasted_iota(jnp.int32, (ROWS, HD), 1)
    is_top = (lane % 8 == 0) & (lane < SIDE * 8)
    tops = jnp.where(is_top, both, FLOOR)
    sums = pltpu.roll(both, HD - 1, 1)
    highest = jnp.maximum(jnp.max(tops, axis=1, keepdims=True), fresh_top)
    factors = jnp.where(is_top, jnp.exp(tops - highest), 0.0)
    fresh_weights = jnp.where(causal, jnp.exp(fresh - highest), 0.0)
    totals = jnp.sum(jnp.where(is_top, factors * sums, 0.0), axis=1, keepdims=True)
    totals += jnp.sum(fresh_weights, axis=1, keepdims=True)
    blended = jnp.dot(fresh_weights.astype(BF), values, preferred_element_type=F32)
    for peer in range(SIDE):
        blended += factors[:, peer * 8 : peer * 8 + 1] * gathered[peer, :ROWS, :].astype(F32)
    result = (blended / totals).astype(BF)

    sent[...] = jnp.zeros_like(sent)
    for slot in range(MIG):
        sent[listed(origin[slot])] = result[slot * QROWS : (slot + 1) * QROWS]
    for slot in range(RES):
        kept[slot] = result[(MIG + slot) * QROWS : (MIG + slot + 1) * QROWS]


def select_kernel(target, returned, kept, out):
    for slot in range(RES):
        out[slot] = kept[slot]
    for slot in range(MIG):
        out[RES + slot] = returned[listed(target[slot])]


def body(
    queries,
    new_entries,
    resident_cache,
    prefill_cache,
    resident_kept,
    kept_tokens,
    prefill_slot,
    decode_slot,
):
    shape = jax.ShapeDtypeStruct
    peers = [[y * SIDE + x for x in range(SIDE)] for y in range(SIDE)]
    turned = [[listed(place) for place in range(GROUPS)]]

    def around(array):
        return lax.all_to_all(array, "group", 0, 0, axis_index_groups=turned, tiled=True)

    def across(array):
        return lax.all_to_all(array, "tensor", 0, 0, axis_index_groups=peers, tiled=True)

    asked = queries.reshape(SLOTS, STEPS, HEADS, HD).transpose(0, 2, 1, 3)
    sent, kept = call(
        pack_kernel,
        (shape((GROUPS, TILES, STEPS, HD), BF), shape((RES, TILES, STEPS, HD), BF)),
        [HB] * 4,
        scratch=[
            pltpu.VMEM((SLOTS, HEADS, STEPS, HD), BF),
            pltpu.VMEM((SLOTS, STEPS, HD), BF),
            pltpu.VMEM((2, HD), jnp.int32),
            pltpu.VMEM((2, HD), jnp.int32),
            pltpu.SemaphoreType.DMA((4,)),
        ],
        limit=FULL,
    )(decode_slot.reshape(2, HD), prefill_slot.reshape(2, HD), asked, new_entries)
    arrived = around(sent)

    later = (resident_kept, kept_tokens, prefill_slot, decode_slot)
    later, kept = lax.optimization_barrier((later, kept))
    resident_kept, kept_tokens, prefill_slot, decode_slot = later
    group = lax.axis_index("group")

    def looked_up(names, first, values):
        wanted = first + jnp.arange(MIG, dtype=jnp.int32)
        return jnp.sum(jnp.where(names[None, :] == wanted[:, None], values[None, :], 0), axis=1)

    target = looked_up(decode_slot, group * SLOTS + RES, prefill_slot) // MIG
    origin = looked_up(prefill_slot, group * MIG, decode_slot) // SLOTS
    moved_len = looked_up(prefill_slot, group * MIG, kept_tokens)
    resident_len = lax.dynamic_slice_in_dim(resident_kept, group * RES, RES)
    lengths = jnp.concatenate([moved_len, resident_len])

    split = call(
        split_kernel,
        (shape((SLOTS, STRIDE, 2 * PAIRS * HD), BF),) * SIDE,
        [VM, VM],
        moved=3 * 2**20,
    )(prefill_cache, resident_cache)
    blocks = [split[0]]
    for step in (2, 1, 3):
        steps = [(t, (t + step * SIDE) % SHARDS) for t in range(SHARDS)]
        blocks.append(lax.ppermute(split[step], "tensor", steps))

    asking = call(
        spread_kernel, shape((SIDE, SLOTS * TILES, STEPS, HD), BF), [SM, VM, VM]
    )(origin, arrived, kept)
    everyone = across(asking).reshape(SIDE, ROWS + ENTRIES, HD)

    payload = call(
        partial_kernel,
        shape((SIDE, PAYLOAD, HD), BF),
        [SM, SM] + [VM] * (1 + SIDE),
        flops=10**8,
        moved=3 * 2**20,
        scratch=[
            pltpu.VMEM((SIDE, ROWS, HD), F32),
            pltpu.VMEM((SIDE, ROWS, HD), BF),
            pltpu.VMEM((2 * HD, HD), F32),
        ],
    )(lengths, target, everyone, *blocks)
    gathered = across(payload)

    finished, here = call(
        merge_kernel,
        (shape((GROUPS, QROWS, HD), BF), shape((RES, QROWS, HD), BF)),
        [SM, SM, VM, VM],
    )(origin, target, gathered, everyone)
    returned = around(finished)

    result = call(select_kernel, shape((SLOTS, QROWS, HD), BF), [SM, VM, VM])(target, returned, here)
    result = result.reshape(SLOTS, HEADS, STEPS, HD).transpose(0, 2, 1, 3)
    return result.reshape(SLOTS, STEPS, HEADS * HD)


def solution(mesh):
    in_specs = (
        P("group", None, "tensor"),
        P("group", None, None),
        P("group", "tensor", None),
        P("group", "tensor", None),
        P(),
        P(),
        P(),
        P(),
    )
    out_specs = P("group", None, "tensor")
    return jax.shard_map(body, mesh=mesh, in_specs=in_specs, out_specs=out_specs, check_vma=False)
```

```python
import math

import jax
import jax.numpy as jnp
from jax import lax
from jax.experimental import pallas as pl
from jax.experimental.pallas import tpu as pltpu
from jax.sharding import PartitionSpec as P

H = 64
KVH = 8
HD = 128
STEPS = 4
MIG = 8
RES = 4
SLOTS = MIG + RES
GROUPS = 32
FIRST_G, STRIDE_G = 16, 15
SHARDS = 16
SIDE = 4
STRIDE = 32
HEADS = H // SHARDS
PAIRS = KVH // SIDE
QROWS = HEADS * STEPS
ROWS = SLOTS * QROWS
FEATURES = KVH * HD
TILES = HEADS + 1
ENTRIES = SLOTS * STEPS
PAYLOAD = ROWS + 16
FLOOR = -(2.0**100)
SCALE = 1.0 / math.sqrt(HD)
LIMIT = 48 * 1024 * 1024
FULL = 60 * 1024 * 1024
BF = jnp.bfloat16
F32 = jnp.float32

VM = pl.BlockSpec(memory_space=pltpu.VMEM)
SM = pl.BlockSpec(memory_space=pltpu.SMEM)
HB = pl.BlockSpec(memory_space=pltpu.HBM)


ANY = pl.BlockSpec(memory_space=pl.ANY)

def call(kernel, outs, specs, flops=0, moved=0, scratch=(), limit=LIMIT, places=None):
    return pl.pallas_call(
        kernel,
        out_shape=outs,
        in_specs=specs,
        out_specs=jax.tree.map(lambda _: VM, outs) if places is None else places,
        scratch_shapes=scratch,
        compiler_params=pltpu.CompilerParams(vmem_limit_bytes=limit),
        cost_estimate=pl.CostEstimate(flops=flops, bytes_accessed=moved, transcendentals=0),
    )


def shifted(y, step):
    return (y + step) & (SIDE - 1)


def place_of():
    shard = lax.axis_index("tensor")
    return shard // SIDE, shard % SIDE


def listed(group):
    return (group * STRIDE_G + FIRST_G) % GROUPS


def pack_kernel(named, holders, asked, fresh, sent, kept, asked_here, fresh_here, named_here, holders_here, sems):
    shard = lax.axis_index("tensor")
    first = pl.multiple_of(shard % 2 * FEATURES + shard // 2 * HD, HD)
    copies = [
        pltpu.make_async_copy(source, target, sems.at[n])
        for n, (source, target) in enumerate(
            (
                (named, named_here),
                (holders, holders_here),
                (asked, asked_here),
                (fresh.at[:, :, pl.ds(first, HD)], fresh_here),
            )
        )
    ]
    for copy in copies:
        copy.start()
    sent[...] = jnp.zeros_like(sent)
    for copy in copies:
        copy.wait()
    names = named_here[...]
    slots = holders_here[...].astype(F32)
    for slot in range(RES):
        kept[slot, :HEADS] = asked_here[slot]
        kept[slot, HEADS] = fresh_here[slot]
    groups = []
    for slot in range(RES, SLOTS):
        mine = names == lax.axis_index("group") * SLOTS + slot
        groups.append(jnp.sum(jnp.where(mine, slots, 0.0)).astype(jnp.int32) >> 3)
    for slot, group in zip(range(RES, SLOTS), groups):
        sent[listed(group), :HEADS] = asked_here[slot]
        sent[listed(group), HEADS] = fresh_here[slot]


def split_kernel(moved, resident, *outs):
    y, _ = place_of()
    for step, out in enumerate(outs):
        for part in range(2):
            first = shifted(y, step) * PAIRS * HD + part * FEATURES
            lanes = pl.ds(pl.multiple_of(first, PAIRS * HD), PAIRS * HD)
            columns = slice(part * PAIRS * HD, (part + 1) * PAIRS * HD)
            out[:MIG, :, columns] = moved[:, :, lanes]
            out[MIG:, :, columns] = resident[:, :, lanes]


def spread_kernel(origin, arrived, kept, asking):
    for row in range(SLOTS):
        chunk = arrived.at[listed(origin[row])] if row < MIG else kept.at[row - MIG]
        for peer in range(SIDE):
            asking[peer, row * HEADS : (row + 1) * HEADS] = chunk[:HEADS]
            asking[peer, SLOTS * HEADS + row] = chunk[HEADS]


def scores_of(left, right):
    return lax.dot_general(left, right, (((1,), (1,)), ((), ())), preferred_element_type=F32) * SCALE


def partial_kernel(lengths, target, asking, *rest):
    *blocks, payload, scores, weights, stats = rest
    column = lax.broadcasted_iota(jnp.int32, (1, HD), 1)
    block = column // STRIDE
    y, x = place_of()
    y = shifted(y, -jnp.where(block > 1, 5 - block, block))
    position = (y * SIDE + x) * STRIDE + column % STRIDE

    def stored(row, place):
        lanes = slice(place * HD, (place + 1) * HD)
        return jnp.concatenate([block[row, :, lanes] for block in blocks], 0)

    for row in range(SLOTS):
        usable = position < lengths[row]
        span = slice(row * QROWS, (row + 1) * QROWS)
        for pair in range(PAIRS):
            asked = jnp.concatenate([asking[2 * pair, span, :], asking[2 * pair + 1, span, :]], 0)
            found = jnp.where(usable, scores_of(asked, stored(row, pair)), FLOOR)
            scores[2 * pair, span, :] = found[:QROWS]
            scores[2 * pair + 1, span, :] = found[QROWS:]
    lane = lax.broadcasted_iota(jnp.int32, (ROWS, HD), 1)
    table = jnp.zeros((ROWS, HD), F32)
    for peer in range(SIDE):
        found = scores[peer]
        top = jnp.max(found, axis=1, keepdims=True)
        first = top.astype(BF).astype(F32)
        second = (top - first).astype(BF).astype(F32)
        weight = jnp.exp(found - (first + second))
        total = jnp.sum(weight, axis=1, keepdims=True)
        weights[peer] = weight.astype(BF)
        total_first = total.astype(BF).astype(F32)
        for place, value in enumerate((first, total_first, second, total - total_first)):
            table = jnp.where(lane == peer * 8 + place, value, table)
    stats[:ROWS, :] = table
    stats[ROWS:, :] = jnp.zeros((2 * HD - ROWS, HD), F32)
    low = stats[:HD, :].T
    high = stats[HD:, :].T
    for peer in range(SIDE):
        rows = slice(peer * 8, (peer + 1) * 8)
        payload[peer, ROWS:, :] = jnp.concatenate([low[rows], high[rows]], 0).astype(BF)
    for row in range(SLOTS):
        span = slice(row * QROWS, (row + 1) * QROWS)
        for pair in range(PAIRS):
            weight = jnp.concatenate([weights[2 * pair, span, :], weights[2 * pair + 1, span, :]], 0)
            blended = jnp.dot(weight, stored(row, PAIRS + pair), preferred_element_type=F32).astype(BF)
            payload[2 * pair, span, :] = blended[:QROWS]
            payload[2 * pair + 1, span, :] = blended[QROWS:]


def merge_kernel(origin, target, gathered, everyone, sent, kept):
    _, x = place_of()
    first = x // 2 * 2
    asked = everyone[first + x % 2, :ROWS, :]
    keys = everyone[first, ROWS:, :]
    values = everyone[first + 1, ROWS:, :]
    row = lax.broadcasted_iota(jnp.int32, (ROWS, ENTRIES), 0)
    lane = lax.broadcasted_iota(jnp.int32, (ROWS, ENTRIES), 1)
    causal = (lane // STEPS == row // QROWS) & (lane % STEPS <= row % STEPS)
    fresh = jnp.where(causal, scores_of(asked, keys), FLOOR)
    fresh_top = jnp.max(fresh, axis=1, keepdims=True)

    tops = gathered[:, ROWS:, :].astype(F32)
    blank = jnp.zeros((HD - SIDE * 8, HD), F32)
    low = jnp.concatenate([tops[:, :8, :].reshape(SIDE * 8, HD), blank], 0).T
    high = jnp.concatenate([tops[:, 8:, :].reshape(SIDE * 8, HD), blank], 0).T[: ROWS - HD]
    pairs = jnp.concatenate([low, high], 0)
    both = pairs + pltpu.roll(pairs, HD - 2, 1)
    lane = lax.broadcasted_iota(jnp.int32, (ROWS, HD), 1)
    is_top = (lane % 8 == 0) & (lane < SIDE * 8)
    tops = jnp.where(is_top, both, FLOOR)
    sums = pltpu.roll(both, HD - 1, 1)
    highest = jnp.maximum(jnp.max(tops, axis=1, keepdims=True), fresh_top)
    factors = jnp.where(is_top, jnp.exp(tops - highest), 0.0)
    fresh_weights = jnp.where(causal, jnp.exp(fresh - highest), 0.0)
    totals = jnp.sum(jnp.where(is_top, factors * sums, 0.0), axis=1, keepdims=True)
    totals += jnp.sum(fresh_weights, axis=1, keepdims=True)
    blended = jnp.dot(fresh_weights.astype(BF), values, preferred_element_type=F32)
    for peer in range(SIDE):
        blended += factors[:, peer * 8 : peer * 8 + 1] * gathered[peer, :ROWS, :].astype(F32)
    result = (blended / totals).astype(BF)

    sent[...] = jnp.zeros_like(sent)
    for slot in range(MIG):
        sent[listed(origin[slot])] = result[slot * QROWS : (slot + 1) * QROWS]
    for slot in range(RES):
        kept[slot] = result[(MIG + slot) * QROWS : (MIG + slot + 1) * QROWS]


def select_kernel(target, returned, kept, out):
    for slot in range(RES):
        out[slot] = kept[slot]
    for slot in range(MIG):
        out[RES + slot] = returned[listed(target[slot])]


def body(
    queries,
    new_entries,
    resident_cache,
    prefill_cache,
    resident_kept,
    kept_tokens,
    prefill_slot,
    decode_slot,
):
    shape = jax.ShapeDtypeStruct
    peers = [[y * SIDE + x for x in range(SIDE)] for y in range(SIDE)]
    turned = [[listed(place) for place in range(GROUPS)]]

    def around(array):
        return lax.all_to_all(array, "group", 0, 0, axis_index_groups=turned, tiled=True)

    def across(array):
        return lax.all_to_all(array, "tensor", 0, 0, axis_index_groups=peers, tiled=True)

    asked = queries.reshape(SLOTS, STEPS, HEADS, HD).transpose(0, 2, 1, 3)
    sent, kept = call(
        pack_kernel,
        (shape((GROUPS, TILES, STEPS, HD), BF), shape((RES, TILES, STEPS, HD), BF)),
        [HB] * 4,
        scratch=[
            pltpu.VMEM((SLOTS, HEADS, STEPS, HD), BF),
            pltpu.VMEM((SLOTS, STEPS, HD), BF),
            pltpu.VMEM((2, HD), jnp.int32),
            pltpu.VMEM((2, HD), jnp.int32),
            pltpu.SemaphoreType.DMA((4,)),
        ],
        limit=FULL,
    )(decode_slot.reshape(2, HD), prefill_slot.reshape(2, HD), asked, new_entries)
    arrived = around(sent)

    later = (resident_kept, kept_tokens, prefill_slot, decode_slot)
    later, kept = lax.optimization_barrier((later, kept))
    resident_kept, kept_tokens, prefill_slot, decode_slot = later
    group = lax.axis_index("group")

    def looked_up(names, first, values):
        wanted = first + jnp.arange(MIG, dtype=jnp.int32)
        return jnp.sum(jnp.where(names[None, :] == wanted[:, None], values[None, :], 0), axis=1)

    target = looked_up(decode_slot, group * SLOTS + RES, prefill_slot) // MIG
    origin = looked_up(prefill_slot, group * MIG, decode_slot) // SLOTS
    moved_len = looked_up(prefill_slot, group * MIG, kept_tokens)
    resident_len = lax.dynamic_slice_in_dim(resident_kept, group * RES, RES)
    lengths = jnp.concatenate([moved_len, resident_len])

    split = call(
        split_kernel,
        (shape((SLOTS, STRIDE, 2 * PAIRS * HD), BF),) * SIDE,
        [VM, VM],
        moved=3 * 2**20,
    )(prefill_cache, resident_cache)
    blocks = [split[0]]
    for step in (1, 3, 2):
        steps = [(t, (t + step * SIDE) % SHARDS) for t in range(SHARDS)]
        blocks.append(lax.ppermute(split[step], "tensor", steps))

    asking = call(
        spread_kernel, shape((SIDE, SLOTS * TILES, STEPS, HD), BF), [SM, VM, VM]
    )(origin, arrived, kept)
    everyone = across(asking).reshape(SIDE, ROWS + ENTRIES, HD)

    payload = call(
        partial_kernel,
        shape((SIDE, PAYLOAD, HD), BF),
        [SM, SM] + [VM] * (1 + SIDE),
        flops=10**8,
        moved=3 * 2**20,
        scratch=[
            pltpu.VMEM((SIDE, ROWS, HD), F32),
            pltpu.VMEM((SIDE, ROWS, HD), BF),
            pltpu.VMEM((2 * HD, HD), F32),
        ],
    )(lengths, target, everyone, *blocks)
    gathered = across(payload)

    finished, here = call(
        merge_kernel,
        (shape((GROUPS, QROWS, HD), BF), shape((RES, QROWS, HD), BF)),
        [SM, SM, VM, VM],
    )(origin, target, gathered, everyone)
    returned = around(finished)

    result = call(select_kernel, shape((SLOTS, QROWS, HD), BF), [SM, VM, VM])(target, returned, here)
    result = result.reshape(SLOTS, HEADS, STEPS, HD).transpose(0, 2, 1, 3)
    return result.reshape(SLOTS, STEPS, HEADS * HD)


def solution(mesh):
    in_specs = (
        P("group", None, "tensor"),
        P("group", None, None),
        P("group", "tensor", None),
        P("group", "tensor", None),
        P(),
        P(),
        P(),
        P(),
    )
    out_specs = P("group", None, "tensor")
    return jax.shard_map(body, mesh=mesh, in_specs=in_specs, out_specs=out_specs, check_vma=False)
```

```python
import math

import jax
import jax.numpy as jnp
from jax import lax
from jax.experimental import pallas as pl
from jax.experimental.pallas import tpu as pltpu
from jax.sharding import PartitionSpec as P

H = 64
KVH = 8
HD = 128
STEPS = 4
MIG = 8
RES = 4
SLOTS = MIG + RES
GROUPS = 32
FIRST_G, STRIDE_G = 16, 15
SHARDS = 16
SIDE = 4
STRIDE = 32
HEADS = H // SHARDS
PAIRS = KVH // SIDE
QROWS = HEADS * STEPS
ROWS = SLOTS * QROWS
FEATURES = KVH * HD
TILES = HEADS + 1
ENTRIES = SLOTS * STEPS
PAYLOAD = ROWS + 16
FLOOR = -(2.0**100)
SCALE = 1.0 / math.sqrt(HD)
LIMIT = 48 * 1024 * 1024
FULL = 60 * 1024 * 1024
BF = jnp.bfloat16
F32 = jnp.float32

VM = pl.BlockSpec(memory_space=pltpu.VMEM)
SM = pl.BlockSpec(memory_space=pltpu.SMEM)
HB = pl.BlockSpec(memory_space=pltpu.HBM)


ANY = pl.BlockSpec(memory_space=pl.ANY)

def call(kernel, outs, specs, flops=0, moved=0, scratch=(), limit=LIMIT, places=None):
    return pl.pallas_call(
        kernel,
        out_shape=outs,
        in_specs=specs,
        out_specs=jax.tree.map(lambda _: VM, outs) if places is None else places,
        scratch_shapes=scratch,
        compiler_params=pltpu.CompilerParams(vmem_limit_bytes=limit),
        cost_estimate=pl.CostEstimate(flops=flops, bytes_accessed=moved, transcendentals=0),
    )


def shifted(y, step):
    return (y + step) & (SIDE - 1)


def place_of():
    shard = lax.axis_index("tensor")
    return shard // SIDE, shard % SIDE


def listed(group):
    return (group * STRIDE_G + FIRST_G) % GROUPS


def pack_kernel(named, holders, asked, fresh, sent, kept, asked_here, fresh_here, named_here, holders_here, sems):
    shard = lax.axis_index("tensor")
    first = pl.multiple_of(shard % 2 * FEATURES + shard // 2 * HD, HD)
    copies = [
        pltpu.make_async_copy(source, target, sems.at[n])
        for n, (source, target) in enumerate(
            (
                (named, named_here),
                (holders, holders_here),
                (asked, asked_here),
                (fresh.at[:, :, pl.ds(first, HD)], fresh_here),
            )
        )
    ]
    for copy in copies:
        copy.start()
    sent[...] = jnp.zeros_like(sent)
    for copy in copies:
        copy.wait()
    names = named_here[...]
    slots = holders_here[...].astype(F32)
    for slot in range(RES):
        kept[slot, :HEADS] = asked_here[slot]
        kept[slot, HEADS] = fresh_here[slot]
    groups = []
    for slot in range(RES, SLOTS):
        mine = names == lax.axis_index("group") * SLOTS + slot
        groups.append(jnp.sum(jnp.where(mine, slots, 0.0)).astype(jnp.int32) >> 3)
    for slot, group in zip(range(RES, SLOTS), groups):
        sent[listed(group), :HEADS] = asked_here[slot]
        sent[listed(group), HEADS] = fresh_here[slot]


def split_kernel(moved, resident, *outs):
    y, _ = place_of()
    for step, out in enumerate(outs):
        for part in range(2):
            first = shifted(y, step) * PAIRS * HD + part * FEATURES
            lanes = pl.ds(pl.multiple_of(first, PAIRS * HD), PAIRS * HD)
            columns = slice(part * PAIRS * HD, (part + 1) * PAIRS * HD)
            out[:MIG, :, columns] = moved[:, :, lanes]
            out[MIG:, :, columns] = resident[:, :, lanes]


def spread_kernel(origin, arrived, kept, asking):
    for row in range(SLOTS):
        chunk = arrived.at[listed(origin[row])] if row < MIG else kept.at[row - MIG]
        for peer in range(SIDE):
            asking[peer, row * HEADS : (row + 1) * HEADS] = chunk[:HEADS]
            asking[peer, SLOTS * HEADS + row] = chunk[HEADS]


def scores_of(left, right):
    return lax.dot_general(left, right, (((1,), (1,)), ((), ())), preferred_element_type=F32) * SCALE


def partial_kernel(lengths, target, asking, *rest):
    *blocks, payload, scores, weights, stats = rest
    column = lax.broadcasted_iota(jnp.int32, (1, HD), 1)
    block = column // STRIDE
    y, x = place_of()
    y = shifted(y, -jnp.where((block == 1) | (block == 2), 3 - block, block))
    position = (y * SIDE + x) * STRIDE + column % STRIDE

    def stored(row, place):
        lanes = slice(place * HD, (place + 1) * HD)
        return jnp.concatenate([block[row, :, lanes] for block in blocks], 0)

    for row in range(SLOTS):
        usable = position < lengths[row]
        span = slice(row * QROWS, (row + 1) * QROWS)
        for pair in range(PAIRS):
            asked = jnp.concatenate([asking[2 * pair, span, :], asking[2 * pair + 1, span, :]], 0)
            found = jnp.where(usable, scores_of(asked, stored(row, pair)), FLOOR)
            scores[2 * pair, span, :] = found[:QROWS]
            scores[2 * pair + 1, span, :] = found[QROWS:]
    lane = lax.broadcasted_iota(jnp.int32, (ROWS, HD), 1)
    table = jnp.zeros((ROWS, HD), F32)
    for peer in range(SIDE):
        found = scores[peer]
        top = jnp.max(found, axis=1, keepdims=True)
        first = top.astype(BF).astype(F32)
        second = (top - first).astype(BF).astype(F32)
        weight = jnp.exp(found - (first + second))
        total = jnp.sum(weight, axis=1, keepdims=True)
        weights[peer] = weight.astype(BF)
        total_first = total.astype(BF).astype(F32)
        for place, value in enumerate((first, total_first, second, total - total_first)):
            table = jnp.where(lane == peer * 8 + place, value, table)
    stats[:ROWS, :] = table
    stats[ROWS:, :] = jnp.zeros((2 * HD - ROWS, HD), F32)
    low = stats[:HD, :].T
    high = stats[HD:, :].T
    for peer in range(SIDE):
        rows = slice(peer * 8, (peer + 1) * 8)
        payload[peer, ROWS:, :] = jnp.concatenate([low[rows], high[rows]], 0).astype(BF)
    for row in range(SLOTS):
        span = slice(row * QROWS, (row + 1) * QROWS)
        for pair in range(PAIRS):
            weight = jnp.concatenate([weights[2 * pair, span, :], weights[2 * pair + 1, span, :]], 0)
            blended = jnp.dot(weight, stored(row, PAIRS + pair), preferred_element_type=F32).astype(BF)
            payload[2 * pair, span, :] = blended[:QROWS]
            payload[2 * pair + 1, span, :] = blended[QROWS:]


def merge_kernel(origin, target, gathered, everyone, sent, kept):
    _, x = place_of()
    first = x // 2 * 2
    asked = everyone[first + x % 2, :ROWS, :]
    keys = everyone[first, ROWS:, :]
    values = everyone[first + 1, ROWS:, :]
    row = lax.broadcasted_iota(jnp.int32, (ROWS, ENTRIES), 0)
    lane = lax.broadcasted_iota(jnp.int32, (ROWS, ENTRIES), 1)
    causal = (lane // STEPS == row // QROWS) & (lane % STEPS <= row % STEPS)
    fresh = jnp.where(causal, scores_of(asked, keys), FLOOR)
    fresh_top = jnp.max(fresh, axis=1, keepdims=True)

    tops = gathered[:, ROWS:, :].astype(F32)
    blank = jnp.zeros((HD - SIDE * 8, HD), F32)
    low = jnp.concatenate([tops[:, :8, :].reshape(SIDE * 8, HD), blank], 0).T
    high = jnp.concatenate([tops[:, 8:, :].reshape(SIDE * 8, HD), blank], 0).T[: ROWS - HD]
    pairs = jnp.concatenate([low, high], 0)
    both = pairs + pltpu.roll(pairs, HD - 2, 1)
    lane = lax.broadcasted_iota(jnp.int32, (ROWS, HD), 1)
    is_top = (lane % 8 == 0) & (lane < SIDE * 8)
    tops = jnp.where(is_top, both, FLOOR)
    sums = pltpu.roll(both, HD - 1, 1)
    highest = jnp.maximum(jnp.max(tops, axis=1, keepdims=True), fresh_top)
    factors = jnp.where(is_top, jnp.exp(tops - highest), 0.0)
    fresh_weights = jnp.where(causal, jnp.exp(fresh - highest), 0.0)
    totals = jnp.sum(jnp.where(is_top, factors * sums, 0.0), axis=1, keepdims=True)
    totals += jnp.sum(fresh_weights, axis=1, keepdims=True)
    blended = jnp.dot(fresh_weights.astype(BF), values, preferred_element_type=F32)
    for peer in range(SIDE):
        blended += factors[:, peer * 8 : peer * 8 + 1] * gathered[peer, :ROWS, :].astype(F32)
    result = (blended / totals).astype(BF)

    sent[...] = jnp.zeros_like(sent)
    for slot in range(MIG):
        sent[listed(origin[slot])] = result[slot * QROWS : (slot + 1) * QROWS]
    for slot in range(RES):
        kept[slot] = result[(MIG + slot) * QROWS : (MIG + slot + 1) * QROWS]


def select_kernel(target, returned, kept, out, sems):
    copies = []
    for slot in range(SLOTS):
        source = kept.at[slot] if slot < RES else returned.at[listed(target[slot - RES])]
        copies.append(pltpu.make_async_copy(source, out.at[slot], sems.at[slot]))
    for copy in copies:
        copy.start()
    for copy in copies:
        copy.wait()


def body(
    queries,
    new_entries,
    resident_cache,
    prefill_cache,
    resident_kept,
    kept_tokens,
    prefill_slot,
    decode_slot,
):
    shape = jax.ShapeDtypeStruct
    peers = [[y * SIDE + x for x in range(SIDE)] for y in range(SIDE)]
    turned = [[listed(place) for place in range(GROUPS)]]

    def around(array):
        return lax.all_to_all(array, "group", 0, 0, axis_index_groups=turned, tiled=True)

    def across(array):
        return lax.all_to_all(array, "tensor", 0, 0, axis_index_groups=peers, tiled=True)

    asked = queries.reshape(SLOTS, STEPS, HEADS, HD).transpose(0, 2, 1, 3)
    sent, kept = call(
        pack_kernel,
        (shape((GROUPS, TILES, STEPS, HD), BF), shape((RES, TILES, STEPS, HD), BF)),
        [HB] * 4,
        scratch=[
            pltpu.VMEM((SLOTS, HEADS, STEPS, HD), BF),
            pltpu.VMEM((SLOTS, STEPS, HD), BF),
            pltpu.VMEM((2, HD), jnp.int32),
            pltpu.VMEM((2, HD), jnp.int32),
            pltpu.SemaphoreType.DMA((4,)),
        ],
        limit=FULL,
    )(decode_slot.reshape(2, HD), prefill_slot.reshape(2, HD), asked, new_entries)
    arrived = around(sent)

    later = (resident_kept, kept_tokens, prefill_slot, decode_slot)
    later, kept = lax.optimization_barrier((later, kept))
    resident_kept, kept_tokens, prefill_slot, decode_slot = later
    group = lax.axis_index("group")

    def looked_up(names, first, values):
        wanted = first + jnp.arange(MIG, dtype=jnp.int32)
        return jnp.sum(jnp.where(names[None, :] == wanted[:, None], values[None, :], 0), axis=1)

    target = looked_up(decode_slot, group * SLOTS + RES, prefill_slot) // MIG
    origin = looked_up(prefill_slot, group * MIG, decode_slot) // SLOTS
    moved_len = looked_up(prefill_slot, group * MIG, kept_tokens)
    resident_len = lax.dynamic_slice_in_dim(resident_kept, group * RES, RES)
    lengths = jnp.concatenate([moved_len, resident_len])

    split = call(
        split_kernel,
        (shape((SLOTS, STRIDE, 2 * PAIRS * HD), BF),) * SIDE,
        [VM, VM],
        moved=3 * 2**20,
    )(prefill_cache, resident_cache)
    blocks = [split[0]]
    for step in (2, 1, 3):
        steps = [(t, (t + step * SIDE) % SHARDS) for t in range(SHARDS)]
        blocks.append(lax.ppermute(split[step], "tensor", steps))

    asking = call(
        spread_kernel, shape((SIDE, SLOTS * TILES, STEPS, HD), BF), [SM, VM, VM]
    )(origin, arrived, kept)
    everyone = across(asking).reshape(SIDE, ROWS + ENTRIES, HD)

    payload = call(
        partial_kernel,
        shape((SIDE, PAYLOAD, HD), BF),
        [SM, SM] + [VM] * (1 + SIDE),
        flops=10**8,
        moved=3 * 2**20,
        scratch=[
            pltpu.VMEM((SIDE, ROWS, HD), F32),
            pltpu.VMEM((SIDE, ROWS, HD), BF),
            pltpu.VMEM((2 * HD, HD), F32),
        ],
    )(lengths, target, everyone, *blocks)
    gathered = across(payload)

    finished, here = call(
        merge_kernel,
        (shape((GROUPS, QROWS, HD), BF), shape((RES, QROWS, HD), BF)),
        [SM, SM, VM, VM],
    )(origin, target, gathered, everyone)
    returned = around(finished)

    result = call(
        select_kernel,
        shape((SLOTS, QROWS, HD), BF),
        [SM, VM, VM],
        scratch=[pltpu.SemaphoreType.DMA((SLOTS,))],
        places=ANY,
    )(target, returned, here)
    result = result.reshape(SLOTS, HEADS, STEPS, HD).transpose(0, 2, 1, 3)
    return result.reshape(SLOTS, STEPS, HEADS * HD)


def solution(mesh):
    in_specs = (
        P("group", None, "tensor"),
        P("group", None, None),
        P("group", "tensor", None),
        P("group", "tensor", None),
        P(),
        P(),
        P(),
        P(),
    )
    out_specs = P("group", None, "tensor")
    return jax.shard_map(body, mesh=mesh, in_specs=in_specs, out_specs=out_specs, check_vma=False)
```
